32 devices in a mesh: rep: 4 (over y, x), shard: 8 (over z, core).
Axes of the slice: x: 2, y: 2, z: 4, core: 2. Of those that a mesh axis runs over, the one named last changes fastest.
Arguments:
- inputs: bfloat16 [32, 256, 1024], P(('rep', 'shard')), may hold values from -6 to 6
- cotangent: bfloat16 [32, 256, 1024], P(('rep', 'shard')), may hold values from -6 to 6
- seq_lengths: int32 [32], replicated, may hold values from 1 to 256, 5120 in all
- dealing: int32 [32], replicated, may hold values from 0 to 31, as said below
- rel_buckets: int32 [511], replicated, may hold values from 0 to 31
- w_query: bfloat16 [1024, 1024], P('shard'), may hold values from -0.09375 to 0.09375
- w_key: bfloat16 [1024, 1024], P('shard'), may hold values from -0.09375 to 0.09375
- w_value: bfloat16 [1024, 1024], P('shard'), may hold values from -0.1875 to 0.1875
- w_mixer: bfloat16 [1024, 1024], P('shard'), may hold values from -1 to 1
- w_inner: bfloat16 [1024, 4096], P('shard'), may hold values from -0.1875 to 0.1875
- w_outer: bfloat16 [4096, 1024], P('shard'), may hold values from -0.09375 to 0.09375
- gain_attn: bfloat16 [1024], P('shard'), may hold values from 0.5 to 1.5
- gain_mlp: bfloat16 [1024], P('shard'), may hold values from 0.5 to 1.5
- bias_table: bfloat16 [32, 16], P('shard'), may hold values from -6 to 6
Outputs:
- layer_out: bfloat16 [32, 256, 1024], P(('rep', 'shard'))
- input_grad: bfloat16 [32, 256, 1024], P(('rep', 'shard'))
- grad_query: float32 [1024, 1024], P('shard')
- grad_key: float32 [1024, 1024], P('shard')
- grad_value: float32 [1024, 1024], P('shard')
- grad_mixer: float32 [1024, 1024], P('shard')
- grad_inner: float32 [1024, 4096], P('shard')
- grad_outer: float32 [4096, 1024], P('shard')
- grad_gain_attn: float32 [1024], P('shard')
- grad_gain_mlp: float32 [1024], P('shard')
- grad_table: float32 [32, 16], P('shard')
The draws below stay inside these ranges and needn't reach their ends.
Inputs may be any that keep to these rules, and one draw needn't show every extreme that they name: A permutation: slot s processes sequence dealing[s]; at least one slot s processes sequence (s + 16) % 32, which slot drawn from the seed. `seq_lengths`: valid tokens stand at the start of each sequence; all lengths sum to 5120 and the longest is exactly 256. `rel_buckets`: entry j - i + 255 is the bucket of key position j seen from query position i.
All inputs are finite; a program needn't handle non-finite values.
Results may differ from the reference program's by a relative error of at most 0.015.
Values may be sent and summed in bfloat16 or wider, within the bound.
No kernel may reach another device: no remote copies, remote signals or barrier semaphores. Data moves between devices by JAX's collectives and lax.ppermute only.
A program may use at most 320 MiB of HBM per device.

```python
import math
import jax
import jax.numpy as jnp
import numpy as np
from jax import lax

D = 1024
HEADS = 16
HEAD = 64
FF = 4096
BUCKETS = 32
LEN = 256
NSEQ = 32
TOTAL = 5120


def draw_dealing(key, part):
    key = jax.random.fold_in(key, 11)
    key_order = jax.random.fold_in(key, 1)
    key_pick = jax.random.fold_in(key, 2)
    order = jax.random.permutation(key_order, NSEQ).astype(jnp.int32)
    chosen = jax.random.randint(key_pick, (), 0, NSEQ).astype(jnp.int32)
    target = ((chosen + NSEQ // 2) % NSEQ).astype(jnp.int32)
    places = jnp.arange(NSEQ, dtype=jnp.int32)
    holder = jnp.sum(jnp.where(order == target, places, 0)).astype(jnp.int32)
    previous = jnp.sum(jnp.where(places == chosen, order, 0)).astype(jnp.int32)
    order = jnp.where(places == holder, previous, order)
    order = jnp.where(places == chosen, target, order)
    return order.astype(jnp.int32)


def touch_ends(values, own_key, least, high):
    index_at = [jax.random.randint(jax.random.fold_in(own_key, axis), (), 0, length) for axis, length in enumerate(values.shape)]
    longest = values.shape.index(max(values.shape))
    beside = index_at[:longest] + [(index_at[longest] + 1) % values.shape[longest]] + index_at[longest + 1:]
    return values.at[tuple(index_at)].set(least).at[tuple(beside)].set(high)


def shard_levels(stream_key, dims, shards, low, top_value):
    level = 1.0
    for axis_at, parts in shards:
        draws = jax.random.uniform(jax.random.fold_in(jax.random.fold_in(stream_key, 6), axis_at), (parts,), jnp.float32, low / len(shards), top_value / len(shards))
        level = level * jnp.repeat(jnp.exp(draws), dims[axis_at] // parts).reshape((-1,) + (1,) * (len(dims) - 1 - axis_at))
    return level


def profile(count, total, limit, slope):
    loads = [(1 << 20) // math.isqrt(rank ** slope) + 1 for rank in range(2, count + 1)]
    rest, counts = total - limit - (count - 1), [1] * (count - 1)
    while rest > 0:
        free = [i for i in range(count - 1) if counts[i] < limit]
        pool, remaining = sum([loads[i] for i in free]), rest
        for i in free:
            addition = min(limit - counts[i], max(1, remaining * loads[i] // pool), rest)
            counts[i] = counts[i] + addition
            rest = rest - addition
    return np.array([limit] + counts)


def uneven_parts(key, amount, total, most, skew):
    if amount == 2:
        one = jax.random.randint(key, (), max(1, total - most), min(most, total - 1) + 1)
        return jnp.stack([one, total - one])
    tallies = jnp.asarray(profile(amount, total, most, skew), jnp.int32)
    pairs = (amount - 1) // 2
    giver, receiver = tallies[1:1 + 2 * pairs:2], tallies[2:2 + 2 * pairs:2]
    margin = jnp.minimum(giver - 1, most - receiver)
    moved = jax.random.randint(jax.random.fold_in(key, 1), (pairs,), 0, 1 << 20) % (margin + 1)
    tallies = tallies.at[1:1 + 2 * pairs:2].set(giver - moved).at[2:2 + 2 * pairs:2].set(receiver + moved)
    return tallies[jax.random.permutation(jax.random.fold_in(key, 2), amount)]


def noise(key, dims, scale, most, pieces=(), kind=jnp.bfloat16):
    result = jax.random.normal(key, dims, jnp.float32) * scale
    if len(pieces) > 0:
        result = shard_levels(key, dims, pieces, -0.22, 0.18) * result
    return jnp.clip(result, min=-most, max=most).astype(kind)


def setup_inputs(seed: int = 0) -> dict:
    key_of = jax.random.split(jax.random.key(seed), 15)
    inputs = noise(key_of[0], (NSEQ, LEN, D), 1.0, 6.0, ((0, 32),))
    cotangent = noise(key_of[1], (NSEQ, LEN, D), 1.0, 6.0, ((0, 32),))
    seq_lengths = uneven_parts(key_of[2], NSEQ, TOTAL, LEN, 1).astype(jnp.int32)
    dealing = draw_dealing(jax.random.fold_in(key_of[14], 71), 0)
    rel_buckets = touch_ends(jax.random.randint(key_of[4], (2 * LEN - 1,), 0, BUCKETS), jax.random.fold_in(key_of[4], 1), 0, BUCKETS - 1).astype(jnp.int32)
    w_query = noise(key_of[5], (D, D), (1.4 * HEAD ** -0.25 * D ** -0.5), 0.09375, ((0, 8),))
    w_key = noise(key_of[6], (D, D), (1.4 * HEAD ** -0.25 * D ** -0.5), 0.09375, ((0, 8),))
    w_value = noise(key_of[7], (D, D), D ** -0.5, 0.1875, ((0, 8),))
    w_mixer = noise(key_of[8], (D, D), (6.0 * D ** -0.5), 1.0, ((0, 8),))
    w_inner = noise(key_of[9], (D, FF), D ** -0.5, 0.1875, ((0, 8),))
    w_outer = noise(key_of[10], (FF, D), FF ** -0.5, 0.09375, ((0, 8),))
    gain_attn = jnp.clip(1.0 + 0.1 * jax.random.normal(key_of[11], (D,), jnp.float32), 0.5, 1.5).astype(jnp.bfloat16)
    gain_mlp = jnp.clip(1.0 + 0.1 * jax.random.normal(key_of[12], (D,), jnp.float32), 0.5, 1.5).astype(jnp.bfloat16)
    bias_table = noise(key_of[13], (BUCKETS, HEADS), 1.0, 6.0, ((0, 8),))
    return {"inputs": inputs, "cotangent": cotangent, "seq_lengths": seq_lengths, "dealing": dealing, "rel_buckets": rel_buckets, "w_query": w_query, "w_key": w_key, "w_value": w_value, "w_mixer": w_mixer, "w_inner": w_inner, "w_outer": w_outer, "gain_attn": gain_attn, "gain_mlp": gain_mlp, "bias_table": bias_table}


EPSILON = 1e-06
MASKED = -1000000000.0
HIGHEST = lax.Precision.HIGHEST

@jax.custom_vjp
def low(v):
    return lax.optimization_barrier(v.astype(jnp.bfloat16)).astype(jnp.float32)

@jax.custom_vjp
def low_back(v):
    return v

def low_keep(v):
    return (low(v), None)

def low_pass(kept, grad):
    return (grad,)

def back_keep(v):
    return (v, None)

def back_low(kept, grad):
    return (low(grad),)
low.defvjp(low_keep, low_pass)
low_back.defvjp(back_keep, back_low)

def rounded_both(value):
    return low_back(low(value))

def matmul(left, right):
    return jnp.matmul(left, right, precision=HIGHEST)

def rms_norm(hidden, gain):
    return hidden * lax.rsqrt(lax.optimization_barrier(jnp.mean(hidden * hidden, axis=-1, keepdims=True)) + EPSILON) * gain

def one_sequence(weights, rel_buckets, seq_input, length):
    w_query, w_key, w_value, w_mixer, w_inner, w_outer, gain_attn, gain_mlp, bias_table = weights
    places = jnp.arange(LEN, dtype=jnp.int32)
    valid_keys = places < length
    normed = low(rms_norm(seq_input, gain_attn))
    queries = rounded_both(matmul(normed, w_query)).reshape(LEN, HEADS, HEAD)
    keys_all = rounded_both(matmul(normed, w_key)).reshape(LEN, HEADS, HEAD)
    values_all = rounded_both(matmul(normed, w_value)).reshape(LEN, HEADS, HEAD)
    offsets = places[None, :] - places[:, None] + LEN - 1
    buckets = rel_buckets[offsets]
    bias = jnp.transpose(bias_table[buckets], (2, 0, 1))
    scores = jnp.einsum('ihd,jhd->hij', queries, keys_all, precision=HIGHEST) + bias
    scores = low_back(scores)
    scores = jnp.where(valid_keys[None, None, :], scores, MASKED)
    probs = jax.nn.softmax(scores, axis=-1)
    mixed = jnp.einsum('hij,jhd->ihd', low(probs), values_all, precision=HIGHEST)
    mixed = rounded_both(mixed).reshape(LEN, D)
    attended = low_back(matmul(mixed, w_mixer))
    middle = seq_input + attended
    normed2 = low(rms_norm(middle, gain_mlp))
    inner = low_back(matmul(normed2, w_inner))
    active = low(jax.nn.gelu(inner, approximate=False))
    outer = low_back(matmul(active, w_outer))
    return (middle + outer) * valid_keys[:, None].astype(jnp.float32)

def reference(inputs, cotangent, seq_lengths, dealing, rel_buckets, w_query, w_key, w_value, w_mixer, w_inner, w_outer, gain_attn, gain_mlp, bias_table):
    params = (w_query, w_key, w_value, w_mixer, w_inner, w_outer, gain_attn, gain_mlp, bias_table)
    params = tuple((weight.astype(jnp.float32) for weight in params))
    dealt = inputs.astype(jnp.float32)[dealing]
    dealt_lengths = seq_lengths[dealing]

    def forward(dealt_in, *weights):

        def per_sequence(packed):
            return one_sequence(weights, rel_buckets, packed[0], packed[1])
        return lax.map(jax.checkpoint(per_sequence), (dealt_in, dealt_lengths))
    layer, pullback = jax.vjp(forward, dealt, *params)
    grads = pullback(cotangent.astype(jnp.float32))
    inverse = jnp.argsort(dealing)
    input_grad = grads[0][inverse].astype(jnp.bfloat16)
    return (layer.astype(jnp.bfloat16), input_grad, grads[1], grads[2], grads[3], grads[4], grads[5], grads[6], grads[7], grads[8], grads[9])
```

```python
import functools

import jax
import jax.numpy as jnp
from jax import lax
from jax.experimental import pallas as pl
from jax.experimental.pallas import tpu as pltpu
from jax.sharding import PartitionSpec as P

EPSILON = 1e-06
MASKED = -1000000000.0
AXES = ("rep", "shard")
BF16 = jnp.bfloat16
F32 = jnp.float32
INV_SQRT2 = 0.7071067811865476
INV_SQRT2PI = 0.3989422804014327

VMEM = pl.BlockSpec(memory_space=pltpu.VMEM)
SMEM = pl.BlockSpec(memory_space=pltpu.SMEM)


def shaped(shape, dtype=BF16):
    return jax.ShapeDtypeStruct(shape, dtype)


def call(body, outs, *args, scalars=1, scratch=(), aliases=None, flops=0, limit=48):
    out_bytes = sum(o.dtype.itemsize * o.size for o in outs)
    in_bytes = sum(a.dtype.itemsize * a.size for a in args)
    return pl.pallas_call(
        body,
        out_shape=outs,
        in_specs=[SMEM] * scalars + [VMEM] * (len(args) - scalars),
        out_specs=[VMEM] * len(outs),
        scratch_shapes=list(scratch),
        input_output_aliases=aliases or {},
        cost_estimate=pl.CostEstimate(
            flops=flops, bytes_accessed=in_bytes + out_bytes, transcendentals=0
        ),
        compiler_params=pltpu.CompilerParams(vmem_limit_bytes=limit * 1024 * 1024),
    )(*args)


def dot(a, b):
    return jnp.dot(a, b, preferred_element_type=F32)


def dot_nt(a, b):
    return lax.dot_general(a, b, (((1,), (1,)), ((), ())), preferred_element_type=F32)


def dot_tn(a, b):
    return lax.dot_general(a, b, (((0,), (0,)), ((), ())), preferred_element_type=F32)


def add(a, b):
    return (a.astype(F32) + b.astype(F32)).astype(BF16)


def row_blocks(sc, j, zs, hb):
    zz = lax.rem(sc[0] + zs - j, zs)
    first = pl.multiple_of((2 * zz + sc[1]) * hb, hb)
    second = pl.multiple_of((2 * zz + 1 - sc[1]) * hb, hb)
    return first, second


def norm_kernel(own, sib, gain, normed):
    half = own.shape[0]
    for at, src in ((0, own), (half, sib)):
        v = src[...].astype(F32)
        scale = lax.rsqrt(jnp.mean(v * v, axis=-1, keepdims=True) + EPSILON)
        normed[at : at + half, :] = (v * scale * gain[...]).astype(BF16)


def toeplitz(row, n):
    wide = jnp.broadcast_to(row, (n, 2 * n))
    return pltpu.roll(wide, n + 1, 1, stride=1, stride_axis=0)[:, :n]


def probabilities(q, kk, bias, length):
    n = q.shape[0]
    s = dot_nt(q, kk) + bias
    col = lax.broadcasted_iota(jnp.int32, (n, n), 1)
    s = jnp.where(col < length, s, MASKED)
    e = jnp.exp(s - jnp.max(s, axis=-1, keepdims=True))
    return e / jnp.sum(e, axis=-1, keepdims=True)


def attn_kernel(zs, hb, hd, sc, normed, off, *refs):
    pieces, (w, qkv, mixed) = refs[:zs], refs[zs:]
    for j in range(zs):
        first, second = row_blocks(sc, j, zs, hb)
        w[pl.ds(first, hb), :] = pieces[j][:hb, : 3 * hb]
        w[pl.ds(second, hb), :] = pieces[j][hb:, : 3 * hb]
    qkv[...] = dot(normed[...], w[...]).astype(BF16)
    half = normed.shape[0] // 2
    for h in range(hb // hd):
        bias = toeplitz(off[h : h + 1, :], half)
        for s in range(2):
            rows = slice(s * half, (s + 1) * half)
            q, kk, v = (qkv[rows, i * hb + h * hd : i * hb + (h + 1) * hd] for i in range(3))
            p = probabilities(q, kk, bias, sc[3 + s]).astype(BF16)
            mixed[rows, h * hd : (h + 1) * hd] = dot(p, v).astype(BF16)


def mixer_kernel(zs, rs, hb, sc, *refs):
    mixed_parts, pieces = refs[:rs], refs[rs : rs + rs * zs]
    mixed, wo, partial = refs[rs + rs * zs :]
    for m in range(rs):
        mixed[:, m * hb : (m + 1) * hb] = mixed_parts[m][...]
    for m in range(rs):
        col = pl.multiple_of(lax.bitwise_xor(sc[2], m) * (2 * hb), 2 * hb)
        for j in range(zs):
            block = lax.bitwise_xor(lax.rem(sc[0] + zs - j, zs), sc[2])
            piece = pieces[m * zs + j]
            both = jnp.concatenate([piece[:hb, 3 * hb :], piece[hb:, 3 * hb :]], axis=1)
            wo[pl.ds(pl.multiple_of(block * hb, hb), hb), pl.ds(col, 2 * hb)] = both
    partial[...] = dot(mixed[...], wo[...]).astype(BF16)


def middle_kernel(own, sib, part, other, gain, middle, normed2):
    half = own.shape[0]
    for s, src in ((0, own), (1, sib)):
        rows = slice(s * half, (s + 1) * half)
        swapped = slice((1 - s) * half, (2 - s) * half)
        v = src[...].astype(F32) + part[rows, :].astype(F32) + other[swapped, :].astype(F32)
        middle[rows, :] = v
        scale = lax.rsqrt(jnp.mean(v * v, axis=-1, keepdims=True) + EPSILON)
        normed2[rows, :] = (v * scale * gain[...]).astype(BF16)


def ffn_kernel(zs, hb, sub, first_chunk, sc, normed2, normed2t, gl, *refs):
    n_in = 2 * zs + (0 if first_chunk else 2)
    pieces_i, pieces_o = refs[:zs], refs[zs : 2 * zs]
    acc_in = refs[2 * zs : n_in]
    outer, gn2, gi, go, w1, w2, act_t = refs[n_in:]
    for j in range(zs):
        first, second = row_blocks(sc, j, zs, hb)
        w1[pl.ds(first, hb), :] = pieces_i[j][:hb, :]
        w1[pl.ds(second, hb), :] = pieces_i[j][hb:, :]
        zz = lax.rem(sc[0] + zs - j, zs)
        w2[pl.ds(pl.multiple_of(zz * sub, sub), sub), :] = pieces_o[j][...]
    h = dot(normed2[...], w1[...])
    cdf = 0.5 * (1.0 + lax.erf(h * INV_SQRT2))
    pdf = jnp.exp(-0.5 * h * h) * INV_SQRT2PI
    act = (h * cdf).astype(BF16)
    ga = dot_nt(gl[...], w2[...])
    gh = (ga * (cdf + h * pdf)).astype(BF16)
    act_t[...] = act.T
    out_part = dot(act, w2[...])
    gn_part = dot_nt(gh, w1[...])
    if not first_chunk:
        out_part = out_part + acc_in[0][...]
        gn_part = gn_part + acc_in[1][...]
    outer[...] = out_part
    gn2[...] = gn_part
    for j in range(zs):
        first, second = row_blocks(sc, j, zs, hb)
        gi[j, :hb, :] = dot(normed2t[pl.ds(first, hb), :], gh).astype(BF16)
        gi[j, hb:, :] = dot(normed2t[pl.ds(second, hb), :], gh).astype(BF16)
        zz = lax.rem(sc[0] + zs - j, zs)
        rows = pl.ds(pl.multiple_of(zz * sub, sub), sub)
        go[j] = dot(act_t[rows, :], gl[...]).astype(BF16)


def middle_back_kernel(zs, rs, hb, sc, part, other, middle, gl, gain, mixed, wo, *refs):
    grad_mid, gm, ggain, gwo, gatt, full = refs
    half = part.shape[0] // 2
    width = part.shape[1]
    for s in range(2):
        rows = slice(s * half, (s + 1) * half)
        swapped = slice((1 - s) * half, (2 - s) * half)
        gn = part[rows, :] + other[swapped, :].astype(F32)
        v = middle[rows, :]
        scale = lax.rsqrt(jnp.mean(v * v, axis=-1, keepdims=True) + EPSILON)
        gg = gn * gain[...]
        inner = jnp.sum(gg * v, axis=-1, keepdims=True) * (1.0 / width)
        g = gl[rows, :].astype(F32) + scale * gg - v * (scale * scale * scale * inner)
        if s == 0:
            grad_mid[...] = g
            ggain[...] = jnp.sum(gn * v * scale, axis=0, keepdims=True)
        gatt[rows, :] = g.astype(BF16)
    gm[...] = dot_nt(gatt[...], wo[...]).astype(BF16)
    full[...] = dot_tn(mixed[...], gatt[...]).astype(BF16)
    for j in range(zs):
        block = lax.bitwise_xor(lax.rem(sc[0] + zs - j, zs), sc[2])
        gwo[j] = full[pl.ds(pl.multiple_of(block * hb, hb), hb), :]


def attn_back_kernel(zs, hb, hd, at, sc, normedt, off, qkv, gmix, *refs):
    gqkv, gw, diag = refs
    half = qkv.shape[0] // 2
    flip = (
        lax.broadcasted_iota(jnp.int32, (half, half), 0)
        + lax.broadcasted_iota(jnp.int32, (half, half), 1)
        == half - 1
    ).astype(BF16)
    for h in range(hb // hd):
        bias = toeplitz(off[h : h + 1, :], half)
        flipped = jnp.zeros((half, half), F32)
        for s in range(2):
            rows = slice(s * half, (s + 1) * half)
            q, kk, v = (qkv[rows, i * hb + h * hd : i * hb + (h + 1) * hd] for i in range(3))
            gm = gmix[rows, at + h * hd : at + (h + 1) * hd]
            p = probabilities(q, kk, bias, sc[3 + s])
            gp = dot_nt(gm, v)
            delta = jnp.sum(p * gp, axis=-1, keepdims=True)
            gs = (p * (gp - delta)).astype(BF16)
            flipped = flipped + dot(flip, gs)
            cols = [slice(i * hb + h * hd, i * hb + (h + 1) * hd) for i in range(3)]
            gqkv[rows, cols[0]] = dot(gs, kk).astype(BF16)
            gqkv[rows, cols[1]] = dot_tn(gs, q).astype(BF16)
            gqkv[rows, cols[2]] = dot_tn(p.astype(BF16), gm).astype(BF16)
        wide = jnp.concatenate([flipped, jnp.zeros((half, half), F32)], axis=1)
        skewed = pltpu.roll(wide, 0, 1, stride=1, stride_axis=0)
        diag[h : h + 1, :] = jnp.sum(skewed, axis=0, keepdims=True)
    for j in range(zs):
        first, second = row_blocks(sc, j, zs, hb)
        gw[j, :hb, :] = dot(normedt[pl.ds(first, hb), :], gqkv[...]).astype(BF16)
        gw[j, hb:, :] = dot(normedt[pl.ds(second, hb), :], gqkv[...]).astype(BF16)


def grad_normed_kernel(rs, *refs):
    grads, weights, (own, sib) = refs[:rs], refs[rs : 2 * rs], refs[2 * rs :]
    half = own.shape[0]
    total = dot_nt(grads[0][...], weights[0][...])
    for m in range(1, rs):
        total = total + dot_nt(grads[m][...], weights[m][...])
    own[...] = total[:half, :]
    sib[...] = total[half:, :].astype(BF16)


def input_back_kernel(own, other, grad_mid, x, gain, out, ggain):
    gn = own[...] + other[...].astype(F32)
    v = x[...].astype(F32)
    scale = lax.rsqrt(jnp.mean(v * v, axis=-1, keepdims=True) + EPSILON)
    gg = gn * gain[...]
    inner = jnp.mean(gg * v, axis=-1, keepdims=True)
    g = grad_mid[...] + scale * gg - v * (scale * scale * scale * inner)
    out[...] = g.astype(BF16)
    ggain[...] = jnp.sum(gn * v * scale, axis=0, keepdims=True)


def layer_kernel(sc, middle, own, other, out):
    half = own.shape[0]
    row = lax.broadcasted_iota(jnp.int32, own.shape, 0)
    v = middle[...] + own[...] + other[...].astype(F32)
    out[...] = jnp.where(row < sc[3], v, 0.0).astype(BF16)


def shuffle_kernel(count, index, src, out):
    for e in range(count):
        out[e] = src[index[e]]


def shuffle(index, blocks):
    body = functools.partial(shuffle_kernel, blocks.shape[0])
    return call(body, [shaped(blocks.shape)], index.astype(jnp.int32), blocks)[0]


def solution(mesh):
    rs, ss = mesh.shape["rep"], mesh.shape["shard"]
    zs = ss // 2
    count = rs * ss

    def pairs(move):
        table = []
        for i in range(count):
            r, z, k = i // ss, (i % ss) // 2, i % 2
            r, z, k = move(r, z, k)
            table.append((i, (r * zs + z) * 2 + k))
        return table

    core_pairs = pairs(lambda r, z, k: (r, z, 1 - k))
    ring_pairs = pairs(lambda r, z, k: (r, (z + 1) % zs, k))
    rep_pairs = {m: pairs(lambda r, z, k, m=m: (r ^ m, z, k)) for m in range(1, rs)}
    z_pairs = {m: pairs(lambda r, z, k, m=m: (r, z ^ m, k)) for m in range(1, zs)}

    def send(value, table):
        return lax.ppermute(value, AXES, table)

    bits = [1 << b for b in range(rs.bit_length() - 1)]

    def hop(m, turn):
        mine = [b for b in bits if m & b]
        return mine[turn % len(mine)]

    by_size = sorted(range(1, rs), key=lambda m: (bin(m).count("1"), m))

    def gather(own):
        got = [[None] * rs for _ in range(zs)]
        got[0] = list(own)
        v = own[0]
        for j in range(1, zs):
            v = send(v, ring_pairs)
            got[j][0] = v
        for m in by_size:
            for j in range(1, zs):
                b = hop(m, j)
                got[j][m] = send(got[j][m ^ b], rep_pairs[b])
        return got

    def sum_reps(parts, turn):
        parts = list(parts)
        for m in reversed(by_size):
            b = hop(m, turn)
            parts[m ^ b] = add(parts[m ^ b], send(parts[m], rep_pairs[b]))
        return parts[0]

    def spread_reps(mine, turn):
        parts = [mine] + [None] * (rs - 1)
        for m in by_size:
            b = hop(m, turn)
            parts[m] = send(parts[m ^ b], rep_pairs[b])
        return parts

    def sum_ring(parts):
        v = parts[1]
        for j in range(2, zs):
            v = add(send(v, ring_pairs), parts[j])
        return add(send(v, ring_pairs), parts[0])

    def exchange(blocks, whole_core=False):
        _, p, width = blocks.shape
        v = blocks.reshape(rs, 2 * zs, p, width)
        v = [v[0]] + [send(v[m], rep_pairs[m]) for m in range(1, rs)]
        v = jnp.stack(v).reshape(rs, zs, 2, p, width)
        v = [v[:, 0]] + [send(v[:, m], z_pairs[m]) for m in range(1, zs)]
        v = jnp.stack(v, axis=1)
        if not whole_core:
            other = send(v[:, :, 1], core_pairs)
            return jnp.stack([v[:, :, 0], other], axis=2).reshape(blocks.shape)
        other = send(v, core_pairs)
        mine = jnp.stack([v[:, :, 0], other[:, :, 1]], axis=2).reshape(blocks.shape)
        theirs = jnp.stack([v[:, :, 1], other[:, :, 0]], axis=2).reshape(blocks.shape)
        return mine, theirs

    def local(
        inputs,
        cotangent,
        seq_lengths,
        dealing,
        rel_buckets,
        w_query,
        w_key,
        w_value,
        w_mixer,
        w_inner,
        w_outer,
        gain_attn,
        gain_mlp,
        bias_table,
    ):
        seq_len, width = inputs.shape[1], inputs.shape[2]
        n_buckets, heads = bias_table.shape[0] * ss, bias_table.shape[1]
        hb = w_query.shape[0]
        fb = w_outer.shape[0]
        sub = fb // rs
        cols = zs * sub
        hd = width // heads
        nh = hb // hd
        tokens = 2 * seq_len

        r, c = lax.axis_index("rep"), lax.axis_index("shard")
        z, k = c // 2, c % 2
        me = r * ss + c
        ids = jnp.arange(count, dtype=jnp.int32)
        inverse = jnp.sum(
            jnp.where(dealing[None, :] == ids[:, None], ids[None, :], 0), axis=1
        ).astype(jnp.int32)
        own_len, sib_len = seq_lengths[me], seq_lengths[me ^ 1]
        sc = jnp.stack([z, k, r, own_len, sib_len]).astype(jnp.int32)

        x_own = inputs[0]
        x_sib = send(x_own, core_pairs)

        outer_own = [lax.dynamic_slice(w_outer, ((r ^ m) * sub, 0), (sub, width)) for m in range(rs)]

        def head_cols(m, core):
            at = (2 * (r ^ m) + core) * hb
            return [lax.dynamic_slice(w, (0, at), (hb, hb)) for w in (w_query, w_key, w_value)]

        def inner_cols(m, core):
            at = [(2 * b + core) * fb + (r ^ m) * sub for b in range(zs)]
            return jnp.concatenate(
                [lax.dynamic_slice(w_inner, (0, a), (hb, sub)) for a in at], axis=1
            )

        attn_sent = jnp.stack([jnp.concatenate(head_cols(m, 1 - k), axis=1) for m in range(rs)])
        attn_got = send(attn_sent, core_pairs)
        attn_own = []
        for m in range(rs):
            mix = lax.dynamic_slice(w_mixer, (0, (r ^ m) * 2 * hb), (hb, 2 * hb))
            top = jnp.concatenate(head_cols(m, k) + [mix[:, :hb]], axis=1)
            low = jnp.concatenate([attn_got[m], mix[:, hb:]], axis=1)
            attn_own.append(jnp.concatenate([top, low], axis=0))
        inner_sent = jnp.stack([inner_cols(m, 1 - k) for m in range(rs)])
        inner_got = send(inner_sent, core_pairs)
        inner_own = [
            jnp.concatenate([inner_cols(m, k), inner_got[m]], axis=0) for m in range(rs)
        ]
        attn_w = gather(attn_own)
        outer_w = gather(outer_own)
        inner_w = gather(inner_own)

        small = jnp.concatenate([gain_attn, gain_mlp, bias_table.reshape(-1)])[None]
        small = jnp.concatenate([small, send(small, core_pairs)], axis=0)
        for b in [1 << i for i in range(zs.bit_length() - 1)]:
            small = jnp.concatenate([small, send(small, z_pairs[b])], axis=0)
        shards = jnp.arange(ss, dtype=jnp.int32)
        order = (shards[:, None] == (shards ^ c)[None, :]).astype(BF16)
        small = dot(order, small)
        gain_a = small[:, :hb].reshape(1, width)
        gain_m = small[:, hb : 2 * hb].reshape(1, width)
        table = small[:, 2 * hb :].reshape(n_buckets, heads)
        groups = jnp.arange(rs, dtype=jnp.int32) ^ r
        head_ids = ((2 * groups + k) * nh)[:, None] + jnp.arange(nh, dtype=jnp.int32)[None]
        head_ids = head_ids.reshape(-1)
        pick = (jnp.arange(heads, dtype=jnp.int32)[:, None] == head_ids[None, :]).astype(BF16)
        padded = jnp.concatenate([rel_buckets, jnp.full((1,), -1, jnp.int32)])
        hot = (padded[None, :] == jnp.arange(n_buckets, dtype=jnp.int32)[:, None]).astype(BF16)
        my_table = dot(table.astype(BF16), pick).astype(BF16)
        offsets = lax.dot_general(
            my_table, hot, (((0,), (0,)), ((), ())), preferred_element_type=F32
        ).reshape(rs, nh, 2 * seq_len)

        rows = seq_len // count
        cot = shuffle(ids ^ me, cotangent[0].reshape(count, rows, width))
        cot = exchange(cot)
        cot = shuffle(inverse[ids ^ me] ^ me, cot)
        cot_own, cot_sib = exchange(cot, whole_core=True)
        both = jnp.concatenate([cot_own, cot_sib], axis=0)
        both = shuffle(jnp.concatenate([ids ^ me, (ids ^ me) + count]), both)
        place = jnp.arange(seq_len, dtype=jnp.int32)
        valid = jnp.concatenate([place < own_len, place < sib_len])[:, None]
        gl = jnp.where(valid, both.reshape(tokens, width), jnp.zeros((), BF16))

        normed = call(norm_kernel, [shaped((tokens, width))], x_own, x_sib, gain_a, scalars=0)[0]
        normed_t = normed.T
        w_heads, qkv, mixed_parts = [], [], []
        for m in range(rs):
            w, q, mix = call(
                functools.partial(attn_kernel, zs, hb, hd),
                [shaped((width, 3 * hb)), shaped((tokens, 3 * hb)), shaped((tokens, hb))],
                sc,
                normed,
                offsets[m],
                *[attn_w[j][m] for j in range(zs)],
                flops=2 * tokens * width * 3 * hb,
            )
            w_heads.append(w)
            qkv.append(q)
            mixed_parts.append(mix)
        mixed, wo, part = call(
            functools.partial(mixer_kernel, zs, rs, hb),
            [shaped((tokens, rs * hb)), shaped((rs * hb, width)), shaped((tokens, width))],
            sc,
            *mixed_parts,
            *[attn_w[j][m] for m in range(rs) for j in range(zs)],
            flops=2 * tokens * width * rs * hb,
        )
        other = send(part, core_pairs)
        middle, normed2 = call(
            middle_kernel,
            [shaped((tokens, width), F32), shaped((tokens, width))],
            x_own,
            x_sib,
            part,
            other,
            gain_m,
            scalars=0,
        )
        normed2_t = normed2.T

        acc = []
        grad_inner, grad_outer = [], []
        for m in range(rs):
            n_in = 4 + 2 * zs
            outs = call(
                functools.partial(ffn_kernel, zs, hb, sub, m == 0),
                [
                    shaped((tokens, width), F32),
                    shaped((tokens, width), F32),
                    shaped((zs, 2 * hb, cols)),
                    shaped((zs, sub, width)),
                ],
                sc,
                normed2,
                normed2_t,
                gl,
                *[inner_w[j][m] for j in range(zs)],
                *[outer_w[j][m] for j in range(zs)],
                *acc,
                scratch=[
                    pltpu.VMEM((width, cols), BF16),
                    pltpu.VMEM((cols, width), BF16),
                    pltpu.VMEM((cols, tokens), BF16),
                ],
                aliases={} if m == 0 else {n_in: 0, n_in + 1: 1},
                flops=12 * tokens * width * cols,
            )
            acc = outs[:2]
            grad_inner.append(outs[2])
            grad_outer.append(outs[3])
        outer_part, gn2_part = acc

        gn2_other = send(gn2_part.astype(BF16), core_pairs)
        outer_other = send(outer_part[seq_len:].astype(BF16), core_pairs)

        inner_sum = sum_reps(grad_inner, 0)
        inner_sum = sum_ring([inner_sum[j] for j in range(zs)])
        outer_ring = [sum_ring([g[j] for j in range(zs)]) for g in grad_outer]

        grad_mid, gmix, ggain_m, grad_wo = call(
            functools.partial(middle_back_kernel, zs, rs, hb),
            [
                shaped((seq_len, width), F32),
                shaped((tokens, rs * hb)),
                shaped((1, width), F32),
                shaped((zs, hb, width)),
            ],
            sc,
            gn2_part,
            gn2_other,
            middle,
            gl,
            gain_m,
            mixed,
            wo,
            scratch=[pltpu.VMEM((tokens, width), BF16), pltpu.VMEM((rs * hb, width), BF16)],
            flops=4 * tokens * width * rs * hb,
        )
        mixer_ring = sum_ring([grad_wo[j] for j in range(zs)])

        layer = call(
            layer_kernel,
            [shaped((seq_len, width))],
            sc,
            middle[:seq_len],
            outer_part[:seq_len],
            outer_other,
        )[0]
        layer = shuffle(ids ^ me, layer.reshape(count, rows, width))
        layer = exchange(layer)
        layer = shuffle(dealing[ids ^ me] ^ me, layer)
        layer = shuffle(ids ^ me, exchange(layer)).reshape(1, seq_len, width)

        grad_heads, gqkv, diag = [None] * rs, [None] * rs, [None] * rs
        for m in reversed(range(rs)):
            gqkv[m], grad_heads[m], diag[m] = call(
                functools.partial(attn_back_kernel, zs, hb, hd, m * hb),
                [
                    shaped((tokens, 3 * hb)),
                    shaped((zs, 2 * hb, 3 * hb)),
                    shaped((nh, 2 * seq_len), F32),
                ],
                sc,
                normed_t,
                offsets[m],
                qkv[m],
                gmix,
                flops=2 * tokens * width * 3 * hb,
            )
        heads_sum = sum_reps(grad_heads, 1)
        heads_sum = sum_ring([heads_sum[j] for j in range(zs)])
        gn_own, gn_sib = call(
            functools.partial(grad_normed_kernel, rs),
            [shaped((seq_len, width), F32), shaped((seq_len, width))],
            *gqkv,
            *w_heads,
            scalars=0,
            flops=2 * tokens * width * 3 * hb * rs,
        )
        gn_other = send(gn_sib, core_pairs)
        input_grad, ggain_a = call(
            input_back_kernel,
            [shaped((seq_len, width)), shaped((1, width), F32)],
            gn_own,
            gn_other,
            grad_mid,
            x_own,
            gain_a,
            scalars=0,
        )

        by_bucket = lax.dot_general(
            hot.astype(F32),
            jnp.concatenate(diag, axis=0),
            (((1,), (1,)), ((), ())),
            precision=lax.Precision.HIGHEST,
        )
        grad_table = lax.dot_general(
            by_bucket,
            pick.astype(F32),
            (((1,), (1,)), ((), ())),
            precision=lax.Precision.HIGHEST,
        )
        tiny = jnp.concatenate([ggain_a[0], ggain_m[0], grad_table.reshape(-1)])
        tiny = tiny.reshape(-1, 128)
        tiny = tiny + send(tiny, core_pairs)
        for b in [1 << i for i in range(zs.bit_length() - 1)]:
            tiny = tiny + send(tiny, z_pairs[b])
        for b in bits:
            tiny = tiny + send(tiny, rep_pairs[b])
        tiny = tiny.reshape(-1)
        sum_ga = lax.dynamic_slice(tiny, (c * hb,), (hb,))
        sum_gm = lax.dynamic_slice(tiny, (width + c * hb,), (hb,))
        tab = tiny[2 * width :].reshape(n_buckets, heads)
        sum_tab = lax.dynamic_slice(tab, (c * (n_buckets // ss), 0), (n_buckets // ss, heads))

        mix_rows = hb // rs
        late = [
            jnp.concatenate(
                [
                    outer_ring[m],
                    lax.dynamic_slice(mixer_ring, ((r ^ m) * mix_rows, 0), (mix_rows, width)),
                ],
                axis=0,
            )
            for m in range(rs)
        ]
        late = jnp.stack(spread_reps(sum_reps(late, 1), 0))
        late = jnp.take(late, groups, axis=0).astype(F32)
        sum_out = late[:, :sub].reshape(fb, width)
        sum_o = late[:, sub:].reshape(hb, width)

        def halves(final):
            final = jnp.take(jnp.stack(final), groups, axis=0)
            mine = final[:, :hb]
            theirs = send(final[:, hb:], core_pairs)
            low = jnp.where(k == 0, mine, theirs)
            high = jnp.where(k == 0, theirs, mine)
            return jnp.stack([low, high], axis=1)

        inner_final = halves(spread_reps(inner_sum, 1))
        inner_final = inner_final.reshape(rs, 2, hb, zs, sub)
        sum_in = jnp.transpose(inner_final, (2, 3, 1, 0, 4)).reshape(hb, -1).astype(F32)
        heads_final = halves(spread_reps(heads_sum, 0)).reshape(rs, 2, hb, 3, hb)
        heads_final = jnp.transpose(heads_final, (3, 2, 0, 1, 4)).reshape(3, hb, width)
        sum_q, sum_k, sum_v = (heads_final[i].astype(F32) for i in range(3))

        return (
            layer,
            input_grad[None],
            sum_q,
            sum_k,
            sum_v,
            sum_o,
            sum_in,
            sum_out,
            sum_ga,
            sum_gm,
            sum_tab,
        )

    tokens_spec = P(AXES, None, None)
    rows_spec, part_spec = P("shard", None), P("shard")
    in_specs = (
        (tokens_spec,) * 2 + (P(),) * 3 + (rows_spec,) * 6 + (part_spec,) * 2 + (rows_spec,)
    )
    out_specs = (tokens_spec,) * 2 + (rows_spec,) * 6 + (part_spec,) * 2 + (rows_spec,)
    return jax.shard_map(local, mesh=mesh, in_specs=in_specs, out_specs=out_specs, check_vma=False)
```

```python
import functools

import jax
import jax.numpy as jnp
from jax import lax
from jax.experimental import pallas as pl
from jax.experimental.pallas import tpu as pltpu
from jax.sharding import PartitionSpec as P

EPSILON = 1e-06
MASKED = -1000000000.0
AXES = ("rep", "shard")
BF16 = jnp.bfloat16
F32 = jnp.float32
INV_SQRT2 = 0.7071067811865476
INV_SQRT2PI = 0.3989422804014327
PAD = 16

VMEM = pl.BlockSpec(memory_space=pltpu.VMEM)
SMEM = pl.BlockSpec(memory_space=pltpu.SMEM)
ANY = pl.BlockSpec(memory_space=pl.ANY)
HBM = pl.BlockSpec(memory_space=pltpu.HBM)


def shaped(shape, dtype=BF16):
    return jax.ShapeDtypeStruct(shape, dtype)


def kept(shape, dtype=BF16):
    return pltpu.VMEM(shape, dtype)


def stored(shape, dtype=BF16):
    return pltpu.HBM(shape, dtype)


class Sequence:
    def __init__(self):
        self.last = None

    def __call__(self, body, outs, *args, scalars=0, hbm=0, scratch=(), limit=12, after=()):
        n = len(args)
        args = [pltpu.with_memory_space_constraint(a, pltpu.HBM) if i >= n - hbm else a for i, a in enumerate(args)]
        specs = [SMEM] * scalars + [VMEM] * (n - scalars - hbm) + [HBM] * hbm
        extra = list(after) + ([] if self.last is None else [self.last])
        m = len(extra)

        def run(*refs):
            body(*refs[:n], *refs[n + m :])

        result = pl.pallas_call(
            run,
            out_shape=outs,
            in_specs=specs + [ANY] * m,
            out_specs=[VMEM] * len(outs),
            scratch_shapes=list(scratch),
            cost_estimate=pl.CostEstimate(flops=0, bytes_accessed=0, transcendentals=0),
            compiler_params=pltpu.CompilerParams(vmem_limit_bytes=limit * 1024 * 1024),
        )(*args, *extra)
        self.last = result[-1]
        return result

    def arrived(self, value):
        self(token_kernel, [kept((8, 128), F32)], after=[value], limit=4)


def dot(a, b):
    return jnp.dot(a, b, preferred_element_type=F32)


def dot_nt(a, b):
    return lax.dot_general(a, b, (((1,), (1,)), ((), ())), preferred_element_type=F32)


def dot_tn(a, b):
    return lax.dot_general(a, b, (((0,), (0,)), ((), ())), preferred_element_type=F32)


def lanes(block, size):
    return pl.ds(pl.multiple_of(block * size, size), size)


class Geometry:
    def __init__(self, rs, zs, hb, fb, heads, seq_len, width):
        self.rs, self.zs, self.hb, self.fb = rs, zs, hb, fb
        self.seq_len, self.width = seq_len, width
        self.tokens = 2 * seq_len
        self.bits = rs.bit_length() - 1
        self.sub = fb // rs
        self.cols = zs * self.sub
        self.hd = width // heads
        self.nh = hb // self.hd
        self.chips = rs * zs
        self.rows = seq_len // self.chips
        self.aligned = hb % 128 == 0 and self.sub % 128 == 0
        self.parts = width // self.cols

    def turned(self, m):
        out = 0
        for b in range(self.bits):
            out = out + (((m >> b) & 1) << (self.bits - 1 - b))
        return out

    def here(self):
        return Here(self)


class Here:
    def __init__(self, g):
        self.g = g
        self.r = lax.axis_index("rep").astype(jnp.int32)
        c = lax.axis_index("shard").astype(jnp.int32)
        self.z = lax.div(c, jnp.int32(2))
        self.k = lax.rem(c, jnp.int32(2))
        self.me = self.r * (2 * g.zs) + c

    def code(self, m, k=None):
        k = self.k if k is None else k
        return m + k * (self.g.turned(m) - m)

    def quarter(self, m):
        return self.r if m == 0 else lax.bitwise_xor(self.r, self.code(jnp.int32(m)))

    def behind(self, j):
        return self.z if j == 0 else lax.rem(self.z + (self.g.zs - j), jnp.int32(self.g.zs))

    def shard(self, j, h):
        return 2 * self.behind(j) + (1 - self.k if h else self.k)


class Box:
    pass


class Copies:
    def __init__(self, sem):
        self.sem, self.all = sem, []

    def start(self, src, dst):
        copy = pltpu.make_async_copy(src, dst, self.sem)
        copy.start()
        self.all.append(copy)

    def wait(self):
        for copy in self.all:
            copy.wait()


def fetch_heads(g, at, copies, s, core, weights, dst, row):
    hb = g.hb
    for i, w in enumerate(weights):
        part = dst.at[pl.ds(row, hb), pl.ds(i * hb, hb)]
        copies.start(w.at[:, lanes(2 * s + core, hb)], part)


def fetch_inner(g, at, copies, s, core, wi, dst, row, col):
    hb, sub = g.hb, g.sub
    for b in range(g.zs):
        place = pl.ds(pl.multiple_of((2 * b + core) * g.fb + s * sub, sub), sub)
        copies.start(wi.at[:, place], dst.at[pl.ds(row, hb), pl.ds(col + b * sub, sub)])


def send_prep_kernel(g, wq, wk, wv, wi, out, sem):
    at, hb = g.here(), g.hb
    copies, other = Copies(sem), 1 - at.k
    for m in range(g.rs):
        s = lax.bitwise_xor(at.r, at.code(jnp.int32(m), other))
        fetch_heads(g, at, copies, s, other, (wq, wk, wv), out, m * hb)
        fetch_inner(g, at, copies, s, other, wi, out, m * hb, 3 * hb)
    copies.wait()


def attn_prep_kernel(g, small, other, got, wq, wk, wv, wm, out, sem):
    at, hb = g.here(), g.hb
    copies = Copies(sem)
    fetch_heads(g, at, copies, at.r, at.k, (wq, wk, wv), out, 0)
    for h in range(2):
        part = out.at[pl.ds(h * hb, hb), pl.ds(3 * hb, hb)]
        copies.start(wm.at[:, lanes(2 * at.r + h, hb)], part)
    out[hb : 2 * hb, : 3 * hb] = got[:hb, : 3 * hb]
    row = lax.broadcasted_iota(jnp.int32, (PAD, 4 * hb), 0)
    theirs = pltpu.roll(other[...].astype(F32), 1, 0)
    out[2 * hb :, :] = jnp.where(row == 0, small[...].astype(F32), theirs).astype(BF16)
    copies.wait()


def ffn_prep_kernel(g, got, wi, wu, out, sem):
    at, hb, sub, cols = g.here(), g.hb, g.sub, g.cols
    copies = Copies(sem)
    fetch_inner(g, at, copies, at.r, at.k, wi, out, 0, 0)
    for i in range(g.parts):
        part = out.at[pl.ds(2 * hb + i * sub, sub), :]
        copies.start(wu.at[lanes(at.r, sub), pl.ds(i * cols, cols)], part)
    out[hb : 2 * hb, :] = got[:hb, 3 * hb :]
    copies.wait()


def stack_kernel(rows, *refs):
    *ins, out = refs
    for i, ref in enumerate(ins):
        out[i] = ref[:rows, :]


def token_kernel(out):
    out[...] = jnp.zeros_like(out)


def deal_first_kernel(g, labels, src, *outs):
    at = g.here()
    for out, some in zip(outs, labels):
        for i, (f, zz) in enumerate(some):
            chip = lax.bitwise_xor(at.r, at.code(jnp.int32(f))) * g.zs
            out[i] = src[chip + lax.bitwise_xor(at.z, zz)]


def deal_stage_kernel(places, n_in, *refs):
    ins, outs = refs[:n_in], refs[n_in:]
    for out, some in zip(outs, places):
        for i, (a, b) in enumerate(some):
            out[i] = ins[a][b]


def deal_middle_kernel(g, labels, back, table, own, got, *refs):
    outs, (lookup,) = refs[:-1], refs[-1:]
    at = g.here()
    if back:
        for s in range(2 * g.chips):
            lookup[table[s]] = jnp.int32(s)
    else:
        lookup = table
    for out, some in zip(outs, labels):
        for i, (f, zz) in enumerate(some):
            chip = lax.bitwise_xor(at.r, at.code(jnp.int32(f))) * g.zs
            dest = (chip + lax.bitwise_xor(at.z, zz)) * 2 + at.k
            src = lookup[dest]
            core = lax.rem(src, 2)
            src = lax.div(src, 2)
            sz, sr = lax.rem(src, g.zs), lax.div(src, g.zs)
            sf = at.code(lax.bitwise_xor(at.r, sr), core)
            place = sf * g.zs + lax.bitwise_xor(at.z, sz)
            mine = own[place].astype(F32)
            theirs = got[place].astype(F32)
            out[i] = jnp.where(core == at.k, mine, theirs).astype(BF16)


def deal_last_kernel(g, places, n_in, masked, lengths, *refs):
    ins, (out, pool) = refs[:n_in], refs[n_in:]
    at = g.here()
    for e, (a, b) in enumerate(places):
        pool[e] = ins[a][b]
    for chip in range(g.chips):
        f = at.code(lax.bitwise_xor(at.r, chip // g.zs))
        value = pool[f * g.zs + lax.bitwise_xor(at.z, chip % g.zs)]
        if masked:
            row = lax.broadcasted_iota(jnp.int32, value.shape, 0) + chip * g.rows
            value = jnp.where(row < lengths[at.me], value.astype(F32), 0.0).astype(BF16)
        out[chip] = value


def sum_kernel(picks, *refs):
    *ins, out = refs
    total = None
    for ref, pick in zip(ins, picks):
        v = (ref[...] if pick is None else ref[pick]).astype(F32)
        total = v if total is None else total + v
    out[...] = total.astype(out.dtype)


def cut_sum_kernel(g, *refs):
    n = len(refs) - g.zs
    for j, out in enumerate(refs[n:]):
        out[...] = sum(ref[j].astype(F32) for ref in refs[:n]).astype(BF16)


def outer_end_kernel(g, *refs):
    half, sub = g.rs // 2, g.sub
    outs = refs[-2:]
    for i in range(2):
        own, got = refs[2 * i : 2 * i + 2]
        for c in range(half):
            m = i * half + c
            rows = slice(c * sub, (c + 1) * sub)
            v = own[rows, :].astype(F32) + got[rows, :].astype(F32)
            outs[m % 2][m // 2] = v.astype(BF16)


def outer_pair_kernel(g, keep, got, *outs):
    for i, out in enumerate(outs):
        out[...] = (keep[i].astype(F32) + got[i].astype(F32)).astype(BF16)


def inner_split_kernel(g, *refs):
    *ins, keep, give = refs
    total = sum(ref[...].astype(F32) for ref in ins).astype(BF16)
    keep[...] = total[: g.hb]
    give[...] = total[g.hb :]


def ffn_pack_kernel(g, keep, got, *refs):
    *ins, out = refs
    first = g.here().k == 0
    hb, sub = g.hb, g.sub
    for b in range(g.zs):
        cols = slice(b * sub, (b + 1) * sub)
        mine, theirs = keep[:, cols].astype(F32), got[:, cols].astype(F32)
        out[:hb, 2 * b * sub : (2 * b + 1) * sub] = jnp.where(first, mine, theirs).astype(BF16)
        out[:hb, (2 * b + 1) * sub : (2 * b + 2) * sub] = jnp.where(first, theirs, mine).astype(BF16)
    out[hb:, :] = sum(ref[...].astype(F32) for ref in ins).astype(BF16)


def ffn_end_kernel(g, *refs):
    at, parts, (inner, outer) = g.here(), refs[: g.rs], refs[g.rs :]
    hb, sub = g.hb, g.sub
    for m in range(g.rs):
        s = at.quarter(m)
        outer[lanes(s, sub), :] = parts[m][hb:, :].astype(F32)
        if g.aligned:
            for b in range(2 * g.zs):
                place = pl.ds(pl.multiple_of(b * g.fb + s * sub, sub), sub)
                inner[:, place] = parts[m][:hb, b * sub : (b + 1) * sub].astype(F32)
        else:
            inner[s] = parts[m][:hb, : 2 * g.zs * sub].astype(F32)


def attn_split_kernel(g, *refs):
    *ins, keep, mixer, give = refs
    hb = g.hb
    total = sum(ref[...].astype(F32) for ref in ins).astype(BF16)
    keep[:hb, :] = total[:hb, : 3 * hb]
    keep[hb:, :] = total[2 * hb :, : 3 * hb]
    mixer[:, :hb] = total[:hb, 3 * hb :]
    mixer[:, hb:] = total[hb : 2 * hb, 3 * hb :]
    give[:hb, :] = total[hb : 2 * hb, : 3 * hb]
    give[hb:, :] = total[2 * hb :, : 3 * hb]


def attn_pack_kernel(g, keep, mixer, got, out):
    first = g.here().k == 0
    hb = g.hb
    for b in range(3):
        cols = slice(b * hb, (b + 1) * hb)
        mine, theirs = keep[:, cols].astype(F32), got[:, cols].astype(F32)
        out[:, 2 * b * hb : (2 * b + 1) * hb] = jnp.where(first, mine, theirs).astype(BF16)
        out[:, (2 * b + 1) * hb : (2 * b + 2) * hb] = jnp.where(first, theirs, mine).astype(BF16)
    out[:hb, 6 * hb :] = mixer[...]
    out[hb:, 6 * hb :] = jnp.zeros((PAD, 2 * hb), BF16)


def attn_end_kernel(g, *refs):
    at, parts, outs = g.here(), refs[: g.rs], refs[g.rs :]
    hb, size = g.hb, 2 * g.hb
    gains, table = outs[4:]
    total = None
    for m in range(g.rs):
        q = at.quarter(m)
        for i in range(4):
            outs[i][:, lanes(q, size)] = parts[m][:hb, size * i : size * (i + 1)].astype(F32)
        tiles = parts[m][hb:, :].astype(F32)
        pair = []
        for core in range(2):
            both = [tiles[:, (2 * b + core) * hb : (2 * b + core + 1) * hb] for b in range(3)]
            for i in range(g.nh):
                head = (2 * q + core) * g.nh + i
                table[pl.ds(head, 1), :] = both[2][2 + i : 3 + i, :]
            pair.append(both)
        own = [jnp.where(at.k == 0, pair[0][b][0:1], pair[1][b][0:1]) for b in range(2)]
        their = [jnp.where(at.k == 0, pair[1][b][1:2], pair[0][b][1:2]) for b in range(2)]
        some = [own[b] + their[b] for b in range(2)]
        total = some if total is None else [total[b] + some[b] for b in range(2)]
    for b in range(2):
        gains[b : b + 1, :] = total[b]


def to_relative(g, at, src, dst):
    hb = g.hb
    for j in range(g.zs):
        for h in range(2):
            e = 2 * j + h
            dst[:, e * hb : (e + 1) * hb] = src[:, lanes(at.shard(j, h), hb)]


def norm_kernel(g, own, sib, gain, normed, normed_t, scaled, *scratch):
    half = own.shape[0]
    plain, plain_scaled = scratch if g.aligned else (normed, scaled)
    for start, src in ((0, own), (half, sib)):
        v = src[...].astype(F32)
        scale = lax.rsqrt(jnp.mean(v * v, axis=-1, keepdims=True) + EPSILON)
        plain[start : start + half, :] = (v * scale * gain[...]).astype(BF16)
        plain_scaled[start : start + half, :] = (v * scale).astype(BF16)
    if g.aligned:
        to_relative(g, g.here(), plain, normed)
        to_relative(g, g.here(), plain_scaled, scaled)
    normed_t[...] = normed[...].T


def toeplitz(row, n):
    wide = jnp.broadcast_to(row, (n, 2 * n))
    return pltpu.roll(wide, n + 1, 1, stride=1, stride_axis=0)[:, :n]


def probabilities(q, kk, bias, length):
    n = q.shape[0]
    s = dot_nt(q, kk) + bias
    col = lax.broadcasted_iota(jnp.int32, (n, n), 1)
    s = jnp.where(col < length, s, MASKED)
    e = jnp.exp(s - jnp.max(s, axis=-1, keepdims=True))
    return e * (1.0 / jnp.sum(e, axis=-1, keepdims=True))


def two_lengths(at, lengths):
    return lengths[at.me], lengths[lax.bitwise_xor(at.me, 1)]


def attn_kernel(g, m, lengths, normed, off, first, rest, *refs):
    hb, hd = g.hb, g.hd
    at = g.here()
    both = two_lengths(at, lengths)
    if m == 0 or not g.aligned:
        qkv, mixed, w = refs
        w[: 2 * hb, :] = first[: 2 * hb, : 3 * hb]
        copies = None
    else:
        weights, (qkv, mixed, w, sem) = refs[:3], refs[3:]
        copies = Copies(sem)
        fetch_heads(g, at, copies, at.quarter(m), at.k, weights, w, 0)
        w[hb : 2 * hb, :] = first[m * hb : (m + 1) * hb, : 3 * hb]
    for j in range(1, g.zs):
        w[2 * hb * j : 2 * hb * (j + 1), :] = rest[j - 1, :, : 3 * hb]
    if copies is not None:
        copies.wait()
    qkv[...] = dot(normed[...], w[...]).astype(BF16)
    half = normed.shape[0] // 2
    for h in range(g.nh):
        bias = toeplitz(off[h : h + 1, :], half)
        for s in range(2):
            rows = slice(s * half, (s + 1) * half)
            q, kk, v = (qkv[rows, i * hb + h * hd : i * hb + (h + 1) * hd] for i in range(3))
            p = probabilities(q, kk, bias, both[s]).astype(BF16)
            mixed[rows, h * hd : (h + 1) * hd] = dot(p, v).astype(BF16)


def turned_head(g, at, block):
    return at.code(lax.bitwise_xor(block, at.r))


def mixer_kernel(g, *refs):
    rs, zs, hb = g.rs, g.zs, g.hb
    at = g.here()
    mixed_parts, own, rest = refs[:rs], refs[rs], refs[rs + 1 : 2 * rs + 1]
    mixed, wo, partial = refs[2 * rs + 1 :]
    for m in range(rs):
        mixed[:, m * hb : (m + 1) * hb] = mixed_parts[m][...]
    wo[lanes(turned_head(g, at, at.z), hb), :] = own[...]
    for m in range(rs):
        for j in range(1, zs):
            rows = lanes(turned_head(g, at, at.behind(j)), hb)
            piece = rest[m][j - 1, :, 3 * hb :]
            both = jnp.concatenate([piece[:hb], piece[hb:]], axis=1)
            wo[rows, lanes(at.quarter(m), 2 * hb)] = both
    partial[...] = dot(mixed[...], wo[...]).astype(BF16)


def middle_kernel(g, own, sib, part, other, gain, *refs):
    middle, normed2, normed2_t = refs[:3]
    plain = refs[3] if g.aligned else normed2
    half = own.shape[0]
    for s, src in ((0, own), (1, sib)):
        rows = slice(s * half, (s + 1) * half)
        swapped = slice((1 - s) * half, (2 - s) * half)
        v = src[...].astype(F32) + part[rows, :].astype(F32) + other[swapped, :].astype(F32)
        middle[rows, :] = v
        scale = lax.rsqrt(jnp.mean(v * v, axis=-1, keepdims=True) + EPSILON)
        plain[rows, :] = (v * scale * gain[...]).astype(BF16)
    if g.aligned:
        to_relative(g, g.here(), plain, normed2)
    normed2_t[...] = normed2[...].T


def ffn_kernel(g, chunks, last, normed2, normed2_t, *refs):
    hb, sub, zs, cols = g.hb, g.sub, g.zs, g.cols
    at = g.here()
    half = g.seq_len
    n = chunks
    rest, refs = refs[: n * (zs - 1)], refs[n * (zs - 1) :]
    firsts, refs = refs[: n if not g.aligned else 2 - last], refs[n if not g.aligned else 2 - last :]
    if last:
        gl, outer_in, gn2_in, refs = *refs[:3], refs[3:]
    else:
        gl_own, gl_sib, refs = *refs[:2], refs[2:]
    if g.aligned:
        wi, wu, refs = *refs[:2], refs[2:]
    if last:
        outer_own, swap, refs = *refs[:2], refs[2:]
    else:
        gl, outer, gn2, refs = *refs[:3], refs[3:]
        gl[:half, :] = gl_own[...]
        gl[half:, :] = gl_sib[...]
    grads, outs, refs = refs[:n], refs[n : n + zs], refs[n + zs :]
    w1s, w2s, go = refs[:n], refs[n : 2 * n], refs[2 * n]
    copies = Copies(refs[2 * n + 1]) if g.aligned else None
    for i in range(n):
        m = i + (n if last else 0)
        w1, w2 = w1s[i], w2s[i]
        mine = pl.ds(pl.multiple_of(at.z * sub, sub), sub)
        if m and g.aligned:
            s = at.quarter(m)
            fetch_inner(g, at, copies, s, at.k, wi, w1, 0, 0)
            copies.start(wu.at[lanes(s, sub), :], w2.at[mine, :])
            w1[hb : 2 * hb, :] = firsts[-1][m * hb : (m + 1) * hb, 3 * hb :]
        else:
            piece = firsts[i]
            w1[: 2 * hb, :] = piece[: 2 * hb, :]
            for b in range(g.parts):
                rows = slice(2 * hb + b * sub, 2 * hb + (b + 1) * sub)
                w2[mine, b * cols : (b + 1) * cols] = piece[rows, :]
        for j in range(1, zs):
            piece = rest[i * (zs - 1) + j - 1]
            w1[2 * hb * j : 2 * hb * (j + 1), :] = piece[: 2 * hb, :]
            place = lanes(at.behind(j), sub)
            for b in range(g.parts):
                rows = slice(2 * hb + b * sub, 2 * hb + (b + 1) * sub)
                w2[place, b * cols : (b + 1) * cols] = piece[rows, :]
    if copies is not None:
        copies.wait()
    out_sum, gn_sum = None, None
    for i in range(n):
        w1, w2 = w1s[i], w2s[i]
        h = dot(normed2[...], w1[...])
        cdf = 0.5 * (1.0 + lax.erf(h * INV_SQRT2))
        pdf = jnp.exp(-0.5 * h * h) * INV_SQRT2PI
        act = (h * cdf).astype(BF16)
        ga = dot_nt(gl[...], w2[...])
        gh = (ga * (cdf + h * pdf)).astype(BF16)
        grads[i][...] = dot(normed2_t[...], gh).astype(BF16).reshape(zs, 2 * hb, cols)
        full = dot_tn(act, gl[...]).astype(BF16)
        for b in range(zs):
            place = lax.rem(at.z + (zs - b), zs)
            go[place, i * sub : (i + 1) * sub, :] = full[b * sub : (b + 1) * sub, :]
        out_part = dot(act, w2[...])
        gn_part = dot_nt(gh, w1[...])
        out_sum = out_part if out_sum is None else out_sum + out_part
        gn_sum = gn_part if gn_sum is None else gn_sum + gn_part
    for j in range(zs):
        outs[j][...] = go[j]
    if last:
        out_sum = out_sum + outer_in[...]
        outer_own[...] = out_sum[:half]
        swap[g.tokens :, :] = out_sum[half:].astype(BF16)
        swap[: g.tokens, :] = (gn_sum + gn2_in[...]).astype(BF16)
    else:
        outer[...] = out_sum
        gn2[...] = gn_sum


def absolute_sum(g, at, part, other, rows, swapped, total):
    hb = g.hb
    if not g.aligned:
        total[...] = part[rows, :].astype(F32) + other[swapped, :].astype(F32)
        return
    for j in range(g.zs):
        for h in range(2):
            mine, theirs = 2 * j + h, 2 * j + 1 - h
            a = part[rows, mine * hb : (mine + 1) * hb].astype(F32)
            b = other[swapped, theirs * hb : (theirs + 1) * hb].astype(F32)
            total[:, lanes(at.shard(j, h), hb)] = a + b


def middle_back_kernel(g, part, other, middle, gl, gain, mixed, wo, *refs):
    grad_mid, gm, ggain, gwo, gatt, total = refs[:6]
    at, hb = g.here(), g.hb
    half, width = g.seq_len, g.width
    for s in range(2):
        rows = slice(s * half, (s + 1) * half)
        swapped = slice((1 - s) * half, (2 - s) * half)
        absolute_sum(g, at, part, other, rows, swapped, total)
        gn = total[...]
        v = middle[rows, :]
        scale = lax.rsqrt(jnp.mean(v * v, axis=-1, keepdims=True) + EPSILON)
        gg = gn * gain[...]
        inner = jnp.sum(gg * v, axis=-1, keepdims=True) * (1.0 / width)
        grad = gl[rows, :].astype(F32) + scale * gg - v * (scale * scale * scale * inner)
        if s == 0:
            grad_mid[...] = grad
            sums = jnp.sum(gn * v * scale, axis=0, keepdims=True)
            if g.aligned:
                refs[6][...] = sums
                to_relative(g, at, refs[6], ggain)
            else:
                ggain[...] = sums
        gatt[rows, :] = grad.astype(BF16)
    gm[...] = dot_nt(gatt[...], wo[...]).astype(BF16)
    full = dot_tn(mixed[...], gatt[...]).astype(BF16)
    for m in range(g.rs):
        place = lax.rem(at.z + (g.zs - at.quarter(m)), g.zs)
        gwo[place] = full[m * hb : (m + 1) * hb, :]


def attn_back_kernel(g, m, step, lengths, normed_t, off, qkv, gmix, gwo, hot, scaled, w, *refs):
    hb, hd = g.hb, g.hd
    at = g.here()
    both = two_lengths(at, lengths)
    half = g.seq_len
    extra, refs = (refs[:1], refs[1:]) if m == 0 else ((), refs)
    before, refs = (refs[0], refs[1:]) if step else (None, refs)
    gw, *gn, gqkv = refs
    flip = (
        lax.broadcasted_iota(jnp.int32, (half, half), 0)
        + lax.broadcasted_iota(jnp.int32, (half, half), 1)
        == half - 1
    ).astype(BF16)
    table = []
    for h in range(g.nh):
        bias = toeplitz(off[h : h + 1, :], half)
        flipped = jnp.zeros((half, half), F32)
        for s in range(2):
            rows = slice(s * half, (s + 1) * half)
            q, kk, v = (qkv[rows, i * hb + h * hd : i * hb + (h + 1) * hd] for i in range(3))
            gm = gmix[rows, m * hb + h * hd : m * hb + (h + 1) * hd]
            p = probabilities(q, kk, bias, both[s])
            gp = dot_nt(gm, v)
            delta = jnp.sum(p * gp, axis=-1, keepdims=True)
            gs = (p * (gp - delta)).astype(BF16)
            flipped = flipped + dot(flip, gs)
            cols = [slice(i * hb + h * hd, i * hb + (h + 1) * hd) for i in range(3)]
            gqkv[rows, cols[0]] = dot(gs, kk).astype(BF16)
            gqkv[rows, cols[1]] = dot_tn(gs, q).astype(BF16)
            gqkv[rows, cols[2]] = dot_tn(p.astype(BF16), gm).astype(BF16)
        wide = jnp.concatenate([flipped, jnp.zeros((half, half), F32)], axis=1)
        skewed = pltpu.roll(wide, 0, 1, stride=1, stride_axis=0)
        diag = jnp.broadcast_to(jnp.sum(skewed, axis=0, keepdims=True), (8, 2 * half))
        top = diag.astype(BF16)
        table.append(dot_nt(top, hot[...]) + dot_nt((diag - top.astype(F32)).astype(BF16), hot[...]))
    gw[:, : 2 * hb, : 3 * hb] = (
        dot(normed_t[...], gqkv[...]).astype(BF16).reshape(g.zs, 2 * hb, 3 * hb)
    )
    row = lax.broadcasted_iota(jnp.int32, (PAD, hb), 0)
    buckets = jnp.zeros((PAD, hb), F32)
    for i, t in enumerate(table):
        buckets = jnp.where(row == 2 + i, jnp.broadcast_to(t[0:1], (PAD, hb)), buckets)
    for j in range(g.zs):
        piece = gwo[j, :, lanes(at.quarter(m), 2 * hb)]
        gw[j, :hb, 3 * hb :] = piece[:, :hb]
        gw[j, hb : 2 * hb, 3 * hb :] = piece[:, hb:]
        part = dot_nt(gqkv[...], w[2 * hb * j : 2 * hb * (j + 1), :])
        cols = slice(2 * hb * j, 2 * hb * (j + 1))
        gain = jnp.sum(part * scaled[:, cols].astype(F32), axis=0, keepdims=True)
        tile = [gain[:, :hb], gain[:, hb:]]
        tile = jnp.where(row == 0, tile[0], jnp.where(row == 1, tile[1], 0.0))
        gw[j, 2 * hb :, :hb] = tile.astype(BF16)
        if m == 0:
            tile = [extra[0][:, (2 * j + h) * hb : (2 * j + h + 1) * hb] for h in range(2)]
            tile = jnp.where(row == 0, tile[0], jnp.where(row == 1, tile[1], 0.0))
        else:
            tile = jnp.zeros((PAD, hb), F32)
        gw[j, 2 * hb :, hb : 2 * hb] = tile.astype(BF16)
        gw[j, 2 * hb :, 2 * hb : 3 * hb] = buckets.astype(BF16)
        gw[j, 2 * hb :, 3 * hb :] = jnp.zeros((PAD, hb), BF16)
        if before is not None:
            part = part + before[:, cols]
        if len(gn) == 1:
            gn[0][:, cols] = part
        else:
            gn[0][:, cols] = part[:half]
            gn[1][:, cols] = part[half:].astype(BF16)


def input_back_kernel(g, own, other, grad_mid, x, gain, out, total):
    everything = slice(None)
    absolute_sum(g, g.here(), own, other, everything, everything, total)
    gn = total[...]
    v = x[...].astype(F32)
    scale = lax.rsqrt(jnp.mean(v * v, axis=-1, keepdims=True) + EPSILON)
    gg = gn * gain[...]
    inner = jnp.mean(gg * v, axis=-1, keepdims=True)
    grad = grad_mid[...] + scale * gg - v * (scale * scale * scale * inner)
    out[...] = grad.astype(BF16)


def layer_kernel(g, lengths, middle, own, other, out):
    half = own.shape[0]
    row = lax.broadcasted_iota(jnp.int32, own.shape, 0)
    v = middle[:half, :] + own[...] + other[g.tokens :, :].astype(F32)
    out[...] = jnp.where(row < lengths[g.here().me], v, 0.0).astype(BF16)


CORE, SMALL, INPUT, MIDDLE, SWAP, NORMED, INNER, ATTN, COT, COT_SIB, LAYER = range(11)
RING_A, RING_F, HOP_A, HOP_F, GI, GI_SUM, GH, GH_SUM, OA, OB, LATE, SPREAD_F, SPREAD_T = range(11, 24)

ORDER = (
    4, 0, ((COT, 0), 2), 5, 1, 6, 7, 3, 2, 12, 14, 8, 13, 15, 9, ((HOP_F, 1), 2), 16, 10,
    ((HOP_F, 1), 3), 17, ((HOP_F, 3), 3), ((COT, 5), 0), ((COT, 5), 2), 18, 11, ((HOP_F, 3), 2),
    ((COT, 0), 0), 19, 20, 21, 23, 24, 22, 28, 32, 29, 31, 25, 33, (GI, 2), 26, 36, 30, 34, 44, 27,
    46, 37, 35, 48, 45, 47, 38, 50, 51, 49, 39, 40, 52, 41, 53, (SPREAD_F, 2), 42, 43, 54, 55,
)


def solution(mesh):
    rs, ss = mesh.shape["rep"], mesh.shape["shard"]
    zs = ss // 2
    count = rs * ss
    nb = rs.bit_length() - 1

    def pairs(move):
        table = []
        for i in range(count):
            r, z, k = i // ss, (i % ss) // 2, i % 2
            r, z, k = move(r, z, k)
            table.append((i, (r * zs + z) * 2 + k))
        return table

    core_pairs = pairs(lambda r, z, k: (r, z, 1 - k))
    up_pairs = pairs(lambda r, z, k: (r, (z + 1) % zs, k))
    rep_pairs = [
        pairs(lambda r, z, k, b=b: (r ^ (1 << (nb - 1 - b if k else b)), z, k)) for b in range(nb)
    ]
    z_pairs = {m: pairs(lambda r, z, k, m=m: (r, z ^ m, k)) for m in range(1, zs)}

    def send(value, table):
        return lax.ppermute(value, AXES, table)

    by_size = sorted(range(1, rs), key=lambda m: (bin(m).count("1"), m))

    def high(m):
        return m.bit_length() - 1

    def low(m):
        return (m & -m).bit_length() - 1

    def local(
        inputs,
        cotangent,
        seq_lengths,
        dealing,
        rel_buckets,
        w_query,
        w_key,
        w_value,
        w_mixer,
        w_inner,
        w_outer,
        gain_attn,
        gain_mlp,
        bias_table,
    ):
        seq = Sequence()
        bind = functools.partial
        n_buckets, heads = bias_table.shape[0] * ss, bias_table.shape[1]
        g = Geometry(rs, zs, w_query.shape[0], w_outer.shape[0], heads, *inputs.shape[1:])
        hb, fb, sub, cols, nh = g.hb, g.fb, g.sub, g.cols, g.nh
        seq_len, width, tokens = g.seq_len, g.width, g.tokens
        chips, rows = g.chips, g.rows
        chunks = rs // 2

        r, c = lax.axis_index("rep"), lax.axis_index("shard")
        z, k = c // 2, c % 2
        shards = jnp.arange(ss, dtype=jnp.int32)
        x_own = inputs[0]
        d = Box()
        parts = {}

        def relative():
            return 2 * ((z + zs - shards // 2) % zs) + (k ^ (shards % 2))

        def permute_cols(x, order):
            return jnp.take(x.reshape(-1, ss, hb), order, axis=1).reshape(x.shape)

        val = {}
        steps = []

        def put(name, value, table):
            val[name] = send(value, table)

        def step(run, *args):
            steps.append(bind(run, *args))

        labels = [(f, zz) for f in range(rs) for zz in range(zs)]

        def groups_of(stage):
            if stage == nb:
                return [[e for e in labels if e[1] == zz] for zz in range(zs)]
            clear = [e for e in labels if not (e[0] >> stage) & 1]
            return [clear, [e for e in labels if e not in clear]]

        def block_shapes(groups):
            outs = [shaped((len(some), rows, width)) for some in groups]
            return outs if len(outs) == 1 else [stored(outs[0].shape)] + outs[1:]

        def dispatch(key, outs, stage):
            groups = groups_of(stage)
            val[key] = outs[0]
            state = [(key, groups[0])]
            for i, (out, some) in enumerate(zip(outs[1:], groups[1:])):
                put((key, i), out, z_pairs[i + 1] if stage == nb else rep_pairs[stage])
                state.append(((key, i), some))
            return state

        def places(state, some):
            at = {e: (a, b) for a, (_, named) in enumerate(state) for b, e in enumerate(named)}
            return [at[e] for e in some]

        def values(state):
            return [val[name] for name, _ in state]

        def deal_first(what, stage):
            groups = groups_of(stage)
            value = parts[what].reshape(chips, rows, width)
            outs = seq(bind(deal_first_kernel, g, groups), block_shapes(groups), value)
            parts[what] = dispatch((what, 0), outs, stage)

        def deal_stage(what, number, stage):
            groups, state = groups_of(stage), parts[what]
            body = bind(deal_stage_kernel, [places(state, some) for some in groups], len(state))
            outs = seq(body, block_shapes(groups), *values(state))
            parts[what] = dispatch((what, number), outs, stage)

        def deal_core(what):
            state = parts[what]
            body = bind(deal_stage_kernel, [places(state, labels)], len(state))
            parts[what] = seq(body, block_shapes([labels]), *values(state))[0]
            put((what, CORE), parts[what], core_pairs)

        def deal_middle(what, number, stage, back):
            groups = groups_of(stage)
            body = bind(deal_middle_kernel, g, groups, back)
            lookup = [pltpu.SMEM((count,), jnp.int32)]
            args = dealing, parts[what], val[what, CORE]
            outs = seq(body, block_shapes(groups), *args, scalars=1, scratch=lookup)
            parts[what] = dispatch((what, number), outs, stage)

        def deal_last(what, masked):
            state = parts[what]
            body = bind(deal_last_kernel, g, places(state, labels), len(state), masked)
            pool = [pltpu.VMEM((chips, rows, width), BF16)]
            shape = [shaped((chips, rows, width))]
            out = seq(body, shape, seq_lengths, *values(state), scalars=1, scratch=pool)[0]
            parts[what] = out.reshape(seq_len, width)

        def deal(what, first, second, back, end):
            step(deal_first, what, first[0])
            for i, stage in list(enumerate(first))[1:]:
                step(deal_stage, what, i, stage)
            step(deal_core, what)
            n = len(first)
            step(deal_middle, what, n, second[0], back)
            for i, stage in list(enumerate(second))[1:]:
                step(deal_stage, what, n + i, stage)
            step(end)

        copy_sem = pltpu.SemaphoreType.DMA(())

        def slices(m, core):
            s = r ^ (m + core * (g.turned(m) - m))
            at = (2 * s + core) * hb
            parts = [lax.dynamic_slice(w, (0, at), (hb, hb)) for w in (w_query, w_key, w_value)]
            at = [(2 * b + core) * fb + s * sub for b in range(zs)]
            inner = [lax.dynamic_slice(w_inner, (0, a), (hb, sub)) for a in at]
            mix = lax.dynamic_slice(w_mixer, (0, s * 2 * hb), (hb, 2 * hb))
            outer = lax.dynamic_slice(w_outer, (s * sub, 0), (sub, width))
            outer = [outer[:, i * cols : (i + 1) * cols] for i in range(g.parts)]
            return parts, inner, mix, outer

        def start_core():
            if g.aligned:
                sent = seq(
                    bind(send_prep_kernel, g),
                    [shaped((rs * hb, 3 * hb + cols))],
                    w_query,
                    w_key,
                    w_value,
                    w_inner,
                    hbm=4,
                    scratch=[copy_sem],
                )[0]
            else:
                sent = []
                for m in range(rs):
                    parts, inner, _, _ = slices(m, 1 - k)
                    sent.append(jnp.concatenate(parts + inner, axis=1))
                sent = jnp.concatenate(sent, axis=0)
            put(CORE, sent, core_pairs)
            small = jnp.concatenate([gain_attn, gain_mlp, bias_table.reshape(-1)])
            d.n_small = small.shape[0]
            d.small = jnp.pad(small[None], ((0, PAD - 1), (0, 4 * hb - small.shape[0])))
            put(SMALL, d.small, core_pairs)

        def start_attn():
            got = val[CORE]
            if g.aligned:
                own = seq(
                    bind(attn_prep_kernel, g),
                    [shaped((2 * hb + PAD, 4 * hb))],
                    d.small,
                    val[SMALL],
                    got,
                    w_query,
                    w_key,
                    w_value,
                    w_mixer,
                    hbm=4,
                    scratch=[copy_sem],
                )
            else:
                own = []
                for m in range(rs):
                    parts, _, mix, _ = slices(m, k)
                    top = jnp.concatenate(parts + [mix[:, :hb]], axis=1)
                    bottom = [got[m * hb : (m + 1) * hb, : 3 * hb], mix[:, hb:]]
                    own.append(jnp.concatenate([top, jnp.concatenate(bottom, axis=1)], axis=0))
                mine, theirs = d.small, val[SMALL]
                both = jnp.concatenate([mine[:1], theirs[:1], mine[2:]], axis=0)
                own[0] = jnp.concatenate([own[0], both], axis=0)
            d.attn_own = own
            ring(RING_A, own[0])

        def start_ffn():
            got = val[CORE]
            if g.aligned:
                own = seq(
                    bind(ffn_prep_kernel, g),
                    [shaped((4 * hb, cols))],
                    got,
                    w_inner,
                    w_outer,
                    hbm=2,
                    scratch=[copy_sem],
                )
            else:
                own = []
                for m in range(rs):
                    _, inner, _, outer = slices(m, k)
                    bottom = got[m * hb : (m + 1) * hb, 3 * hb :]
                    own.append(
                        jnp.concatenate([jnp.concatenate(inner, axis=1), bottom] + outer, axis=0)
                    )
            d.ffn_own = own
            ring(RING_F, own[0])
            for j in range(1, zs):
                hops((HOP_F, j), val[RING_F, j])

        def ring(name, value):
            for j in range(1, zs):
                put((name, j), value if j == 1 else val[name, j - 1], up_pairs)

        def hops(name, value):
            val[name, 0] = value
            for m in by_size:
                put((name, m), val[name, m ^ (1 << high(m))], rep_pairs[high(m)])

        def stack_attn():
            pieces = [val[RING_A, j] for j in range(1, zs)]
            shape = [shaped((zs - 1, 2 * hb, 4 * hb))]
            hops(HOP_A, seq(bind(stack_kernel, 2 * hb), shape, *pieces)[0])

        def rest_of(j, m):
            return val[(HOP_F, j), m]

        def small_params():
            n_small = d.n_small
            pieces = [d.attn_own[0]] + [val[RING_A, j] for j in range(1, zs)]
            some = [piece[2 * hb : 2 * hb + 2, :n_small] for piece in pieces]
            order = (shards[:, None] == relative()[None, :]).astype(BF16)
            some = dot(order, jnp.concatenate(some, axis=0))
            d.gain_a = some[:, :hb].reshape(1, width)
            d.gain_m = some[:, hb : 2 * hb].reshape(1, width)
            table = some[:, 2 * hb :].reshape(n_buckets, heads)
            quarters = jnp.arange(rs, dtype=jnp.int32)
            quarters = r ^ (quarters + k * (g.turned(quarters) - quarters))
            head_ids = ((2 * quarters + k) * nh)[:, None] + jnp.arange(nh, dtype=jnp.int32)[None]
            pick = jnp.arange(heads, dtype=jnp.int32)[:, None] == head_ids.reshape(1, -1)
            padded = jnp.concatenate([rel_buckets, jnp.full((1,), -1, jnp.int32)])
            hot = padded[None, :] == jnp.arange(hb, dtype=jnp.int32)[:, None]
            d.hot = hot.astype(BF16)
            my_table = dot(table.astype(BF16), pick.astype(BF16)).astype(BF16)
            d.offsets = lax.dot_general(
                my_table,
                d.hot[:n_buckets],
                (((0,), (0,)), ((), ())),
                preferred_element_type=F32,
            ).reshape(rs, nh, 2 * seq_len)

        spare = [pltpu.VMEM((tokens, width), BF16)] if g.aligned else []

        def norm():
            small_params()
            normed, normed_t, scaled = seq(
                bind(norm_kernel, g),
                [shaped((tokens, width)), stored((width, tokens)), stored((tokens, width))],
                x_own,
                val[INPUT],
                d.gain_a,
                scratch=spare * 2,
            )
            if not g.aligned:
                normed = permute_cols(normed, relative())
                scaled = permute_cols(scaled, relative())
                normed_t = normed.T
            d.normed, d.normed_t, d.scaled = normed, normed_t, scaled
            d.qkv, d.mixed_parts, d.attn_w = ([None] * rs for _ in range(3))

        def attend(m):
            own = m == 0 or not g.aligned
            weights = () if own else (w_query, w_key, w_value)
            d.qkv[m], d.mixed_parts[m], d.attn_w[m] = seq(
                bind(attn_kernel, g, m),
                [stored((tokens, 3 * hb)), stored((tokens, hb)), stored((width, 3 * hb))],
                seq_lengths,
                d.normed,
                d.offsets[m],
                d.attn_own[m] if own else val[CORE],
                val[HOP_A, m],
                *weights,
                scalars=1,
                hbm=len(weights),
                scratch=() if own else [copy_sem],
            )

        def mixer():
            d.mixed, d.wo, d.partial = seq(
                bind(mixer_kernel, g),
                [stored((tokens, rs * hb)), stored((rs * hb, width)), shaped((tokens, width))],
                *d.mixed_parts,
                w_mixer,
                *[val[HOP_A, m] for m in range(rs)],
            )
            put(MIDDLE, d.partial, core_pairs)

        def middle():
            d.middle, normed2, normed2_t = seq(
                bind(middle_kernel, g),
                [stored((tokens, width), F32), shaped((tokens, width)), shaped((width, tokens))],
                x_own,
                val[INPUT],
                d.partial,
                val[MIDDLE],
                d.gain_m,
                scratch=spare,
            )
            if not g.aligned:
                normed2 = permute_cols(normed2, relative())
                normed2_t = normed2.T
            d.normed2, d.normed2_t = normed2, normed2_t

        def ffn(part):
            some = range(part * chunks, (part + 1) * chunks)
            if not g.aligned:
                firsts = [d.ffn_own[m] for m in some]
            else:
                firsts = ([] if part else [d.ffn_own[0]]) + [val[CORE]]
            if part == 0:
                more = parts[COT], val[COT_SIB]
                head = [shaped((tokens, width))] + [shaped((tokens, width), F32)] * 2
            else:
                more = (d.gl, *d.acc)
                head = [shaped((seq_len, width), F32), shaped((tokens + seq_len, width))]
            weights = (w_inner, w_outer) if g.aligned else ()
            scratch = [pltpu.VMEM((width, cols), BF16)] * chunks
            scratch += [pltpu.VMEM((cols, width), BF16)] * chunks
            scratch += [pltpu.VMEM((zs, chunks * sub, width), BF16)]
            outs = seq(
                bind(ffn_kernel, g, chunks, part == 1),
                head
                + [shaped((zs, 2 * hb, cols))] * chunks
                + [shaped((chunks * sub, width))] * zs,
                d.normed2,
                d.normed2_t,
                *[rest_of(j, m) for m in some for j in range(1, zs)],
                *firsts,
                *more,
                *weights,
                hbm=len(weights),
                scratch=scratch + ([copy_sem] if g.aligned else []),
                limit=28,
            )
            parts[GI] = (parts[GI] if part else []) + list(outs[len(head) : -zs])
            parts[(OA, OB)[part]] = outs[-zs:]
            if part == 0:
                d.gl, d.acc = outs[0], outs[1:3]
            else:
                d.outer_part, swap = outs[:2]
                if not g.aligned:
                    first = permute_cols(swap[:tokens], jnp.argsort(relative()))
                    swap = jnp.concatenate([first, swap[tokens:]], axis=0)
                d.swap = swap
                put(SWAP, swap, core_pairs)
            for m in some:
                if m % 2:
                    hop_start(GI, m)
            name = (OA, OB)[part]
            put((name, 1), parts[name][1], up_pairs)

        def add(*terms):
            shape = [shaped(terms[0].shape)]
            return seq(bind(sum_kernel, [None] * len(terms)), shape, *terms)[0]

        def sum_step(name, j):
            put((name, j), add(val[name, j - 1], parts[name][j]), up_pairs)

        def hop_start(name, m):
            put((name, m), parts[name][m], rep_pairs[low(m)])

        def hop_add(name, ring, m):
            some = parts[name]
            bits = [b for b in range(nb) if not (m >> b) & 1 and low(m | 1 << b) == b]
            terms = [some[m]] + [val[name, m | 1 << b] for b in bits]
            if m:
                some[m] = add(*terms)
                hop_start(name, m)
            else:
                shape = [shaped(some[0].shape[1:])] * zs
                parts[ring] = seq(bind(cut_sum_kernel, g), shape, *terms)
                put((ring, 1), parts[ring][1], up_pairs)

        def outer_end():
            half, last = rs // 2, zs - 1
            d.late, give = seq(
                bind(outer_end_kernel, g),
                [shaped((half, sub, width))] * 2,
                parts[OA][0],
                val[OA, last],
                parts[OB][0],
                val[OB, last],
            )
            put((LATE, 1), give, rep_pairs[0])

        def outer_pair():
            half = rs // 2
            shape = [shaped((sub, width))] * half
            parts = list(seq(bind(outer_pair_kernel, g), shape, d.late, val[LATE, 1]))
            d.late, names = parts, []
            for i in range(half - 1, 0, -1):
                b = low(i)
                put((LATE, i + 1), parts[i], rep_pairs[b + 1])
                if i ^ (1 << b):
                    parts[i ^ (1 << b)] = add(parts[i ^ (1 << b)], val[LATE, i + 1])
                else:
                    names.append((LATE, i + 1))
            d.late_names = names

        def inner_split():
            keep, give = seq(
                bind(inner_split_kernel, g),
                [shaped((hb, cols))] * 2,
                parts[GI_SUM][0],
                val[GI_SUM, zs - 1],
            )
            d.inner_keep = keep
            put(INNER, give, core_pairs)

        def ffn_pack():
            late = [d.late[0]] + [val[name] for name in d.late_names]
            shape = [shaped((hb + sub, width))]
            body = bind(ffn_pack_kernel, g)
            hops(SPREAD_F, seq(body, shape, d.inner_keep, val[INNER], *late)[0])

        def ffn_end():
            shape = (hb, 2 * zs * fb) if g.aligned else (rs, hb, 2 * zs * sub)
            inner, d.sum_out = seq(
                bind(ffn_end_kernel, g),
                [stored(shape, F32), stored((fb, width), F32)],
                *[val[SPREAD_F, m] for m in range(rs)],
            )
            if not g.aligned:
                inner = jnp.transpose(inner.reshape(rs, hb, 2 * zs, sub), (1, 2, 0, 3))
                inner = inner.reshape(hb, -1)
            d.sum_in = inner

        def attn_split():
            d.attn_keep, d.mixer_keep, give = seq(
                bind(attn_split_kernel, g),
                [
                    shaped((hb + PAD, 3 * hb)),
                    shaped((hb, 2 * hb)),
                    shaped((hb + PAD, 3 * hb)),
                ],
                parts[GH_SUM][0],
                val[GH_SUM, zs - 1],
            )
            put(ATTN, give, core_pairs)

        def attn_pack():
            shape = [shaped((hb + PAD, 8 * hb))]
            args = d.attn_keep, d.mixer_keep, val[ATTN]
            hops(SPREAD_T, seq(bind(attn_pack_kernel, g), shape, *args)[0])

        def attn_end():
            *d.sum_attn, d.gains, d.table = seq(
                bind(attn_end_kernel, g),
                [stored((hb, width), F32)] * 4 + [shaped((8, hb), F32), shaped((heads, hb), F32)],
                *[val[SPREAD_T, m] for m in range(rs)],
            )

        def middle_back():
            more = [pltpu.VMEM((1, width), F32)] if g.aligned else []
            d.grad_mid, d.gmix, ggain, d.grad_wo = seq(
                bind(middle_back_kernel, g),
                [
                    stored((seq_len, width), F32),
                    shaped((tokens, rs * hb)),
                    shaped((1, width), F32),
                    shaped((zs, hb, width)),
                ],
                d.swap,
                val[SWAP],
                d.middle,
                d.gl,
                d.gain_m,
                d.mixed,
                d.wo,
                scratch=[pltpu.VMEM((tokens, width), BF16), pltpu.VMEM((seq_len, width), F32)]
                + more,
            )
            d.ggain_m = ggain if g.aligned else permute_cols(ggain, relative())
            parts[GH] = [None] * rs

        def attend_back(m, turn):
            if turn == rs - 1:
                outs = [shaped((seq_len, width), F32), shaped((seq_len, width))]
            else:
                outs = [shaped((tokens, width), F32)]
            outs = seq(
                bind(attn_back_kernel, g, m, turn),
                [shaped((zs, 2 * hb + PAD, 4 * hb))] + outs,
                seq_lengths,
                d.normed_t,
                d.offsets[m],
                d.qkv[m],
                d.gmix,
                d.grad_wo,
                d.hot,
                d.scaled,
                d.attn_w[m],
                *([d.ggain_m] if m == 0 else []),
                *([d.gn] if turn else []),
                scalars=1,
                scratch=[pltpu.VMEM((tokens, 3 * hb), BF16)],
            )
            parts[GH][m] = outs[0]
            if m % 2:
                hop_start(GH, m)
            if turn < rs - 1:
                d.gn = outs[1]
            else:
                own, sib = outs[1:]
                if not g.aligned:
                    back_to = jnp.argsort(relative())
                    own, sib = permute_cols(own, back_to), permute_cols(sib, back_to)
                d.gn = own
                put(NORMED, sib, core_pairs)

        def input_back():
            d.input_grad = seq(
                bind(input_back_kernel, g),
                [stored((seq_len, width))],
                d.gn,
                val[NORMED],
                d.grad_mid,
                x_own,
                d.gain_a,
                scratch=[pltpu.VMEM((seq_len, width), F32)],
            )[0]

        def layer_out():
            parts[LAYER] = seq(
                bind(layer_kernel, g),
                [shaped((seq_len, width))],
                seq_lengths,
                d.middle,
                d.outer_part,
                val[SWAP],
                scalars=1,
            )[0]

        def cot_end():
            deal_last(COT, True)
            put(COT_SIB, parts[COT], core_pairs)

        parts[COT] = cotangent[0]
        put(INPUT, x_own, core_pairs)
        bits = list(range(nb))
        step(start_core)
        step(start_attn)
        step(start_ffn)
        step(stack_attn)
        deal(COT, [nb] + bits, bits + [nb], True, cot_end)
        step(norm)
        for m in range(rs):
            step(attend, m)
        step(mixer)
        step(middle)
        step(ffn, 0)
        step(ffn, 1)
        step(middle_back)
        step(layer_out)
        back_order = [m for m in range(1, rs, 2)] + [m for m in range(rs - 2, -1, -2)]
        for turn, m in enumerate(back_order):
            step(attend_back, m, turn)
        step(input_back)
        for j in range(2, zs):
            step(sum_step, OA, j)
            step(sum_step, OB, j)
        for m in range(rs - 2, -1, -2):
            step(hop_add, GI, GI_SUM, m)
            step(hop_add, GH, GH_SUM, m)
        deal(LAYER, [nb] + bits, bits + [nb], False, bind(deal_last, LAYER, False))
        step(outer_end)
        step(outer_pair)
        for j in range(2, zs):
            step(sum_step, GI_SUM, j)
            step(sum_step, GH_SUM, j)
        step(inner_split)
        step(ffn_pack)
        step(attn_split)
        step(attn_pack)
        step(ffn_end)
        step(attn_end)
        for item in ORDER if (rs, zs) == (4, 4) else range(len(steps)):
            if isinstance(item, int):
                steps[item]()
            else:
                seq.arrived(val[item if len(item) > 1 else item[0]])

        gains, table = d.gains, d.table[:, :n_buckets].T
        sum_tab = lax.dynamic_slice(table, (c * (n_buckets // ss), 0), (n_buckets // ss, heads))
        return (
            parts[LAYER][None],
            d.input_grad[None],
            *d.sum_attn,
            d.sum_in,
            d.sum_out,
            gains[0],
            gains[1],
            sum_tab,
        )

    tokens_spec = P(AXES, None, None)
    rows_spec, part_spec = P("shard", None), P("shard")
    in_specs = (
        (tokens_spec,) * 2 + (P(),) * 3 + (rows_spec,) * 6 + (part_spec,) * 2 + (rows_spec,)
    )
    out_specs = (tokens_spec,) * 2 + (rows_spec,) * 6 + (part_spec,) * 2 + (rows_spec,)
    return jax.shard_map(local, mesh=mesh, in_specs=in_specs, out_specs=out_specs, check_vma=False)
```

```python
import functools

import jax
import jax.numpy as jnp
from jax import lax
from jax.experimental import pallas as pl
from jax.experimental.pallas import tpu as pltpu
from jax.sharding import PartitionSpec as P

EPSILON = 1e-06
MASKED = -1000000000.0
AXES = ("rep", "shard")
BF16 = jnp.bfloat16
F32 = jnp.float32
INV_SQRT2 = 0.7071067811865476
INV_SQRT2PI = 0.3989422804014327
PAD = 16

VMEM = pl.BlockSpec(memory_space=pltpu.VMEM)
SMEM = pl.BlockSpec(memory_space=pltpu.SMEM)
ANY = pl.BlockSpec(memory_space=pl.ANY)
HBM = pl.BlockSpec(memory_space=pltpu.HBM)


def shaped(shape, dtype=BF16):
    return jax.ShapeDtypeStruct(shape, dtype)


def kept(shape, dtype=BF16):
    return pltpu.VMEM(shape, dtype)


def stored(shape, dtype=BF16):
    return pltpu.HBM(shape, dtype)


class Sequence:
    def __init__(self):
        self.last = None

    def __call__(self, body, outs, *args, scalars=0, hbm=0, scratch=(), limit=12, after=()):
        n = len(args)
        args = [pltpu.with_memory_space_constraint(a, pltpu.HBM) if i >= n - hbm else a for i, a in enumerate(args)]
        specs = [SMEM] * scalars + [VMEM] * (n - scalars - hbm) + [HBM] * hbm
        extra = list(after) + ([] if self.last is None else [self.last])
        m = len(extra)

        def run(*refs):
            body(*refs[:n], *refs[n + m :])

        result = pl.pallas_call(
            run,
            out_shape=outs,
            in_specs=specs + [ANY] * m,
            out_specs=[VMEM] * len(outs),
            scratch_shapes=list(scratch),
            cost_estimate=pl.CostEstimate(flops=0, bytes_accessed=0, transcendentals=0),
            compiler_params=pltpu.CompilerParams(vmem_limit_bytes=limit * 1024 * 1024),
        )(*args, *extra)
        self.last = result[-1]
        return result

    def arrived(self, value):
        self(token_kernel, [kept((8, 128), F32)], after=[value], limit=4)


def dot(a, b):
    return jnp.dot(a, b, preferred_element_type=F32)


def dot_nt(a, b):
    return lax.dot_general(a, b, (((1,), (1,)), ((), ())), preferred_element_type=F32)


def dot_tn(a, b):
    return lax.dot_general(a, b, (((0,), (0,)), ((), ())), preferred_element_type=F32)


def lanes(block, size):
    return pl.ds(pl.multiple_of(block * size, size), size)


class Geometry:
    def __init__(self, rs, zs, hb, fb, heads, seq_len, width):
        self.rs, self.zs, self.hb, self.fb = rs, zs, hb, fb
        self.seq_len, self.width = seq_len, width
        self.tokens = 2 * seq_len
        self.bits = rs.bit_length() - 1
        self.sub = fb // rs
        self.cols = zs * self.sub
        self.hd = width // heads
        self.nh = hb // self.hd
        self.chips = rs * zs
        self.rows = seq_len // self.chips
        self.aligned = hb % 128 == 0 and self.sub % 128 == 0
        self.parts = width // self.cols

    def turned(self, m):
        out = 0
        for b in range(self.bits):
            out = out + (((m >> b) & 1) << (self.bits - 1 - b))
        return out

    def here(self):
        return Here(self)


class Here:
    def __init__(self, g):
        self.g = g
        self.r = lax.axis_index("rep").astype(jnp.int32)
        c = lax.axis_index("shard").astype(jnp.int32)
        self.z = lax.div(c, jnp.int32(2))
        self.k = lax.rem(c, jnp.int32(2))
        self.me = self.r * (2 * g.zs) + c

    def code(self, m, k=None):
        k = self.k if k is None else k
        return m + k * (self.g.turned(m) - m)

    def quarter(self, m):
        return self.r if m == 0 else lax.bitwise_xor(self.r, self.code(jnp.int32(m)))

    def behind(self, j):
        return self.z if j == 0 else lax.rem(self.z + (self.g.zs - j), jnp.int32(self.g.zs))

    def shard(self, j, h):
        return 2 * self.behind(j) + (1 - self.k if h else self.k)


class Box:
    pass


class Copies:
    def __init__(self, sem):
        self.sem, self.all = sem, []

    def start(self, src, dst):
        copy = pltpu.make_async_copy(src, dst, self.sem)
        copy.start()
        self.all.append(copy)

    def wait(self):
        for copy in self.all:
            copy.wait()


def fetch_heads(g, at, copies, s, core, weights, dst, row):
    hb = g.hb
    for i, w in enumerate(weights):
        part = dst.at[pl.ds(row, hb), pl.ds(i * hb, hb)]
        copies.start(w.at[:, lanes(2 * s + core, hb)], part)


def fetch_inner(g, at, copies, s, core, wi, dst, row, col):
    hb, sub = g.hb, g.sub
    for b in range(g.zs):
        place = pl.ds(pl.multiple_of((2 * b + core) * g.fb + s * sub, sub), sub)
        copies.start(wi.at[:, place], dst.at[pl.ds(row, hb), pl.ds(col + b * sub, sub)])


def send_prep_kernel(g, wq, wk, wv, wi, out, sem):
    at, hb = g.here(), g.hb
    copies, other = Copies(sem), 1 - at.k
    for m in range(g.rs):
        s = lax.bitwise_xor(at.r, at.code(jnp.int32(m), other))
        fetch_heads(g, at, copies, s, other, (wq, wk, wv), out, m * hb)
        fetch_inner(g, at, copies, s, other, wi, out, m * hb, 3 * hb)
    copies.wait()


def attn_prep_kernel(g, small, other, got, wq, wk, wv, wm, out, sem):
    at, hb = g.here(), g.hb
    copies = Copies(sem)
    fetch_heads(g, at, copies, at.r, at.k, (wq, wk, wv), out, 0)
    for h in range(2):
        part = out.at[pl.ds(h * hb, hb), pl.ds(3 * hb, hb)]
        copies.start(wm.at[:, lanes(2 * at.r + h, hb)], part)
    out[hb : 2 * hb, : 3 * hb] = got[:hb, : 3 * hb]
    row = lax.broadcasted_iota(jnp.int32, (PAD, 4 * hb), 0)
    theirs = pltpu.roll(other[...].astype(F32), 1, 0)
    out[2 * hb :, :] = jnp.where(row == 0, small[...].astype(F32), theirs).astype(BF16)
    copies.wait()


def ffn_prep_kernel(g, got, wi, wu, out, sem):
    at, hb, sub, cols = g.here(), g.hb, g.sub, g.cols
    copies = Copies(sem)
    fetch_inner(g, at, copies, at.r, at.k, wi, out, 0, 0)
    for i in range(g.parts):
        part = out.at[pl.ds(2 * hb + i * sub, sub), :]
        copies.start(wu.at[lanes(at.r, sub), pl.ds(i * cols, cols)], part)
    out[hb : 2 * hb, :] = got[:hb, 3 * hb :]
    copies.wait()


def stack_kernel(rows, *refs):
    *ins, out = refs
    for i, ref in enumerate(ins):
        out[i] = ref[:rows, :]


def token_kernel(out):
    out[...] = jnp.zeros_like(out)


def deal_first_kernel(g, labels, src, *outs):
    at = g.here()
    for out, some in zip(outs, labels):
        for i, (f, zz) in enumerate(some):
            chip = lax.bitwise_xor(at.r, at.code(jnp.int32(f))) * g.zs
            out[i] = src[chip + lax.bitwise_xor(at.z, zz)]


def deal_stage_kernel(places, n_in, *refs):
    ins, outs = refs[:n_in], refs[n_in:]
    for out, some in zip(outs, places):
        for i, (a, b) in enumerate(some):
            out[i] = ins[a][b]


def deal_middle_kernel(g, labels, back, table, own, got, *refs):
    outs, (lookup,) = refs[:-1], refs[-1:]
    at = g.here()
    if back:
        for s in range(2 * g.chips):
            lookup[table[s]] = jnp.int32(s)
    else:
        lookup = table
    for out, some in zip(outs, labels):
        for i, (f, zz) in enumerate(some):
            chip = lax.bitwise_xor(at.r, at.code(jnp.int32(f))) * g.zs
            dest = (chip + lax.bitwise_xor(at.z, zz)) * 2 + at.k
            src = lookup[dest]
            core = lax.rem(src, 2)
            src = lax.div(src, 2)
            sz, sr = lax.rem(src, g.zs), lax.div(src, g.zs)
            sf = at.code(lax.bitwise_xor(at.r, sr), core)
            place = sf * g.zs + lax.bitwise_xor(at.z, sz)
            mine = own[place].astype(F32)
            theirs = got[place].astype(F32)
            out[i] = jnp.where(core == at.k, mine, theirs).astype(BF16)


def deal_last_kernel(g, places, n_in, masked, lengths, *refs):
    ins, (out, pool) = refs[:n_in], refs[n_in:]
    at = g.here()
    for e, (a, b) in enumerate(places):
        pool[e] = ins[a][b]
    for chip in range(g.chips):
        f = at.code(lax.bitwise_xor(at.r, chip // g.zs))
        value = pool[f * g.zs + lax.bitwise_xor(at.z, chip % g.zs)]
        if masked:
            row = lax.broadcasted_iota(jnp.int32, value.shape, 0) + chip * g.rows
            value = jnp.where(row < lengths[at.me], value.astype(F32), 0.0).astype(BF16)
        out[chip] = value


def sum_kernel(picks, *refs):
    *ins, out = refs
    total = None
    for ref, pick in zip(ins, picks):
        v = (ref[...] if pick is None else ref[pick]).astype(F32)
        total = v if total is None else total + v
    out[...] = total.astype(out.dtype)


def cut_sum_kernel(g, *refs):
    n = len(refs) - g.zs
    for j, out in enumerate(refs[n:]):
        out[...] = sum(ref[j].astype(F32) for ref in refs[:n]).astype(BF16)


def outer_end_kernel(g, *refs):
    half, sub = g.rs // 2, g.sub
    outs = refs[-2:]
    for i in range(2):
        own, got = refs[2 * i : 2 * i + 2]
        for c in range(half):
            m = i * half + c
            rows = slice(c * sub, (c + 1) * sub)
            v = own[rows, :].astype(F32) + got[rows, :].astype(F32)
            outs[m % 2][m // 2] = v.astype(BF16)


def outer_pair_kernel(g, keep, got, *outs):
    for i, out in enumerate(outs):
        out[...] = (keep[i].astype(F32) + got[i].astype(F32)).astype(BF16)


def inner_split_kernel(g, *refs):
    *ins, keep, give = refs
    total = sum(ref[...].astype(F32) for ref in ins).astype(BF16)
    keep[...] = total[: g.hb]
    give[...] = total[g.hb :]


def ffn_pack_kernel(g, keep, got, *refs):
    *ins, out = refs
    first = g.here().k == 0
    hb, sub = g.hb, g.sub
    for b in range(g.zs):
        cols = slice(b * sub, (b + 1) * sub)
        mine, theirs = keep[:, cols].astype(F32), got[:, cols].astype(F32)
        out[:hb, 2 * b * sub : (2 * b + 1) * sub] = jnp.where(first, mine, theirs).astype(BF16)
        out[:hb, (2 * b + 1) * sub : (2 * b + 2) * sub] = jnp.where(first, theirs, mine).astype(BF16)
    out[hb:, :] = sum(ref[...].astype(F32) for ref in ins).astype(BF16)


def ffn_end_kernel(g, *refs):
    at, parts, (inner, outer) = g.here(), refs[: g.rs], refs[g.rs :]
    hb, sub = g.hb, g.sub
    for m in range(g.rs):
        s = at.quarter(m)
        outer[lanes(s, sub), :] = parts[m][hb:, :].astype(F32)
        if g.aligned:
            for b in range(2 * g.zs):
                place = pl.ds(pl.multiple_of(b * g.fb + s * sub, sub), sub)
                inner[:, place] = parts[m][:hb, b * sub : (b + 1) * sub].astype(F32)
        else:
            inner[s] = parts[m][:hb, : 2 * g.zs * sub].astype(F32)


def attn_split_kernel(g, *refs):
    *ins, keep, mixer, give = refs
    hb = g.hb
    total = sum(ref[...].astype(F32) for ref in ins).astype(BF16)
    keep[:hb, :] = total[:hb, : 3 * hb]
    keep[hb:, :] = total[2 * hb :, : 3 * hb]
    mixer[:, :hb] = total[:hb, 3 * hb :]
    mixer[:, hb:] = total[hb : 2 * hb, 3 * hb :]
    give[:hb, :] = total[hb : 2 * hb, : 3 * hb]
    give[hb:, :] = total[2 * hb :, : 3 * hb]


def attn_pack_kernel(g, keep, mixer, got, out):
    first = g.here().k == 0
    hb = g.hb
    for b in range(3):
        cols = slice(b * hb, (b + 1) * hb)
        mine, theirs = keep[:, cols].astype(F32), got[:, cols].astype(F32)
        out[:, 2 * b * hb : (2 * b + 1) * hb] = jnp.where(first, mine, theirs).astype(BF16)
        out[:, (2 * b + 1) * hb : (2 * b + 2) * hb] = jnp.where(first, theirs, mine).astype(BF16)
    out[:hb, 6 * hb :] = mixer[...]
    out[hb:, 6 * hb :] = jnp.zeros((PAD, 2 * hb), BF16)


def attn_end_kernel(g, *refs):
    at, parts, outs = g.here(), refs[: g.rs], refs[g.rs :]
    hb, size = g.hb, 2 * g.hb
    gains, table = outs[4:]
    total = None
    for m in range(g.rs):
        q = at.quarter(m)
        for i in range(4):
            outs[i][:, lanes(q, size)] = parts[m][:hb, size * i : size * (i + 1)].astype(F32)
        tiles = parts[m][hb:, :].astype(F32)
        pair = []
        for core in range(2):
            both = [tiles[:, (2 * b + core) * hb : (2 * b + core + 1) * hb] for b in range(3)]
            for i in range(g.nh):
                head = (2 * q + core) * g.nh + i
                table[pl.ds(head, 1), :] = both[2][2 + i : 3 + i, :]
            pair.append(both)
        own = [jnp.where(at.k == 0, pair[0][b][0:1], pair[1][b][0:1]) for b in range(2)]
        their = [jnp.where(at.k == 0, pair[1][b][1:2], pair[0][b][1:2]) for b in range(2)]
        some = [own[b] + their[b] for b in range(2)]
        total = some if total is None else [total[b] + some[b] for b in range(2)]
    for b in range(2):
        gains[b : b + 1, :] = total[b]


def to_relative(g, at, src, dst):
    hb = g.hb
    for j in range(g.zs):
        for h in range(2):
            e = 2 * j + h
            dst[:, e * hb : (e + 1) * hb] = src[:, lanes(at.shard(j, h), hb)]


def norm_kernel(g, own, sib, gain, normed, normed_t, scaled, *scratch):
    half = own.shape[0]
    plain, plain_scaled = scratch if g.aligned else (normed, scaled)
    for start, src in ((0, own), (half, sib)):
        v = src[...].astype(F32)
        scale = lax.rsqrt(jnp.mean(v * v, axis=-1, keepdims=True) + EPSILON)
        plain[start : start + half, :] = (v * scale * gain[...]).astype(BF16)
        plain_scaled[start : start + half, :] = (v * scale).astype(BF16)
    if g.aligned:
        to_relative(g, g.here(), plain, normed)
        to_relative(g, g.here(), plain_scaled, scaled)
    normed_t[...] = normed[...].T


def toeplitz(row, n):
    wide = jnp.broadcast_to(row, (n, 2 * n))
    return pltpu.roll(wide, n + 1, 1, stride=1, stride_axis=0)[:, :n]


def probabilities(q, kk, bias, length):
    n = q.shape[0]
    s = dot_nt(q, kk) + bias
    col = lax.broadcasted_iota(jnp.int32, (n, n), 1)
    s = jnp.where(col < length, s, MASKED)
    e = jnp.exp(s - jnp.max(s, axis=-1, keepdims=True))
    return e * (1.0 / jnp.sum(e, axis=-1, keepdims=True))


def two_lengths(at, lengths):
    return lengths[at.me], lengths[lax.bitwise_xor(at.me, 1)]


def attn_kernel(g, m, lengths, normed, off, first, rest, *refs):
    hb, hd = g.hb, g.hd
    at = g.here()
    both = two_lengths(at, lengths)
    if m == 0 or not g.aligned:
        qkv, mixed, w = refs
        w[: 2 * hb, :] = first[: 2 * hb, : 3 * hb]
        copies = None
    else:
        weights, (qkv, mixed, w, sem) = refs[:3], refs[3:]
        copies = Copies(sem)
        fetch_heads(g, at, copies, at.quarter(m), at.k, weights, w, 0)
        w[hb : 2 * hb, :] = first[m * hb : (m + 1) * hb, : 3 * hb]
    for j in range(1, g.zs):
        w[2 * hb * j : 2 * hb * (j + 1), :] = rest[j - 1, :, : 3 * hb]
    if copies is not None:
        copies.wait()
    qkv[...] = dot(normed[...], w[...]).astype(BF16)
    half = normed.shape[0] // 2
    for h in range(g.nh):
        bias = toeplitz(off[h : h + 1, :], half)
        for s in range(2):
            rows = slice(s * half, (s + 1) * half)
            q, kk, v = (qkv[rows, i * hb + h * hd : i * hb + (h + 1) * hd] for i in range(3))
            p = probabilities(q, kk, bias, both[s]).astype(BF16)
            mixed[rows, h * hd : (h + 1) * hd] = dot(p, v).astype(BF16)


def turned_head(g, at, block):
    return at.code(lax.bitwise_xor(block, at.r))


def mixer_kernel(g, *refs):
    rs, zs, hb = g.rs, g.zs, g.hb
    at = g.here()
    mixed_parts, own, rest = refs[:rs], refs[rs], refs[rs + 1 : 2 * rs + 1]
    mixed, wo, partial = refs[2 * rs + 1 :]
    for m in range(rs):
        mixed[:, m * hb : (m + 1) * hb] = mixed_parts[m][...]
    wo[lanes(turned_head(g, at, at.z), hb), :] = own[...]
    for m in range(rs):
        for j in range(1, zs):
            rows = lanes(turned_head(g, at, at.behind(j)), hb)
            piece = rest[m][j - 1, :, 3 * hb :]
            both = jnp.concatenate([piece[:hb], piece[hb:]], axis=1)
            wo[rows, lanes(at.quarter(m), 2 * hb)] = both
    partial[...] = dot(mixed[...], wo[...]).astype(BF16)


def middle_kernel(g, own, sib, part, other, gain, *refs):
    middle, normed2, normed2_t = refs[:3]
    plain = refs[3] if g.aligned else normed2
    half = own.shape[0]
    for s, src in ((0, own), (1, sib)):
        rows = slice(s * half, (s + 1) * half)
        swapped = slice((1 - s) * half, (2 - s) * half)
        v = src[...].astype(F32) + part[rows, :].astype(F32) + other[swapped, :].astype(F32)
        middle[rows, :] = v
        scale = lax.rsqrt(jnp.mean(v * v, axis=-1, keepdims=True) + EPSILON)
        plain[rows, :] = (v * scale * gain[...]).astype(BF16)
    if g.aligned:
        to_relative(g, g.here(), plain, normed2)
    normed2_t[...] = normed2[...].T


def ffn_kernel(g, chunks, last, normed2, normed2_t, *refs):
    hb, sub, zs, cols = g.hb, g.sub, g.zs, g.cols
    at = g.here()
    half = g.seq_len
    n = chunks
    rest, refs = refs[: n * (zs - 1)], refs[n * (zs - 1) :]
    firsts, refs = refs[: n if not g.aligned else 2 - last], refs[n if not g.aligned else 2 - last :]
    if last:
        gl, outer_in, gn2_in, refs = *refs[:3], refs[3:]
    else:
        gl_own, gl_sib, refs = *refs[:2], refs[2:]
    if g.aligned:
        wi, wu, refs = *refs[:2], refs[2:]
    if last:
        outer_own, swap, refs = *refs[:2], refs[2:]
    else:
        gl, outer, gn2, refs = *refs[:3], refs[3:]
        gl[:half, :] = gl_own[...]
        gl[half:, :] = gl_sib[...]
    grads, outs, refs = refs[:n], refs[n : n + zs], refs[n + zs :]
    w1s, w2s, go = refs[:n], refs[n : 2 * n], refs[2 * n]
    copies = Copies(refs[2 * n + 1]) if g.aligned else None
    for i in range(n):
        m = i + (n if last else 0)
        w1, w2 = w1s[i], w2s[i]
        mine = pl.ds(pl.multiple_of(at.z * sub, sub), sub)
        if m and g.aligned:
            s = at.quarter(m)
            fetch_inner(g, at, copies, s, at.k, wi, w1, 0, 0)
            copies.start(wu.at[lanes(s, sub), :], w2.at[mine, :])
            w1[hb : 2 * hb, :] = firsts[-1][m * hb : (m + 1) * hb, 3 * hb :]
        else:
            piece = firsts[i]
            w1[: 2 * hb, :] = piece[: 2 * hb, :]
            for b in range(g.parts):
                rows = slice(2 * hb + b * sub, 2 * hb + (b + 1) * sub)
                w2[mine, b * cols : (b + 1) * cols] = piece[rows, :]
        for j in range(1, zs):
            piece = rest[i * (zs - 1) + j - 1]
            w1[2 * hb * j : 2 * hb * (j + 1), :] = piece[: 2 * hb, :]
            place = lanes(at.behind(j), sub)
            for b in range(g.parts):
                rows = slice(2 * hb + b * sub, 2 * hb + (b + 1) * sub)
                w2[place, b * cols : (b + 1) * cols] = piece[rows, :]
    if copies is not None:
        copies.wait()
    out_sum, gn_sum = None, None
    for i in range(n):
        w1, w2 = w1s[i], w2s[i]
        h = dot(normed2[...], w1[...])
        cdf = 0.5 * (1.0 + lax.erf(h * INV_SQRT2))
        pdf = jnp.exp(-0.5 * h * h) * INV_SQRT2PI
        act = (h * cdf).astype(BF16)
        ga = dot_nt(gl[...], w2[...])
        gh = (ga * (cdf + h * pdf)).astype(BF16)
        grads[i][...] = dot(normed2_t[...], gh).astype(BF16).reshape(zs, 2 * hb, cols)
        full = dot_tn(act, gl[...]).astype(BF16)
        for b in range(zs):
            place = lax.rem(at.z + (zs - b), zs)
            go[place, i * sub : (i + 1) * sub, :] = full[b * sub : (b + 1) * sub, :]
        out_part = dot(act, w2[...])
        gn_part = dot_nt(gh, w1[...])
        out_sum = out_part if out_sum is None else out_sum + out_part
        gn_sum = gn_part if gn_sum is None else gn_sum + gn_part
    for j in range(zs):
        outs[j][...] = go[j]
    if last:
        out_sum = out_sum + outer_in[...]
        outer_own[...] = out_sum[:half]
        swap[g.tokens :, :] = out_sum[half:].astype(BF16)
        swap[: g.tokens, :] = (gn_sum + gn2_in[...]).astype(BF16)
    else:
        outer[...] = out_sum
        gn2[...] = gn_sum


def absolute_sum(g, at, part, other, rows, swapped, total):
    hb = g.hb
    if not g.aligned:
        total[...] = part[rows, :].astype(F32) + other[swapped, :].astype(F32)
        return
    for j in range(g.zs):
        for h in range(2):
            mine, theirs = 2 * j + h, 2 * j + 1 - h
            a = part[rows, mine * hb : (mine + 1) * hb].astype(F32)
            b = other[swapped, theirs * hb : (theirs + 1) * hb].astype(F32)
            total[:, lanes(at.shard(j, h), hb)] = a + b


def middle_back_kernel(g, part, other, middle, gl, gain, mixed, wo, *refs):
    grad_mid, gm, ggain, gwo, gatt, total = refs[:6]
    at, hb = g.here(), g.hb
    half, width = g.seq_len, g.width
    for s in range(2):
        rows = slice(s * half, (s + 1) * half)
        swapped = slice((1 - s) * half, (2 - s) * half)
        absolute_sum(g, at, part, other, rows, swapped, total)
        gn = total[...]
        v = middle[rows, :]
        scale = lax.rsqrt(jnp.mean(v * v, axis=-1, keepdims=True) + EPSILON)
        gg = gn * gain[...]
        inner = jnp.sum(gg * v, axis=-1, keepdims=True) * (1.0 / width)
        grad = gl[rows, :].astype(F32) + scale * gg - v * (scale * scale * scale * inner)
        if s == 0:
            grad_mid[...] = grad
            sums = jnp.sum(gn * v * scale, axis=0, keepdims=True)
            if g.aligned:
                refs[6][...] = sums
                to_relative(g, at, refs[6], ggain)
            else:
                ggain[...] = sums
        gatt[rows, :] = grad.astype(BF16)
    gm[...] = dot_nt(gatt[...], wo[...]).astype(BF16)
    full = dot_tn(mixed[...], gatt[...]).astype(BF16)
    for m in range(g.rs):
        place = lax.rem(at.z + (g.zs - at.quarter(m)), g.zs)
        gwo[place] = full[m * hb : (m + 1) * hb, :]


def attn_back_kernel(g, m, step, lengths, normed_t, off, qkv, gmix, gwo, hot, scaled, w, *refs):
    hb, hd = g.hb, g.hd
    at = g.here()
    both = two_lengths(at, lengths)
    half = g.seq_len
    extra, refs = (refs[:1], refs[1:]) if m == 0 else ((), refs)
    before, refs = (refs[0], refs[1:]) if step else (None, refs)
    gw, *gn, gqkv = refs
    flip = (
        lax.broadcasted_iota(jnp.int32, (half, half), 0)
        + lax.broadcasted_iota(jnp.int32, (half, half), 1)
        == half - 1
    ).astype(BF16)
    table = []
    for h in range(g.nh):
        bias = toeplitz(off[h : h + 1, :], half)
        flipped = jnp.zeros((half, half), F32)
        for s in range(2):
            rows = slice(s * half, (s + 1) * half)
            q, kk, v = (qkv[rows, i * hb + h * hd : i * hb + (h + 1) * hd] for i in range(3))
            gm = gmix[rows, m * hb + h * hd : m * hb + (h + 1) * hd]
            p = probabilities(q, kk, bias, both[s])
            gp = dot_nt(gm, v)
            delta = jnp.sum(p * gp, axis=-1, keepdims=True)
            gs = (p * (gp - delta)).astype(BF16)
            flipped = flipped + dot(flip, gs)
            cols = [slice(i * hb + h * hd, i * hb + (h + 1) * hd) for i in range(3)]
            gqkv[rows, cols[0]] = dot(gs, kk).astype(BF16)
            gqkv[rows, cols[1]] = dot_tn(gs, q).astype(BF16)
            gqkv[rows, cols[2]] = dot_tn(p.astype(BF16), gm).astype(BF16)
        wide = jnp.concatenate([flipped, jnp.zeros((half, half), F32)], axis=1)
        skewed = pltpu.roll(wide, 0, 1, stride=1, stride_axis=0)
        diag = jnp.broadcast_to(jnp.sum(skewed, axis=0, keepdims=True), (8, 2 * half))
        top = diag.astype(BF16)
        table.append(dot_nt(top, hot[...]) + dot_nt((diag - top.astype(F32)).astype(BF16), hot[...]))
    gw[:, : 2 * hb, : 3 * hb] = (
        dot(normed_t[...], gqkv[...]).astype(BF16).reshape(g.zs, 2 * hb, 3 * hb)
    )
    row = lax.broadcasted_iota(jnp.int32, (PAD, hb), 0)
    buckets = jnp.zeros((PAD, hb), F32)
    for i, t in enumerate(table):
        buckets = jnp.where(row == 2 + i, jnp.broadcast_to(t[0:1], (PAD, hb)), buckets)
    for j in range(g.zs):
        piece = gwo[j, :, lanes(at.quarter(m), 2 * hb)]
        gw[j, :hb, 3 * hb :] = piece[:, :hb]
        gw[j, hb : 2 * hb, 3 * hb :] = piece[:, hb:]
        part = dot_nt(gqkv[...], w[2 * hb * j : 2 * hb * (j + 1), :])
        cols = slice(2 * hb * j, 2 * hb * (j + 1))
        gain = jnp.sum(part * scaled[:, cols].astype(F32), axis=0, keepdims=True)
        tile = [gain[:, :hb], gain[:, hb:]]
        tile = jnp.where(row == 0, tile[0], jnp.where(row == 1, tile[1], 0.0))
        gw[j, 2 * hb :, :hb] = tile.astype(BF16)
        if m == 0:
            tile = [extra[0][:, (2 * j + h) * hb : (2 * j + h + 1) * hb] for h in range(2)]
            tile = jnp.where(row == 0, tile[0], jnp.where(row == 1, tile[1], 0.0))
        else:
            tile = jnp.zeros((PAD, hb), F32)
        gw[j, 2 * hb :, hb : 2 * hb] = tile.astype(BF16)
        gw[j, 2 * hb :, 2 * hb : 3 * hb] = buckets.astype(BF16)
        gw[j, 2 * hb :, 3 * hb :] = jnp.zeros((PAD, hb), BF16)
        if before is not None:
            part = part + before[:, cols]
        if len(gn) == 1:
            gn[0][:, cols] = part
        else:
            gn[0][:, cols] = part[:half]
            gn[1][:, cols] = part[half:].astype(BF16)


def input_back_kernel(g, own, other, grad_mid, x, gain, out, total):
    everything = slice(None)
    absolute_sum(g, g.here(), own, other, everything, everything, total)
    gn = total[...]
    v = x[...].astype(F32)
    scale = lax.rsqrt(jnp.mean(v * v, axis=-1, keepdims=True) + EPSILON)
    gg = gn * gain[...]
    inner = jnp.mean(gg * v, axis=-1, keepdims=True)
    grad = grad_mid[...] + scale * gg - v * (scale * scale * scale * inner)
    out[...] = grad.astype(BF16)


def layer_kernel(g, lengths, middle, own, other, out):
    half = own.shape[0]
    row = lax.broadcasted_iota(jnp.int32, own.shape, 0)
    v = middle[:half, :] + own[...] + other[g.tokens :, :].astype(F32)
    out[...] = jnp.where(row < lengths[g.here().me], v, 0.0).astype(BF16)


CORE, SMALL, INPUT, MIDDLE, SWAP, NORMED, INNER, ATTN, COT, COT_SIB, LAYER = range(11)
RING_A, RING_F, HOP_A, HOP_F, GI, GI_SUM, GH, GH_SUM, OA, OB, LATE, SPREAD_F, SPREAD_T = range(11, 24)

ORDER = (
    0, 1, 4, 5, 2, 6, 3, 12, 7, 8, 13, 15, 9, 14, 10, ((COT, 0), 1), ((HOP_F, 2), 2), 16, 17, 11,
    ((HOP_F, 1), 3), ((HOP_F, 2), 3), 18, ((HOP_F, 3), 3), (INPUT,), 19, 20, 22, 21, 23, 29, 36, 24,
    28, 37, 32, 25, (GI, 1), 31, 33, 38, 30, 39, 34, (OB, 3), 40, 46, 26, 44, 35, 27, 48, 41, 47,
    50, 45, 42, (GH_SUM, 2), (OB, 1), 51, 49, 52, ((LAYER, 5), 0), (SPREAD_F, 2), 53, 54, 43,
    (SPREAD_T, 2), (RING_F, 1), (SPREAD_T, 1), (RING_A, 3), ((HOP_F, 3), 1), ((COT, 5), 2),
    (LATE, 2), 55,
)


def solution(mesh):
    rs, ss = mesh.shape["rep"], mesh.shape["shard"]
    zs = ss // 2
    count = rs * ss
    nb = rs.bit_length() - 1

    def pairs(move):
        table = []
        for i in range(count):
            r, z, k = i // ss, (i % ss) // 2, i % 2
            r, z, k = move(r, z, k)
            table.append((i, (r * zs + z) * 2 + k))
        return table

    core_pairs = pairs(lambda r, z, k: (r, z, 1 - k))
    up_pairs = pairs(lambda r, z, k: (r, (z + 1) % zs, k))
    rep_pairs = [
        pairs(lambda r, z, k, b=b: (r ^ (1 << (nb - 1 - b if k else b)), z, k)) for b in range(nb)
    ]
    z_pairs = {m: pairs(lambda r, z, k, m=m: (r, z ^ m, k)) for m in range(1, zs)}

    def send(value, table):
        return lax.ppermute(value, AXES, table)

    by_size = sorted(range(1, rs), key=lambda m: (bin(m).count("1"), m))

    def high(m):
        return m.bit_length() - 1

    def low(m):
        return (m & -m).bit_length() - 1

    def local(
        inputs,
        cotangent,
        seq_lengths,
        dealing,
        rel_buckets,
        w_query,
        w_key,
        w_value,
        w_mixer,
        w_inner,
        w_outer,
        gain_attn,
        gain_mlp,
        bias_table,
    ):
        seq = Sequence()
        bind = functools.partial
        n_buckets, heads = bias_table.shape[0] * ss, bias_table.shape[1]
        g = Geometry(rs, zs, w_query.shape[0], w_outer.shape[0], heads, *inputs.shape[1:])
        hb, fb, sub, cols, nh = g.hb, g.fb, g.sub, g.cols, g.nh
        seq_len, width, tokens = g.seq_len, g.width, g.tokens
        chips, rows = g.chips, g.rows
        chunks = rs // 2

        r, c = lax.axis_index("rep"), lax.axis_index("shard")
        z, k = c // 2, c % 2
        shards = jnp.arange(ss, dtype=jnp.int32)
        x_own = inputs[0]
        d = Box()
        parts = {}

        def relative():
            return 2 * ((z + zs - shards // 2) % zs) + (k ^ (shards % 2))

        def permute_cols(x, order):
            return jnp.take(x.reshape(-1, ss, hb), order, axis=1).reshape(x.shape)

        val = {}
        steps = []

        def put(name, value, table):
            val[name] = send(value, table)

        def step(run, *args):
            steps.append(bind(run, *args))

        labels = [(f, zz) for f in range(rs) for zz in range(zs)]

        def groups_of(stage):
            if stage == nb:
                return [[e for e in labels if e[1] == zz] for zz in range(zs)]
            clear = [e for e in labels if not (e[0] >> stage) & 1]
            return [clear, [e for e in labels if e not in clear]]

        def block_shapes(groups):
            outs = [shaped((len(some), rows, width)) for some in groups]
            return outs if len(outs) == 1 else [stored(outs[0].shape)] + outs[1:]

        def dispatch(key, outs, stage):
            groups = groups_of(stage)
            val[key] = outs[0]
            state = [(key, groups[0])]
            for i, (out, some) in enumerate(zip(outs[1:], groups[1:])):
                put((key, i), out, z_pairs[i + 1] if stage == nb else rep_pairs[stage])
                state.append(((key, i), some))
            return state

        def places(state, some):
            at = {e: (a, b) for a, (_, named) in enumerate(state) for b, e in enumerate(named)}
            return [at[e] for e in some]

        def values(state):
            return [val[name] for name, _ in state]

        def deal_first(what, stage):
            groups = groups_of(stage)
            value = parts[what].reshape(chips, rows, width)
            outs = seq(bind(deal_first_kernel, g, groups), block_shapes(groups), value)
            parts[what] = dispatch((what, 0), outs, stage)

        def deal_stage(what, number, stage):
            groups, state = groups_of(stage), parts[what]
            body = bind(deal_stage_kernel, [places(state, some) for some in groups], len(state))
            outs = seq(body, block_shapes(groups), *values(state))
            parts[what] = dispatch((what, number), outs, stage)

        def deal_core(what):
            state = parts[what]
            body = bind(deal_stage_kernel, [places(state, labels)], len(state))
            parts[what] = seq(body, block_shapes([labels]), *values(state))[0]
            put((what, CORE), parts[what], core_pairs)

        def deal_middle(what, number, stage, back):
            groups = groups_of(stage)
            body = bind(deal_middle_kernel, g, groups, back)
            lookup = [pltpu.SMEM((count,), jnp.int32)]
            args = dealing, parts[what], val[what, CORE]
            outs = seq(body, block_shapes(groups), *args, scalars=1, scratch=lookup)
            parts[what] = dispatch((what, number), outs, stage)

        def deal_last(what, masked):
            state = parts[what]
            body = bind(deal_last_kernel, g, places(state, labels), len(state), masked)
            pool = [pltpu.VMEM((chips, rows, width), BF16)]
            shape = [shaped((chips, rows, width))]
            out = seq(body, shape, seq_lengths, *values(state), scalars=1, scratch=pool)[0]
            parts[what] = out.reshape(seq_len, width)

        def deal(what, first, second, back, end):
            step(deal_first, what, first[0])
            for i, stage in list(enumerate(first))[1:]:
                step(deal_stage, what, i, stage)
            step(deal_core, what)
            n = len(first)
            step(deal_middle, what, n, second[0], back)
            for i, stage in list(enumerate(second))[1:]:
                step(deal_stage, what, n + i, stage)
            step(end)

        copy_sem = pltpu.SemaphoreType.DMA(())

        def slices(m, core):
            s = r ^ (m + core * (g.turned(m) - m))
            at = (2 * s + core) * hb
            parts = [lax.dynamic_slice(w, (0, at), (hb, hb)) for w in (w_query, w_key, w_value)]
            at = [(2 * b + core) * fb + s * sub for b in range(zs)]
            inner = [lax.dynamic_slice(w_inner, (0, a), (hb, sub)) for a in at]
            mix = lax.dynamic_slice(w_mixer, (0, s * 2 * hb), (hb, 2 * hb))
            outer = lax.dynamic_slice(w_outer, (s * sub, 0), (sub, width))
            outer = [outer[:, i * cols : (i + 1) * cols] for i in range(g.parts)]
            return parts, inner, mix, outer

        def start_core():
            if g.aligned:
                sent = seq(
                    bind(send_prep_kernel, g),
                    [shaped((rs * hb, 3 * hb + cols))],
                    w_query,
                    w_key,
                    w_value,
                    w_inner,
                    hbm=4,
                    scratch=[copy_sem],
                )[0]
            else:
                sent = []
                for m in range(rs):
                    parts, inner, _, _ = slices(m, 1 - k)
                    sent.append(jnp.concatenate(parts + inner, axis=1))
                sent = jnp.concatenate(sent, axis=0)
            put(CORE, sent, core_pairs)
            small = jnp.concatenate([gain_attn, gain_mlp, bias_table.reshape(-1)])
            d.n_small = small.shape[0]
            d.small = jnp.pad(small[None], ((0, PAD - 1), (0, 4 * hb - small.shape[0])))
            put(SMALL, d.small, core_pairs)

        def start_attn():
            got = val[CORE]
            if g.aligned:
                own = seq(
                    bind(attn_prep_kernel, g),
                    [shaped((2 * hb + PAD, 4 * hb))],
                    d.small,
                    val[SMALL],
                    got,
                    w_query,
                    w_key,
                    w_value,
                    w_mixer,
                    hbm=4,
                    scratch=[copy_sem],
                )
            else:
                own = []
                for m in range(rs):
                    parts, _, mix, _ = slices(m, k)
                    top = jnp.concatenate(parts + [mix[:, :hb]], axis=1)
                    bottom = [got[m * hb : (m + 1) * hb, : 3 * hb], mix[:, hb:]]
                    own.append(jnp.concatenate([top, jnp.concatenate(bottom, axis=1)], axis=0))
                mine, theirs = d.small, val[SMALL]
                both = jnp.concatenate([mine[:1], theirs[:1], mine[2:]], axis=0)
                own[0] = jnp.concatenate([own[0], both], axis=0)
            d.attn_own = own
            ring(RING_A, own[0])

        def start_ffn():
            got = val[CORE]
            if g.aligned:
                own = seq(
                    bind(ffn_prep_kernel, g),
                    [shaped((4 * hb, cols))],
                    got,
                    w_inner,
                    w_outer,
                    hbm=2,
                    scratch=[copy_sem],
                )
            else:
                own = []
                for m in range(rs):
                    _, inner, _, outer = slices(m, k)
                    bottom = got[m * hb : (m + 1) * hb, 3 * hb :]
                    own.append(
                        jnp.concatenate([jnp.concatenate(inner, axis=1), bottom] + outer, axis=0)
                    )
            d.ffn_own = own
            ring(RING_F, own[0])
            for j in range(1, zs):
                hops((HOP_F, j), val[RING_F, j])

        def ring(name, value):
            for j in range(1, zs):
                put((name, j), value if j == 1 else val[name, j - 1], up_pairs)

        def hops(name, value):
            val[name, 0] = value
            for m in by_size:
                put((name, m), val[name, m ^ (1 << high(m))], rep_pairs[high(m)])

        def stack_attn():
            pieces = [val[RING_A, j] for j in range(1, zs)]
            shape = [shaped((zs - 1, 2 * hb, 4 * hb))]
            hops(HOP_A, seq(bind(stack_kernel, 2 * hb), shape, *pieces)[0])

        def rest_of(j, m):
            return val[(HOP_F, j), m]

        def small_params():
            n_small = d.n_small
            pieces = [d.attn_own[0]] + [val[RING_A, j] for j in range(1, zs)]
            some = [piece[2 * hb : 2 * hb + 2, :n_small] for piece in pieces]
            order = (shards[:, None] == relative()[None, :]).astype(BF16)
            some = dot(order, jnp.concatenate(some, axis=0))
            d.gain_a = some[:, :hb].reshape(1, width)
            d.gain_m = some[:, hb : 2 * hb].reshape(1, width)
            table = some[:, 2 * hb :].reshape(n_buckets, heads)
            quarters = jnp.arange(rs, dtype=jnp.int32)
            quarters = r ^ (quarters + k * (g.turned(quarters) - quarters))
            head_ids = ((2 * quarters + k) * nh)[:, None] + jnp.arange(nh, dtype=jnp.int32)[None]
            pick = jnp.arange(heads, dtype=jnp.int32)[:, None] == head_ids.reshape(1, -1)
            padded = jnp.concatenate([rel_buckets, jnp.full((1,), -1, jnp.int32)])
            hot = padded[None, :] == jnp.arange(hb, dtype=jnp.int32)[:, None]
            d.hot = hot.astype(BF16)
            my_table = dot(table.astype(BF16), pick.astype(BF16)).astype(BF16)
            d.offsets = lax.dot_general(
                my_table,
                d.hot[:n_buckets],
                (((0,), (0,)), ((), ())),
                preferred_element_type=F32,
            ).reshape(rs, nh, 2 * seq_len)

        spare = [pltpu.VMEM((tokens, width), BF16)] if g.aligned else []

        def norm():
            small_params()
            normed, normed_t, scaled = seq(
                bind(norm_kernel, g),
                [shaped((tokens, width)), stored((width, tokens)), stored((tokens, width))],
                x_own,
                val[INPUT],
                d.gain_a,
                scratch=spare * 2,
            )
            if not g.aligned:
                normed = permute_cols(normed, relative())
                scaled = permute_cols(scaled, relative())
                normed_t = normed.T
            d.normed, d.normed_t, d.scaled = normed, normed_t, scaled
            d.qkv, d.mixed_parts, d.attn_w = ([None] * rs for _ in range(3))

        def attend(m):
            own = m == 0 or not g.aligned
            weights = () if own else (w_query, w_key, w_value)
            d.qkv[m], d.mixed_parts[m], d.attn_w[m] = seq(
                bind(attn_kernel, g, m),
                [stored((tokens, 3 * hb)), stored((tokens, hb)), stored((width, 3 * hb))],
                seq_lengths,
                d.normed,
                d.offsets[m],
                d.attn_own[m] if own else val[CORE],
                val[HOP_A, m],
                *weights,
                scalars=1,
                hbm=len(weights),
                scratch=() if own else [copy_sem],
            )

        def mixer():
            d.mixed, d.wo, d.partial = seq(
                bind(mixer_kernel, g),
                [stored((tokens, rs * hb)), stored((rs * hb, width)), shaped((tokens, width))],
                *d.mixed_parts,
                w_mixer,
                *[val[HOP_A, m] for m in range(rs)],
            )
            put(MIDDLE, d.partial, core_pairs)

        def middle():
            d.middle, normed2, normed2_t = seq(
                bind(middle_kernel, g),
                [stored((tokens, width), F32), shaped((tokens, width)), shaped((width, tokens))],
                x_own,
                val[INPUT],
                d.partial,
                val[MIDDLE],
                d.gain_m,
                scratch=spare,
            )
            if not g.aligned:
                normed2 = permute_cols(normed2, relative())
                normed2_t = normed2.T
            d.normed2, d.normed2_t = normed2, normed2_t

        def ffn(part):
            some = range(part * chunks, (part + 1) * chunks)
            if not g.aligned:
                firsts = [d.ffn_own[m] for m in some]
            else:
                firsts = ([] if part else [d.ffn_own[0]]) + [val[CORE]]
            if part == 0:
                more = parts[COT], val[COT_SIB]
                head = [shaped((tokens, width))] + [shaped((tokens, width), F32)] * 2
            else:
                more = (d.gl, *d.acc)
                head = [shaped((seq_len, width), F32), shaped((tokens + seq_len, width))]
            weights = (w_inner, w_outer) if g.aligned else ()
            scratch = [pltpu.VMEM((width, cols), BF16)] * chunks
            scratch += [pltpu.VMEM((cols, width), BF16)] * chunks
            scratch += [pltpu.VMEM((zs, chunks * sub, width), BF16)]
            outs = seq(
                bind(ffn_kernel, g, chunks, part == 1),
                head
                + [shaped((zs, 2 * hb, cols))] * chunks
                + [shaped((chunks * sub, width))] * zs,
                d.normed2,
                d.normed2_t,
                *[rest_of(j, m) for m in some for j in range(1, zs)],
                *firsts,
                *more,
                *weights,
                hbm=len(weights),
                scratch=scratch + ([copy_sem] if g.aligned else []),
                limit=28,
            )
            parts[GI] = (parts[GI] if part else []) + list(outs[len(head) : -zs])
            parts[(OA, OB)[part]] = outs[-zs:]
            if part == 0:
                d.gl, d.acc = outs[0], outs[1:3]
            else:
                d.outer_part, swap = outs[:2]
                if not g.aligned:
                    first = permute_cols(swap[:tokens], jnp.argsort(relative()))
                    swap = jnp.concatenate([first, swap[tokens:]], axis=0)
                d.swap = swap
                put(SWAP, swap, core_pairs)
            for m in some:
                if m % 2:
                    hop_start(GI, m)
            name = (OA, OB)[part]
            put((name, 1), parts[name][1], up_pairs)

        def add(*terms):
            shape = [shaped(terms[0].shape)]
            return seq(bind(sum_kernel, [None] * len(terms)), shape, *terms)[0]

        def sum_step(name, j):
            put((name, j), add(val[name, j - 1], parts[name][j]), up_pairs)

        def hop_start(name, m):
            put((name, m), parts[name][m], rep_pairs[low(m)])

        def hop_add(name, ring, m):
            some = parts[name]
            bits = [b for b in range(nb) if not (m >> b) & 1 and low(m | 1 << b) == b]
            terms = [some[m]] + [val[name, m | 1 << b] for b in bits]
            if m:
                some[m] = add(*terms)
                hop_start(name, m)
            else:
                shape = [shaped(some[0].shape[1:])] * zs
                parts[ring] = seq(bind(cut_sum_kernel, g), shape, *terms)
                put((ring, 1), parts[ring][1], up_pairs)

        def outer_end():
            half, last = rs // 2, zs - 1
            d.late, give = seq(
                bind(outer_end_kernel, g),
                [shaped((half, sub, width))] * 2,
                parts[OA][0],
                val[OA, last],
                parts[OB][0],
                val[OB, last],
            )
            put((LATE, 1), give, rep_pairs[0])

        def outer_pair():
            half = rs // 2
            shape = [shaped((sub, width))] * half
            parts = list(seq(bind(outer_pair_kernel, g), shape, d.late, val[LATE, 1]))
            d.late, names = parts, []
            for i in range(half - 1, 0, -1):
                b = low(i)
                put((LATE, i + 1), parts[i], rep_pairs[b + 1])
                if i ^ (1 << b):
                    parts[i ^ (1 << b)] = add(parts[i ^ (1 << b)], val[LATE, i + 1])
                else:
                    names.append((LATE, i + 1))
            d.late_names = names

        def inner_split():
            keep, give = seq(
                bind(inner_split_kernel, g),
                [shaped((hb, cols))] * 2,
                parts[GI_SUM][0],
                val[GI_SUM, zs - 1],
            )
            d.inner_keep = keep
            put(INNER, give, core_pairs)

        def ffn_pack():
            late = [d.late[0]] + [val[name] for name in d.late_names]
            shape = [shaped((hb + sub, width))]
            body = bind(ffn_pack_kernel, g)
            hops(SPREAD_F, seq(body, shape, d.inner_keep, val[INNER], *late)[0])

        def ffn_end():
            shape = (hb, 2 * zs * fb) if g.aligned else (rs, hb, 2 * zs * sub)
            inner, d.sum_out = seq(
                bind(ffn_end_kernel, g),
                [stored(shape, F32), stored((fb, width), F32)],
                *[val[SPREAD_F, m] for m in range(rs)],
            )
            if not g.aligned:
                inner = jnp.transpose(inner.reshape(rs, hb, 2 * zs, sub), (1, 2, 0, 3))
                inner = inner.reshape(hb, -1)
            d.sum_in = inner

        def attn_split():
            d.attn_keep, d.mixer_keep, give = seq(
                bind(attn_split_kernel, g),
                [
                    shaped((hb + PAD, 3 * hb)),
                    shaped((hb, 2 * hb)),
                    shaped((hb + PAD, 3 * hb)),
                ],
                parts[GH_SUM][0],
                val[GH_SUM, zs - 1],
            )
            put(ATTN, give, core_pairs)

        def attn_pack():
            shape = [shaped((hb + PAD, 8 * hb))]
            args = d.attn_keep, d.mixer_keep, val[ATTN]
            hops(SPREAD_T, seq(bind(attn_pack_kernel, g), shape, *args)[0])

        def attn_end():
            *d.sum_attn, d.gains, d.table = seq(
                bind(attn_end_kernel, g),
                [stored((hb, width), F32)] * 4 + [shaped((8, hb), F32), shaped((heads, hb), F32)],
                *[val[SPREAD_T, m] for m in range(rs)],
            )

        def middle_back():
            more = [pltpu.VMEM((1, width), F32)] if g.aligned else []
            d.grad_mid, d.gmix, ggain, d.grad_wo = seq(
                bind(middle_back_kernel, g),
                [
                    stored((seq_len, width), F32),
                    shaped((tokens, rs * hb)),
                    shaped((1, width), F32),
                    shaped((zs, hb, width)),
                ],
                d.swap,
                val[SWAP],
                d.middle,
                d.gl,
                d.gain_m,
                d.mixed,
                d.wo,
                scratch=[pltpu.VMEM((tokens, width), BF16), pltpu.VMEM((seq_len, width), F32)]
                + more,
            )
            d.ggain_m = ggain if g.aligned else permute_cols(ggain, relative())
            parts[GH] = [None] * rs

        def attend_back(m, turn):
            if turn == rs - 1:
                outs = [shaped((seq_len, width), F32), shaped((seq_len, width))]
            else:
                outs = [shaped((tokens, width), F32)]
            outs = seq(
                bind(attn_back_kernel, g, m, turn),
                [shaped((zs, 2 * hb + PAD, 4 * hb))] + outs,
                seq_lengths,
                d.normed_t,
                d.offsets[m],
                d.qkv[m],
                d.gmix,
                d.grad_wo,
                d.hot,
                d.scaled,
                d.attn_w[m],
                *([d.ggain_m] if m == 0 else []),
                *([d.gn] if turn else []),
                scalars=1,
                scratch=[pltpu.VMEM((tokens, 3 * hb), BF16)],
            )
            parts[GH][m] = outs[0]
            if m % 2:
                hop_start(GH, m)
            if turn < rs - 1:
                d.gn = outs[1]
            else:
                own, sib = outs[1:]
                if not g.aligned:
                    back_to = jnp.argsort(relative())
                    own, sib = permute_cols(own, back_to), permute_cols(sib, back_to)
                d.gn = own
                put(NORMED, sib, core_pairs)

        def input_back():
            d.input_grad = seq(
                bind(input_back_kernel, g),
                [stored((seq_len, width))],
                d.gn,
                val[NORMED],
                d.grad_mid,
                x_own,
                d.gain_a,
                scratch=[pltpu.VMEM((seq_len, width), F32)],
            )[0]

        def layer_out():
            parts[LAYER] = seq(
                bind(layer_kernel, g),
                [shaped((seq_len, width))],
                seq_lengths,
                d.middle,
                d.outer_part,
                val[SWAP],
                scalars=1,
            )[0]

        def cot_end():
            deal_last(COT, True)
            put(COT_SIB, parts[COT], core_pairs)

        parts[COT] = cotangent[0]
        put(INPUT, x_own, core_pairs)
        bits = list(range(nb))
        step(start_core)
        step(start_attn)
        step(start_ffn)
        step(stack_attn)
        deal(COT, [nb] + bits, bits + [nb], True, cot_end)
        step(norm)
        for m in range(rs):
            step(attend, m)
        step(mixer)
        step(middle)
        step(ffn, 0)
        step(ffn, 1)
        step(middle_back)
        step(layer_out)
        back_order = [m for m in range(1, rs, 2)] + [m for m in range(rs - 2, -1, -2)]
        for turn, m in enumerate(back_order):
            step(attend_back, m, turn)
        step(input_back)
        for j in range(2, zs):
            step(sum_step, OA, j)
            step(sum_step, OB, j)
        for m in range(rs - 2, -1, -2):
            step(hop_add, GI, GI_SUM, m)
            step(hop_add, GH, GH_SUM, m)
        deal(LAYER, [nb] + bits, bits + [nb], False, bind(deal_last, LAYER, False))
        step(outer_end)
        step(outer_pair)
        for j in range(2, zs):
            step(sum_step, GI_SUM, j)
            step(sum_step, GH_SUM, j)
        step(inner_split)
        step(ffn_pack)
        step(attn_split)
        step(attn_pack)
        step(ffn_end)
        step(attn_end)
        for item in ORDER if (rs, zs) == (4, 4) else range(len(steps)):
            if isinstance(item, int):
                steps[item]()
            else:
                seq.arrived(val[item if len(item) > 1 else item[0]])

        gains, table = d.gains, d.table[:, :n_buckets].T
        sum_tab = lax.dynamic_slice(table, (c * (n_buckets // ss), 0), (n_buckets // ss, heads))
        return (
            parts[LAYER][None],
            d.input_grad[None],
            *d.sum_attn,
            d.sum_in,
            d.sum_out,
            gains[0],
            gains[1],
            sum_tab,
        )

    tokens_spec = P(AXES, None, None)
    rows_spec, part_spec = P("shard", None), P("shard")
    in_specs = (
        (tokens_spec,) * 2 + (P(),) * 3 + (rows_spec,) * 6 + (part_spec,) * 2 + (rows_spec,)
    )
    out_specs = (tokens_spec,) * 2 + (rows_spec,) * 6 + (part_spec,) * 2 + (rows_spec,)
    return jax.shard_map(local, mesh=mesh, in_specs=in_specs, out_specs=out_specs, check_vma=False)
```

```python
import functools

import jax
import jax.numpy as jnp
from jax import lax
from jax.experimental import pallas as pl
from jax.experimental.pallas import tpu as pltpu
from jax.sharding import PartitionSpec as P

EPSILON = 1e-06
MASKED = -1000000000.0
AXES = ("rep", "shard")
BF16 = jnp.bfloat16
F32 = jnp.float32
INV_SQRT2 = 0.7071067811865476
INV_SQRT2PI = 0.3989422804014327
PAD = 16

VMEM = pl.BlockSpec(memory_space=pltpu.VMEM)
SMEM = pl.BlockSpec(memory_space=pltpu.SMEM)
ANY = pl.BlockSpec(memory_space=pl.ANY)
HBM = pl.BlockSpec(memory_space=pltpu.HBM)


def shaped(shape, dtype=BF16):
    return jax.ShapeDtypeStruct(shape, dtype)


def kept(shape, dtype=BF16):
    return pltpu.VMEM(shape, dtype)


def stored(shape, dtype=BF16):
    return pltpu.HBM(shape, dtype)


class Sequence:
    def __init__(self):
        self.last = None

    def __call__(self, body, outs, *args, scalars=0, hbm=0, scratch=(), limit=12, after=()):
        n = len(args)
        args = [pltpu.with_memory_space_constraint(a, pltpu.HBM) if i >= n - hbm else a for i, a in enumerate(args)]
        specs = [SMEM] * scalars + [VMEM] * (n - scalars - hbm) + [HBM] * hbm
        extra = list(after) + ([] if self.last is None else [self.last])
        m = len(extra)

        def run(*refs):
            body(*refs[:n], *refs[n + m :])

        result = pl.pallas_call(
            run,
            out_shape=outs,
            in_specs=specs + [ANY] * m,
            out_specs=[VMEM] * len(outs),
            scratch_shapes=list(scratch),
            cost_estimate=pl.CostEstimate(flops=0, bytes_accessed=0, transcendentals=0),
            compiler_params=pltpu.CompilerParams(vmem_limit_bytes=limit * 1024 * 1024),
        )(*args, *extra)
        self.last = result[-1]
        return result

    def arrived(self, value):
        self(token_kernel, [kept((8, 128), F32)], after=[value], limit=4)


def dot(a, b):
    return jnp.dot(a, b, preferred_element_type=F32)


def dot_nt(a, b):
    return lax.dot_general(a, b, (((1,), (1,)), ((), ())), preferred_element_type=F32)


def dot_tn(a, b):
    return lax.dot_general(a, b, (((0,), (0,)), ((), ())), preferred_element_type=F32)


def lanes(block, size):
    return pl.ds(pl.multiple_of(block * size, size), size)


class Geometry:
    def __init__(self, rs, zs, hb, fb, heads, seq_len, width):
        self.rs, self.zs, self.hb, self.fb = rs, zs, hb, fb
        self.seq_len, self.width = seq_len, width
        self.tokens = 2 * seq_len
        self.bits = rs.bit_length() - 1
        self.sub = fb // rs
        self.cols = zs * self.sub
        self.hd = width // heads
        self.nh = hb // self.hd
        self.chips = rs * zs
        self.rows = seq_len // self.chips
        self.aligned = hb % 128 == 0 and self.sub % 128 == 0
        self.parts = width // self.cols

    def turned(self, m):
        out = 0
        for b in range(self.bits):
            out = out + (((m >> b) & 1) << (self.bits - 1 - b))
        return out

    def here(self):
        return Here(self)


class Here:
    def __init__(self, g):
        self.g = g
        self.r = lax.axis_index("rep").astype(jnp.int32)
        c = lax.axis_index("shard").astype(jnp.int32)
        self.z = lax.div(c, jnp.int32(2))
        self.k = lax.rem(c, jnp.int32(2))
        self.me = self.r * (2 * g.zs) + c

    def code(self, m, k=None):
        k = self.k if k is None else k
        return m + k * (self.g.turned(m) - m)

    def quarter(self, m):
        return self.r if m == 0 else lax.bitwise_xor(self.r, self.code(jnp.int32(m)))

    def even(self, c):
        return self.r if c == 0 else lax.bitwise_xor(self.r, jnp.int32(2 * c))

    def behind(self, j):
        return self.z if j == 0 else lax.rem(self.z + (self.g.zs - j), jnp.int32(self.g.zs))

    def shard(self, j, h):
        return 2 * self.behind(j) + (1 - self.k if h else self.k)


class Box:
    pass


class Copies:
    def __init__(self, sem):
        self.sem, self.all = sem, []

    def start(self, src, dst):
        copy = pltpu.make_async_copy(src, dst, self.sem)
        copy.start()
        self.all.append(copy)

    def wait(self):
        for copy in self.all:
            copy.wait()


def fetch_heads(g, at, copies, s, core, weights, dst, row):
    hb = g.hb
    for i, w in enumerate(weights):
        part = dst.at[pl.ds(row, hb), pl.ds(i * hb, hb)]
        copies.start(w.at[:, lanes(2 * s + core, hb)], part)


def fetch_inner(g, at, copies, s, core, wi, dst, row, col):
    hb, sub = g.hb, g.sub
    for b in range(g.zs):
        place = pl.ds(pl.multiple_of((2 * b + core) * g.fb + s * sub, sub), sub)
        copies.start(wi.at[:, place], dst.at[pl.ds(row, hb), pl.ds(col + b * sub, sub)])


def small_tile(g, gain_a, gain_m, table, out):
    hb = g.hb
    zero = jnp.zeros((PAD, hb), F32)
    row = lax.broadcasted_iota(jnp.int32, (PAD, hb), 0)
    for i, gain in enumerate((gain_a, gain_m)):
        tile = jnp.where(row == 0, jnp.broadcast_to(gain[...].astype(F32), (PAD, hb)), zero)
        out[:, i * hb : (i + 1) * hb] = tile.astype(BF16)
    out[:, 2 * hb :] = jnp.zeros((PAD, out.shape[1] - 2 * hb), BF16)
    n, heads = table.shape
    out[8 : 8 + n, 2 * hb : 2 * hb + heads] = table[...]


def send_prep_kernel(g, gain_a, gain_m, table, wq, wk, wv, wi, x, out, sem):
    at, hb = g.here(), g.hb
    copies, other = Copies(sem), 1 - at.k
    copies.start(x, out.at[pl.ds(g.rs * hb + PAD, g.seq_len), :])
    small_tile(g, gain_a, gain_m, table, out.at[pl.ds(g.rs * hb, PAD), :])
    for m in range(g.rs):
        s = lax.bitwise_xor(at.r, at.code(jnp.int32(m), other))
        fetch_heads(g, at, copies, s, other, (wq, wk, wv), out, m * hb)
    for c in range(g.rs // 2):
        fetch_inner(g, at, copies, at.even(c), other, wi, out, c * hb, 3 * hb)
    copies.wait()


def attn_prep_kernel(g, gain_a, gain_m, table, got, wq, wk, wv, wm, out, mine, sem):
    at, hb = g.here(), g.hb
    copies = Copies(sem)
    fetch_heads(g, at, copies, at.r, at.k, (wq, wk, wv), out, 0)
    for h in range(2):
        part = out.at[pl.ds(h * hb, hb), pl.ds(3 * hb, hb)]
        copies.start(wm.at[:, lanes(2 * at.r + h, hb)], part)
    out[hb : 2 * hb, : 3 * hb] = got[:hb, : 3 * hb]
    small_tile(g, gain_a, gain_m, table, mine)
    row = lax.broadcasted_iota(jnp.int32, (PAD, 4 * hb), 0)
    theirs = got[g.rs * hb : g.rs * hb + PAD, : 4 * hb].astype(F32)
    theirs = jnp.where(row < 8, pltpu.roll(theirs, 1, 0), pltpu.roll(theirs, 4, 0))
    ours = mine[...].astype(F32)
    both = jnp.where((row == 1) | (row >= 12), theirs, ours)
    out[2 * hb :, :] = both.astype(BF16)
    copies.wait()


def ffn_prep_kernel(g, got, wi, wu, out, sem):
    at, hb, sub, cols = g.here(), g.hb, g.sub, g.cols
    copies = Copies(sem)
    fetch_inner(g, at, copies, at.r, at.k, wi, out, 0, 0)
    for i in range(g.parts):
        part = out.at[pl.ds(2 * hb + i * sub, sub), :]
        copies.start(wu.at[lanes(at.r, sub), pl.ds(i * cols, cols)], part)
    out[hb : 2 * hb, :] = got[:hb, 3 * hb : 3 * hb + cols]
    copies.wait()


def spread_pack_kernel(*refs):
    *ins, out = refs
    for i, ref in enumerate(ins[:2]):
        out[i] = ref[...]
    at = 2
    for ref in ins[2:]:
        out[at : at + ref.shape[0]] = ref[...]
        at += ref.shape[0]


def spread_part(refs, m):
    if m < 2:
        return refs[m]
    b = m.bit_length() - 1
    return refs[b + 1].at[m - (1 << b)]


def stack_kernel(rows, *refs):
    *ins, out = refs
    for i, ref in enumerate(ins):
        out[i] = ref[:rows, :]


def token_kernel(out):
    out[...] = jnp.zeros_like(out)


def deal_first_kernel(g, labels, src, *outs):
    at = g.here()
    for out, some in zip(outs, labels):
        for i, (f, zz) in enumerate(some):
            chip = lax.bitwise_xor(at.r, at.code(jnp.int32(f))) * g.zs
            out[i] = src[chip + lax.bitwise_xor(at.z, zz)]


def deal_stage_kernel(places, n_in, *refs):
    ins, outs = refs[:n_in], refs[n_in:]
    for out, some in zip(outs, places):
        for i, (a, b) in enumerate(some):
            out[i] = ins[a][b]


def deal_middle_kernel(g, labels, back, table, own, got, *refs):
    outs, (lookup,) = refs[:-1], refs[-1:]
    at = g.here()
    if back:
        for s in range(2 * g.chips):
            lookup[table[s]] = jnp.int32(s)
    else:
        lookup = table
    for out, some in zip(outs, labels):
        for i, (f, zz) in enumerate(some):
            chip = lax.bitwise_xor(at.r, at.code(jnp.int32(f))) * g.zs
            dest = (chip + lax.bitwise_xor(at.z, zz)) * 2 + at.k
            src = lookup[dest]
            core = lax.rem(src, 2)
            src = lax.div(src, 2)
            sz, sr = lax.rem(src, g.zs), lax.div(src, g.zs)
            sf = at.code(lax.bitwise_xor(at.r, sr), core)
            place = sf * g.zs + lax.bitwise_xor(at.z, sz)
            mine = own[place].astype(F32)
            theirs = got[place].astype(F32)
            out[i] = jnp.where(core == at.k, mine, theirs).astype(BF16)


def deal_last_kernel(g, places, n_in, masked, lengths, *refs):
    ins, (out, pool) = refs[:n_in], refs[n_in:]
    at = g.here()
    for e, (a, b) in enumerate(places):
        pool[e] = ins[a][b]
    for chip in range(g.chips):
        f = at.code(lax.bitwise_xor(at.r, chip // g.zs))
        value = pool[f * g.zs + lax.bitwise_xor(at.z, chip % g.zs)]
        if masked:
            row = lax.broadcasted_iota(jnp.int32, value.shape, 0) + chip * g.rows
            value = jnp.where(row < lengths[at.me], value.astype(F32), 0.0).astype(BF16)
        out[chip] = value


def sum_kernel(picks, *refs):
    *ins, out = refs
    total = None
    for ref, pick in zip(ins, picks):
        v = (ref[...] if pick is None else ref[pick]).astype(F32)
        total = v if total is None else total + v
    out[...] = total.astype(out.dtype)


def cut_sum_kernel(g, *refs):
    n = len(refs) - g.zs
    for j, out in enumerate(refs[n:]):
        out[...] = sum(ref[j].astype(F32) for ref in refs[:n]).astype(BF16)


def outer_end_kernel(g, own, got, *outs):
    sub = g.sub
    for c, out in enumerate(outs):
        rows = slice(c * sub, (c + 1) * sub)
        out[...] = (own[rows, :].astype(F32) + got[rows, :].astype(F32)).astype(BF16)


def inner_split_kernel(g, *refs):
    *ins, keep, give = refs
    total = sum(ref[...].astype(F32) for ref in ins).astype(BF16)
    keep[...] = total[: g.hb]
    give[...] = total[g.hb :]


def ffn_pack_kernel(g, keep, got, *refs):
    *ins, out = refs
    first = g.here().k == 0
    hb, sub = g.hb, g.sub
    for b in range(g.zs):
        cols = slice(b * sub, (b + 1) * sub)
        mine, theirs = keep[:, cols].astype(F32), got[:, cols].astype(F32)
        out[:hb, 2 * b * sub : (2 * b + 1) * sub] = jnp.where(first, mine, theirs).astype(BF16)
        out[:hb, (2 * b + 1) * sub : (2 * b + 2) * sub] = jnp.where(first, theirs, mine).astype(BF16)
    out[hb:, :] = sum(ref[...].astype(F32) for ref in ins).astype(BF16)


def ffn_end_kernel(g, *refs):
    at, (inner, outer) = g.here(), refs[-2:]
    parts = [spread_part(refs, m) for m in range(g.rs)]
    hb, sub = g.hb, g.sub
    for m in range(g.rs):
        s = at.quarter(m)
        outer[lanes(s, sub), :] = parts[m][hb:, :].astype(F32)
        if g.aligned:
            for b in range(2 * g.zs):
                place = pl.ds(pl.multiple_of(b * g.fb + s * sub, sub), sub)
                inner[:, place] = parts[m][:hb, b * sub : (b + 1) * sub].astype(F32)
        else:
            inner[s] = parts[m][:hb, : 2 * g.zs * sub].astype(F32)


def attn_split_kernel(g, *refs):
    *ins, keep, mixer, give = refs
    hb = g.hb
    total = sum(ref[...].astype(F32) for ref in ins).astype(BF16)
    keep[:hb, :] = total[:hb, : 3 * hb]
    keep[hb:, :] = total[2 * hb :, : 3 * hb]
    mixer[:, :hb] = total[:hb, 3 * hb :]
    mixer[:, hb:] = total[hb : 2 * hb, 3 * hb :]
    give[:hb, :] = total[hb : 2 * hb, : 3 * hb]
    give[hb:, :] = total[2 * hb :, : 3 * hb]


def attn_pack_kernel(g, keep, mixer, got, out):
    first = g.here().k == 0
    hb = g.hb
    for b in range(3):
        cols = slice(b * hb, (b + 1) * hb)
        mine, theirs = keep[:, cols].astype(F32), got[:, cols].astype(F32)
        out[:, 2 * b * hb : (2 * b + 1) * hb] = jnp.where(first, mine, theirs).astype(BF16)
        out[:, (2 * b + 1) * hb : (2 * b + 2) * hb] = jnp.where(first, theirs, mine).astype(BF16)
    out[:hb, 6 * hb :] = mixer[...]
    out[hb:, 6 * hb :] = jnp.zeros((PAD, 2 * hb), BF16)


def attn_end_kernel(g, *refs):
    at, outs = g.here(), refs[-6:]
    parts = [spread_part(refs, m) for m in range(g.rs)]
    hb, size = g.hb, 2 * g.hb
    gains, table = outs[4:]
    total = None
    for m in range(g.rs):
        q = at.quarter(m)
        for i in range(4):
            outs[i][:, lanes(q, size)] = parts[m][:hb, size * i : size * (i + 1)].astype(F32)
        tiles = parts[m][hb:, :].astype(F32)
        pair = []
        for core in range(2):
            both = [tiles[:, (2 * b + core) * hb : (2 * b + core + 1) * hb] for b in range(3)]
            for i in range(g.nh):
                head = (2 * q + core) * g.nh + i
                table[pl.ds(head, 1), :] = both[2][2 + i : 3 + i, :]
            pair.append(both)
        own = [jnp.where(at.k == 0, pair[0][b][0:1], pair[1][b][0:1]) for b in range(2)]
        their = [jnp.where(at.k == 0, pair[1][b][1:2], pair[0][b][1:2]) for b in range(2)]
        some = [own[b] + their[b] for b in range(2)]
        total = some if total is None else [total[b] + some[b] for b in range(2)]
    for b in range(2):
        gains[b : b + 1, :] = total[b]


def to_relative(g, at, src, dst):
    hb = g.hb
    for j in range(g.zs):
        for h in range(2):
            e = 2 * j + h
            dst[:, e * hb : (e + 1) * hb] = src[:, lanes(at.shard(j, h), hb)]


def norm_kernel(g, own, got, gain, normed, normed_t, scaled, *scratch):
    half = own.shape[0]
    sib = got.at[pl.ds(g.rs * g.hb + PAD, half), :]
    plain, plain_scaled = scratch if g.aligned else (normed, scaled)
    for start, src in ((0, own), (half, sib)):
        v = src[...].astype(F32)
        scale = lax.rsqrt(jnp.mean(v * v, axis=-1, keepdims=True) + EPSILON)
        plain[start : start + half, :] = (v * scale * gain[...]).astype(BF16)
        plain_scaled[start : start + half, :] = (v * scale).astype(BF16)
    if g.aligned:
        to_relative(g, g.here(), plain, normed)
        to_relative(g, g.here(), plain_scaled, scaled)
    normed_t[...] = normed[...].T


def toeplitz(row, n):
    wide = jnp.broadcast_to(row, (n, 2 * n))
    return pltpu.roll(wide, n + 1, 1, stride=1, stride_axis=0)[:, :n]


def probabilities(q, kk, bias, length):
    n = q.shape[0]
    s = dot_nt(q, kk) + bias
    col = lax.broadcasted_iota(jnp.int32, (n, n), 1)
    s = jnp.where(col < length, s, MASKED)
    e = jnp.exp(s - jnp.max(s, axis=-1, keepdims=True))
    return e * (1.0 / jnp.sum(e, axis=-1, keepdims=True))


def two_lengths(at, lengths):
    return lengths[at.me], lengths[lax.bitwise_xor(at.me, 1)]


def attn_kernel(g, m, lengths, normed, off, first, rest, *refs):
    hb, hd = g.hb, g.hd
    at = g.here()
    both = two_lengths(at, lengths)
    if m == 0 or not g.aligned:
        qkv, mixed, w = refs
        w[: 2 * hb, :] = first[: 2 * hb, : 3 * hb]
        copies = None
    else:
        weights, (qkv, mixed, w, sem) = refs[:3], refs[3:]
        copies = Copies(sem)
        fetch_heads(g, at, copies, at.quarter(m), at.k, weights, w, 0)
        w[hb : 2 * hb, :] = first[m * hb : (m + 1) * hb, : 3 * hb]
    for j in range(1, g.zs):
        w[2 * hb * j : 2 * hb * (j + 1), :] = rest[j - 1, :, : 3 * hb]
    if copies is not None:
        copies.wait()
    qkv[...] = dot(normed[...], w[...]).astype(BF16)
    half = normed.shape[0] // 2
    for h in range(g.nh):
        bias = toeplitz(off[h : h + 1, :], half)
        for s in range(2):
            rows = slice(s * half, (s + 1) * half)
            q, kk, v = (qkv[rows, i * hb + h * hd : i * hb + (h + 1) * hd] for i in range(3))
            p = probabilities(q, kk, bias, both[s]).astype(BF16)
            mixed[rows, h * hd : (h + 1) * hd] = dot(p, v).astype(BF16)


def turned_head(g, at, block):
    return at.code(lax.bitwise_xor(block, at.r))


def mixer_kernel(g, *refs):
    rs, zs, hb = g.rs, g.zs, g.hb
    at = g.here()
    mixed_parts, own, rest = refs[:rs], refs[rs], refs[rs + 1 : 2 * rs + 1]
    mixed, wo, partial = refs[2 * rs + 1 :]
    for m in range(rs):
        mixed[:, m * hb : (m + 1) * hb] = mixed_parts[m][...]
    wo[lanes(turned_head(g, at, at.z), hb), :] = own[...]
    for m in range(rs):
        for j in range(1, zs):
            rows = lanes(turned_head(g, at, at.behind(j)), hb)
            piece = rest[m][j - 1, :, 3 * hb :]
            both = jnp.concatenate([piece[:hb], piece[hb:]], axis=1)
            wo[rows, lanes(at.quarter(m), 2 * hb)] = both
    partial[...] = dot(mixed[...], wo[...]).astype(BF16)


def middle_kernel(g, own, got, part, other, gain, *refs):
    sib = got.at[pl.ds(g.rs * g.hb + PAD, g.seq_len), :]
    middle, normed2, normed2_t, mine = refs[:4]
    plain = refs[4] if g.aligned else normed2
    half = own.shape[0]
    for s, src in ((0, own), (1, sib)):
        rows = slice(s * half, (s + 1) * half)
        swapped = slice((1 - s) * half, (2 - s) * half)
        v = src[...].astype(F32) + part[rows, :].astype(F32) + other[swapped, :].astype(F32)
        middle[rows, :] = v
        scale = lax.rsqrt(jnp.mean(v * v, axis=-1, keepdims=True) + EPSILON)
        plain[rows, :] = (v * scale * gain[...]).astype(BF16)
    if g.aligned:
        to_relative(g, g.here(), plain, normed2)
    normed2_t[...] = normed2[...].T
    mine[...] = normed2[:half, :]


def pair_swapped(g, value):
    if not g.aligned:
        return value
    hb = g.hb
    blocks = [value[:, e * hb : (e + 1) * hb] for e in range(2 * g.zs)]
    return jnp.concatenate([blocks[e ^ 1] for e in range(2 * g.zs)], axis=1)


def ffn_work(g, at, n2, n2_t, gl, w1s, w2s, done):
    out_sum, gn_sum = None, None
    for c in range(g.rs // 2):
        w1, w2 = w1s[c], w2s[c]
        h = dot(n2[...], w1[...])
        cdf = 0.5 * (1.0 + lax.erf(h * INV_SQRT2))
        pdf = jnp.exp(-0.5 * h * h) * INV_SQRT2PI
        act = (h * cdf).astype(BF16)
        ga = dot_nt(gl[...], w2[...])
        gh = (ga * (cdf + h * pdf)).astype(BF16)
        done(c, dot(n2_t[...], gh), dot_tn(act, gl[...]))
        out_part = dot(act, w2[...])
        gn_part = dot_nt(gh, w1[...])
        out_sum = out_part if out_sum is None else out_sum + out_part
        gn_sum = gn_part if gn_sum is None else gn_sum + gn_part
    return gn_sum, out_sum


def share_out(g, sums, own, swap):
    half = g.seq_len
    for i, total in enumerate(sums):
        own[i] = total[:half]
        swap[i] = total[half:].astype(BF16)


def ffn_own_kernel(g, n2, n2_t, gl_own, gl_sib, *refs):
    hb, sub, zs, cols = g.hb, g.sub, g.zs, g.cols
    at = g.here()
    half, n = g.seq_len, g.rs // 2
    pieces, refs = refs[: n * (zs - 1)], refs[n * (zs - 1) :]
    n_first = 2 if g.aligned else n
    firsts, refs = refs[:n_first], refs[n_first:]
    if g.aligned:
        wi, wu, refs = *refs[:2], refs[2:]
    gl, own, swap, go, refs = *refs[:4], refs[4:]
    grads, w1s, w2s, refs = refs[:n], refs[n : 2 * n], refs[2 * n : 3 * n], refs[3 * n :]
    copies = Copies(refs[0]) if g.aligned else None
    gl[:half, :] = gl_own[...]
    gl[half:, :] = gl_sib[...]

    def place_piece(piece, w1, w2, j):
        w1[2 * hb * j : 2 * hb * (j + 1), :] = piece[: 2 * hb, :]
        place = lanes(at.behind(j), sub)
        for b in range(g.parts):
            rows = slice(2 * hb + b * sub, 2 * hb + (b + 1) * sub)
            w2[place, b * cols : (b + 1) * cols] = piece[rows, :]

    for c in range(n):
        w1, w2 = w1s[c], w2s[c]
        if c and g.aligned:
            s = at.even(c)
            fetch_inner(g, at, copies, s, at.k, wi, w1, 0, 0)
            copies.start(wu.at[lanes(s, sub), :], w2.at[lanes(at.z, sub), :])
            w1[hb : 2 * hb, :] = firsts[-1][c * hb : (c + 1) * hb, 3 * hb : 3 * hb + cols]
        else:
            place_piece(firsts[c], w1, w2, 0)
        for j in range(1, zs):
            place_piece(pieces[c * (zs - 1) + j - 1], w1, w2, j)
    if copies is not None:
        copies.wait()

    def done(c, inner, outer):
        grads[c][...] = inner.astype(BF16).reshape(grads[c].shape)
        outer = outer.astype(BF16)
        for b in range(zs):
            place = lax.rem(at.z + (zs - b), zs)
            go[place, c * sub : (c + 1) * sub, :] = outer[b * sub : (b + 1) * sub, :]

    share_out(g, ffn_work(g, at, n2, n2_t, gl, w1s, w2s, done), own, swap)


def ffn_other_kernel(g, nx, nxk, gx, gxk, *refs):
    sub, zs, n, half = g.sub, g.zs, g.rs // 2, g.seq_len
    at = g.here()
    w1s, w2s, gi_in, refs = refs[:n], refs[n : 2 * n], refs[2 * n : 3 * n], refs[3 * n :]
    go_in, own, swap, refs = refs[0], refs[1], refs[2], refs[3:]
    grads, outs, (n2, n2_t, gl, go) = refs[:n], refs[n : n + zs], refs[n + zs :]
    n2[:half, :] = nx[...]
    n2[half:, :] = pair_swapped(g, nxk[...])
    n2_t[...] = n2[...].T
    gl[:half, :] = gx[...]
    gl[half:, :] = gxk[...]

    def done(c, inner, outer):
        shape = grads[c].shape
        grads[c][...] = (inner.reshape(shape) + gi_in[c][...].astype(F32)).astype(BF16)
        for b in range(zs):
            place = lax.rem(at.z + (zs - b), zs)
            rows = slice(c * sub, (c + 1) * sub)
            before = go_in[place, rows, :].astype(F32)
            go[place, rows, :] = (outer[b * sub : (b + 1) * sub, :] + before).astype(BF16)

    share_out(g, ffn_work(g, at, n2, n2_t, gl, w1s, w2s, done), own, swap)
    for j in range(zs):
        outs[j][...] = go[j]


def cross_sum_kernel(g, part, got, gn_out, outer_out):
    gn = part[0] + pair_swapped(g, got[0].astype(F32))
    gn_out[...] = gn.astype(BF16)
    outer_out[...] = (part[1] + got[1].astype(F32)).astype(BF16)


def own_sum_kernel(g, part, got, cross, out):
    total = part[0] + pair_swapped(g, got[0].astype(F32)) + cross[...].astype(F32)
    out[...] = total.astype(BF16)


def absolute_sum(g, at, part, other, rows, swapped, total):
    hb = g.hb
    if not g.aligned:
        total[...] = part[rows, :].astype(F32) + other[swapped, :].astype(F32)
        return
    for j in range(g.zs):
        for h in range(2):
            mine, theirs = 2 * j + h, 2 * j + 1 - h
            a = part[rows, mine * hb : (mine + 1) * hb].astype(F32)
            b = other[swapped, theirs * hb : (theirs + 1) * hb].astype(F32)
            total[:, lanes(at.shard(j, h), hb)] = a + b


def middle_back_kernel(g, own, other, middle, gl, gain, mixed, wo, *refs):
    grad_mid, gm, ggain, gwo, gatt, total = refs[:6]
    at, hb = g.here(), g.hb
    half, width = g.seq_len, g.width
    for s in range(2):
        rows = slice(s * half, (s + 1) * half)
        if g.aligned:
            for j in range(g.zs):
                for h in range(2):
                    e = 2 * j + (1 - h if s else h)
                    some = (other if s else own)[:, e * hb : (e + 1) * hb]
                    total[:, lanes(at.shard(j, h), hb)] = some.astype(F32)
        else:
            total[...] = (other if s else own)[...].astype(F32)
        gn = total[...]
        v = middle[rows, :]
        scale = lax.rsqrt(jnp.mean(v * v, axis=-1, keepdims=True) + EPSILON)
        gg = gn * gain[...]
        inner = jnp.sum(gg * v, axis=-1, keepdims=True) * (1.0 / width)
        grad = gl[rows, :].astype(F32) + scale * gg - v * (scale * scale * scale * inner)
        if s == 0:
            grad_mid[...] = grad
            sums = jnp.sum(gn * v * scale, axis=0, keepdims=True)
            if g.aligned:
                refs[6][...] = sums
                to_relative(g, at, refs[6], ggain)
            else:
                ggain[...] = sums
        gatt[rows, :] = grad.astype(BF16)
    gm[...] = dot_nt(gatt[...], wo[...]).astype(BF16)
    full = dot_tn(mixed[...], gatt[...]).astype(BF16)
    for m in range(g.rs):
        place = lax.rem(at.z + (g.zs - at.quarter(m)), g.zs)
        gwo[place] = full[m * hb : (m + 1) * hb, :]


def attn_back_kernel(g, m, step, lengths, normed_t, off, qkv, gmix, gwo, hot, scaled, w, *refs):
    hb, hd = g.hb, g.hd
    at = g.here()
    both = two_lengths(at, lengths)
    half = g.seq_len
    extra, refs = (refs[:1], refs[1:]) if m == 0 else ((), refs)
    before, refs = (refs[0], refs[1:]) if step else (None, refs)
    gw, *gn, gqkv = refs
    flip = (
        lax.broadcasted_iota(jnp.int32, (half, half), 0)
        + lax.broadcasted_iota(jnp.int32, (half, half), 1)
        == half - 1
    ).astype(BF16)
    table = []
    for h in range(g.nh):
        bias = toeplitz(off[h : h + 1, :], half)
        flipped = jnp.zeros((half, half), F32)
        for s in range(2):
            rows = slice(s * half, (s + 1) * half)
            q, kk, v = (qkv[rows, i * hb + h * hd : i * hb + (h + 1) * hd] for i in range(3))
            gm = gmix[rows, m * hb + h * hd : m * hb + (h + 1) * hd]
            p = probabilities(q, kk, bias, both[s])
            gp = dot_nt(gm, v)
            delta = jnp.sum(p * gp, axis=-1, keepdims=True)
            gs = (p * (gp - delta)).astype(BF16)
            flipped = flipped + dot(flip, gs)
            cols = [slice(i * hb + h * hd, i * hb + (h + 1) * hd) for i in range(3)]
            gqkv[rows, cols[0]] = dot(gs, kk).astype(BF16)
            gqkv[rows, cols[1]] = dot_tn(gs, q).astype(BF16)
            gqkv[rows, cols[2]] = dot_tn(p.astype(BF16), gm).astype(BF16)
        wide = jnp.concatenate([flipped, jnp.zeros((half, half), F32)], axis=1)
        skewed = pltpu.roll(wide, 0, 1, stride=1, stride_axis=0)
        diag = jnp.broadcast_to(jnp.sum(skewed, axis=0, keepdims=True), (8, 2 * half))
        top = diag.astype(BF16)
        table.append(dot_nt(top, hot[...]) + dot_nt((diag - top.astype(F32)).astype(BF16), hot[...]))
    gw[:, : 2 * hb, : 3 * hb] = (
        dot(normed_t[...], gqkv[...]).astype(BF16).reshape(g.zs, 2 * hb, 3 * hb)
    )
    row = lax.broadcasted_iota(jnp.int32, (PAD, hb), 0)
    buckets = jnp.zeros((PAD, hb), F32)
    for i, t in enumerate(table):
        buckets = jnp.where(row == 2 + i, jnp.broadcast_to(t[0:1], (PAD, hb)), buckets)
    for j in range(g.zs):
        piece = gwo[j, :, lanes(at.quarter(m), 2 * hb)]
        gw[j, :hb, 3 * hb :] = piece[:, :hb]
        gw[j, hb : 2 * hb, 3 * hb :] = piece[:, hb:]
        part = dot_nt(gqkv[...], w[2 * hb * j : 2 * hb * (j + 1), :])
        cols = slice(2 * hb * j, 2 * hb * (j + 1))
        gain = jnp.sum(part * scaled[:, cols].astype(F32), axis=0, keepdims=True)
        tile = [gain[:, :hb], gain[:, hb:]]
        tile = jnp.where(row == 0, tile[0], jnp.where(row == 1, tile[1], 0.0))
        gw[j, 2 * hb :, :hb] = tile.astype(BF16)
        if m == 0:
            tile = [extra[0][:, (2 * j + h) * hb : (2 * j + h + 1) * hb] for h in range(2)]
            tile = jnp.where(row == 0, tile[0], jnp.where(row == 1, tile[1], 0.0))
        else:
            tile = jnp.zeros((PAD, hb), F32)
        gw[j, 2 * hb :, hb : 2 * hb] = tile.astype(BF16)
        gw[j, 2 * hb :, 2 * hb : 3 * hb] = buckets.astype(BF16)
        gw[j, 2 * hb :, 3 * hb :] = jnp.zeros((PAD, hb), BF16)
        if before is not None:
            part = part + before[:, cols]
        if len(gn) == 1:
            gn[0][:, cols] = part
        else:
            gn[0][:, cols] = part[:half]
            gn[1][:, cols] = part[half:].astype(BF16)


def input_back_kernel(g, own, other, grad_mid, x, gain, out, total):
    everything = slice(None)
    absolute_sum(g, g.here(), own, other, everything, everything, total)
    gn = total[...]
    v = x[...].astype(F32)
    scale = lax.rsqrt(jnp.mean(v * v, axis=-1, keepdims=True) + EPSILON)
    gg = gn * gain[...]
    inner = jnp.mean(gg * v, axis=-1, keepdims=True)
    grad = grad_mid[...] + scale * gg - v * (scale * scale * scale * inner)
    out[...] = grad.astype(BF16)


def layer_kernel(g, lengths, middle, part, got, cross, out):
    half = g.seq_len
    row = lax.broadcasted_iota(jnp.int32, out.shape, 0)
    v = middle[:half, :] + part[1] + got[1].astype(F32) + cross[...].astype(F32)
    out[...] = jnp.where(row < lengths[g.here().me], v, 0.0).astype(BF16)


CORE, MIDDLE, SWAP, SWAP_X, NORMED, INNER, ATTN, COT, COT_SIB, COT_X, COT_XK, LAYER = range(12)
MINE_X, MINE_XK, GN_X, GN_K, OUTER_X = range(12, 17)
RING_A, RING_F, HOP_A, HOP_F, GI, GI_SUM, GH, GH_SUM, OA, LATE, SPREAD_F, SPREAD_T = range(17, 29)

ORDER = (
    0, 4, ((COT, 0), 2), 1, 5, (RING_A, 2), 6, 2, (RING_A, 3), ((COT, 2), 0), 3, 12, 13, 7, 15, 8,
    9, 14, 16, 10, ((HOP_F, 1), 1), ((COT, 0), 0), (RING_F, 3), 17, 18, ((COT, 5), 1),
    ((HOP_F, 3), 1), 11, ((HOP_F, 2), 1), (MINE_XK,), 19, (CORE,), 20, 21, 22, 30, 23, 25, 32, 31,
    24, 44, 26, 35, 27, (GH, 1), 46, 36, 33, 28, 34, 43, 37, 48, 45, 49, (OA, 3), (NORMED,), 38, 39,
    47, 40, 52, 50, ((LAYER, 4), 0), (OA, 1), 41, 51, ((LAYER, 5), 2), 29, ((LAYER, 5), 0), 53, 54,
    42, 55,
)


def solution(mesh):
    rs, ss = mesh.shape["rep"], mesh.shape["shard"]
    zs = ss // 2
    count = rs * ss
    nb = rs.bit_length() - 1

    def pairs(move):
        table = []
        for i in range(count):
            r, z, k = i // ss, (i % ss) // 2, i % 2
            r, z, k = move(r, z, k)
            table.append((i, (r * zs + z) * 2 + k))
        return table

    core_pairs = pairs(lambda r, z, k: (r, z, 1 - k))
    up_pairs = pairs(lambda r, z, k: (r, (z + 1) % zs, k))
    rep_pairs = [
        pairs(lambda r, z, k, b=b: (r ^ (1 << (nb - 1 - b if k else b)), z, k)) for b in range(nb)
    ]
    plain_pairs = [pairs(lambda r, z, k, b=b: (r ^ (1 << b), z, k)) for b in range(nb)]
    z_pairs = {m: pairs(lambda r, z, k, m=m: (r, z ^ m, k)) for m in range(1, zs)}

    def send(value, table):
        return lax.ppermute(value, AXES, table)

    by_size = sorted(range(1, rs), key=lambda m: (bin(m).count("1"), m))

    def high(m):
        return m.bit_length() - 1

    def low(m):
        return (m & -m).bit_length() - 1

    def local(
        inputs,
        cotangent,
        seq_lengths,
        dealing,
        rel_buckets,
        w_query,
        w_key,
        w_value,
        w_mixer,
        w_inner,
        w_outer,
        gain_attn,
        gain_mlp,
        bias_table,
    ):
        seq = Sequence()
        bind = functools.partial
        n_buckets, heads = bias_table.shape[0] * ss, bias_table.shape[1]
        g = Geometry(rs, zs, w_query.shape[0], w_outer.shape[0], heads, *inputs.shape[1:])
        hb, fb, sub, cols, nh = g.hb, g.fb, g.sub, g.cols, g.nh
        seq_len, width, tokens = g.seq_len, g.width, g.tokens
        chips, rows = g.chips, g.rows
        chunks = rs // 2

        r, c = lax.axis_index("rep"), lax.axis_index("shard")
        z, k = c // 2, c % 2
        shards = jnp.arange(ss, dtype=jnp.int32)
        x_own = inputs[0]
        d = Box()
        parts = {}

        def relative():
            return 2 * ((z + zs - shards // 2) % zs) + (k ^ (shards % 2))

        def permute_cols(x, order):
            return jnp.take(x.reshape(-1, ss, hb), order, axis=1).reshape(x.shape)

        val = {}
        steps = []

        def put(name, value, table):
            val[name] = send(value, table)

        def step(run, *args):
            steps.append(bind(run, *args))

        labels = [(f, zz) for f in range(rs) for zz in range(zs)]

        def groups_of(stage):
            if stage == nb:
                return [[e for e in labels if e[1] == zz] for zz in range(zs)]
            clear = [e for e in labels if not (e[0] >> stage) & 1]
            return [clear, [e for e in labels if e not in clear]]

        def block_shapes(groups):
            outs = [shaped((len(some), rows, width)) for some in groups]
            return outs if len(outs) == 1 else [stored(outs[0].shape)] + outs[1:]

        def dispatch(key, outs, stage):
            groups = groups_of(stage)
            val[key] = outs[0]
            state = [(key, groups[0])]
            for i, (out, some) in enumerate(zip(outs[1:], groups[1:])):
                put((key, i), out, z_pairs[i + 1] if stage == nb else rep_pairs[stage])
                state.append(((key, i), some))
            return state

        def places(state, some):
            at = {e: (a, b) for a, (_, named) in enumerate(state) for b, e in enumerate(named)}
            return [at[e] for e in some]

        def values(state):
            return [val[name] for name, _ in state]

        def deal_first(what, stage):
            groups = groups_of(stage)
            value = parts[what].reshape(chips, rows, width)
            outs = seq(bind(deal_first_kernel, g, groups), block_shapes(groups), value)
            parts[what] = dispatch((what, 0), outs, stage)

        def deal_stage(what, number, stage):
            groups, state = groups_of(stage), parts[what]
            body = bind(deal_stage_kernel, [places(state, some) for some in groups], len(state))
            outs = seq(body, block_shapes(groups), *values(state))
            parts[what] = dispatch((what, number), outs, stage)

        def deal_core(what):
            state = parts[what]
            body = bind(deal_stage_kernel, [places(state, labels)], len(state))
            parts[what] = seq(body, block_shapes([labels]), *values(state))[0]
            put((what, CORE), parts[what], core_pairs)

        def deal_middle(what, number, stage, back):
            groups = groups_of(stage)
            body = bind(deal_middle_kernel, g, groups, back)
            lookup = [pltpu.SMEM((count,), jnp.int32)]
            args = dealing, parts[what], val[what, CORE]
            outs = seq(body, block_shapes(groups), *args, scalars=1, scratch=lookup)
            parts[what] = dispatch((what, number), outs, stage)

        def deal_last(what, masked):
            state = parts[what]
            body = bind(deal_last_kernel, g, places(state, labels), len(state), masked)
            pool = [pltpu.VMEM((chips, rows, width), BF16)]
            shape = [shaped((chips, rows, width))]
            out = seq(body, shape, seq_lengths, *values(state), scalars=1, scratch=pool)[0]
            parts[what] = out.reshape(seq_len, width)

        def deal(what, first, second, back, end):
            step(deal_first, what, first[0])
            for i, stage in list(enumerate(first))[1:]:
                step(deal_stage, what, i, stage)
            step(deal_core, what)
            n = len(first)
            step(deal_middle, what, n, second[0], back)
            for i, stage in list(enumerate(second))[1:]:
                step(deal_stage, what, n + i, stage)
            step(end)

        copy_sem = pltpu.SemaphoreType.DMA(())

        def slices(m, core):
            s = r ^ (m + core * (g.turned(m) - m))
            at = (2 * s + core) * hb
            parts = [lax.dynamic_slice(w, (0, at), (hb, hb)) for w in (w_query, w_key, w_value)]
            return parts, lax.dynamic_slice(w_mixer, (0, s * 2 * hb), (hb, 2 * hb))

        def inner_slices(c, core):
            s = r ^ (2 * c)
            at = [(2 * b + core) * fb + s * sub for b in range(zs)]
            inner = [lax.dynamic_slice(w_inner, (0, a), (hb, sub)) for a in at]
            outer = lax.dynamic_slice(w_outer, (s * sub, 0), (sub, width))
            return inner, [outer[:, i * cols : (i + 1) * cols] for i in range(g.parts)]

        small_args = gain_attn.reshape(1, hb), gain_mlp.reshape(1, hb), bias_table

        def start_core():
            if g.aligned:
                sent = seq(
                    bind(send_prep_kernel, g),
                    [shaped((rs * hb + PAD + seq_len, width))],
                    *small_args,
                    w_query,
                    w_key,
                    w_value,
                    w_inner,
                    x_own,
                    hbm=5,
                    scratch=[copy_sem],
                )[0]
            else:
                sent = []
                for m in range(rs):
                    parts = slices(m, 1 - k)[0]
                    inner = inner_slices(m % (rs // 2), 1 - k)[0]
                    sent.append(jnp.concatenate(parts + inner, axis=1))
                sent = jnp.concatenate(sent + [small_rows()], axis=0)
                sent = jnp.pad(sent, ((0, 0), (0, width - sent.shape[1])))
                sent = jnp.concatenate([sent, x_own], axis=0)
            put(CORE, sent, core_pairs)

        def small_rows():
            tile = jnp.zeros((PAD, 3 * hb + cols), BF16)
            tile = tile.at[0, :hb].set(gain_attn).at[0, hb : 2 * hb].set(gain_mlp)
            n = bias_table.shape[0]
            return tile.at[8 : 8 + n, 2 * hb : 2 * hb + heads].set(bias_table)

        def start_attn():
            got = val[CORE]
            if g.aligned:
                own = seq(
                    bind(attn_prep_kernel, g),
                    [shaped((2 * hb + PAD, 4 * hb))],
                    *small_args,
                    got,
                    w_query,
                    w_key,
                    w_value,
                    w_mixer,
                    hbm=4,
                    scratch=[pltpu.VMEM((PAD, 4 * hb), BF16), copy_sem],
                )
            else:
                own = []
                for m in range(rs):
                    parts, mix = slices(m, k)
                    top = jnp.concatenate(parts + [mix[:, :hb]], axis=1)
                    bottom = [got[m * hb : (m + 1) * hb, : 3 * hb], mix[:, hb:]]
                    own.append(jnp.concatenate([top, jnp.concatenate(bottom, axis=1)], axis=0))
                mine = small_rows()[:, : 4 * hb]
                theirs = got[rs * hb : rs * hb + PAD, : 4 * hb]
                both = [mine[:1], theirs[:1], mine[2:12], theirs[8:12]]
                both = jnp.concatenate(both, axis=0)
                own[0] = jnp.concatenate([own[0], both], axis=0)
            d.attn_own = own
            ring(RING_A, own[0])

        def start_ffn():
            got = val[CORE]
            if g.aligned:
                own = seq(
                    bind(ffn_prep_kernel, g),
                    [shaped((4 * hb, cols))],
                    got,
                    w_inner,
                    w_outer,
                    hbm=2,
                    scratch=[copy_sem],
                )
            else:
                own = []
                for c in range(rs // 2):
                    top, below = inner_slices(c, k)
                    bottom = got[c * hb : (c + 1) * hb, 3 * hb : 3 * hb + cols]
                    own.append(
                        jnp.concatenate([jnp.concatenate(top, axis=1), bottom] + below, axis=0)
                    )
            d.ffn_own = own
            ring(RING_F, own[0])
            for j in range(1, zs):
                even_hops((HOP_F, j), val[RING_F, j])

        def ring(name, value):
            for j in range(1, zs):
                put((name, j), value if j == 1 else val[name, j - 1], up_pairs)

        def hops(name, value):
            val[name, 0] = value
            for m in by_size:
                put((name, m), val[name, m ^ (1 << high(m))], rep_pairs[high(m)])

        def even_hops(name, value):
            val[name, 0] = value
            for c in range(1, rs // 2):
                b = high(c)
                put((name, c), val[name, c ^ (1 << b)], plain_pairs[b + 1])

        def stack_attn():
            pieces = [val[RING_A, j] for j in range(1, zs)]
            shape = [shaped((zs - 1, 2 * hb, 4 * hb))]
            hops(HOP_A, seq(bind(stack_kernel, 2 * hb), shape, *pieces)[0])

        def small_params():
            pieces = [d.attn_own[0]] + [val[RING_A, j] for j in range(1, zs)]
            tiles = jnp.stack([piece[2 * hb :, :] for piece in pieces])
            order = (shards[:, None] == relative()[None, :]).astype(BF16)
            gains = dot(order, tiles[:, :2, : 2 * hb].reshape(ss, 2 * hb))
            d.gain_a = gains[:, :hb].reshape(1, width)
            d.gain_m = gains[:, hb:].reshape(1, width)
            n = n_buckets // ss
            table = tiles[:, 8:, 2 * hb : 2 * hb + heads].reshape(ss, 4, heads)[:, :n]
            table = dot(order, table.reshape(ss, n * heads)).reshape(n_buckets, heads)
            quarters = jnp.arange(rs, dtype=jnp.int32)
            quarters = r ^ (quarters + k * (g.turned(quarters) - quarters))
            head_ids = ((2 * quarters + k) * nh)[:, None] + jnp.arange(nh, dtype=jnp.int32)[None]
            pick = jnp.arange(heads, dtype=jnp.int32)[:, None] == head_ids.reshape(1, -1)
            padded = jnp.concatenate([rel_buckets, jnp.full((1,), -1, jnp.int32)])
            hot = padded[None, :] == jnp.arange(hb, dtype=jnp.int32)[:, None]
            d.hot = hot.astype(BF16)
            my_table = dot(table.astype(BF16), pick.astype(BF16)).astype(BF16)
            d.offsets = lax.dot_general(
                my_table,
                d.hot[:n_buckets],
                (((0,), (0,)), ((), ())),
                preferred_element_type=F32,
            ).reshape(rs, nh, 2 * seq_len)

        spare = [pltpu.VMEM((tokens, width), BF16)] if g.aligned else []

        def norm():
            small_params()
            normed, normed_t, scaled = seq(
                bind(norm_kernel, g),
                [shaped((tokens, width)), stored((width, tokens)), stored((tokens, width))],
                x_own,
                val[CORE],
                d.gain_a,
                scratch=spare * 2,
            )
            if not g.aligned:
                normed = permute_cols(normed, relative())
                scaled = permute_cols(scaled, relative())
                normed_t = normed.T
            d.normed, d.normed_t, d.scaled = normed, normed_t, scaled
            d.qkv, d.mixed_parts, d.attn_w = ([None] * rs for _ in range(3))

        def attend(m):
            own = m == 0 or not g.aligned
            weights = () if own else (w_query, w_key, w_value)
            d.qkv[m], d.mixed_parts[m], d.attn_w[m] = seq(
                bind(attn_kernel, g, m),
                [stored((tokens, 3 * hb)), stored((tokens, hb)), stored((width, 3 * hb))],
                seq_lengths,
                d.normed,
                d.offsets[m],
                d.attn_own[m] if own else val[CORE],
                val[HOP_A, m],
                *weights,
                scalars=1,
                hbm=len(weights),
                scratch=() if own else [copy_sem],
            )

        def mixer():
            d.mixed, d.wo, d.partial = seq(
                bind(mixer_kernel, g),
                [stored((tokens, rs * hb)), stored((rs * hb, width)), shaped((tokens, width))],
                *d.mixed_parts,
                w_mixer,
                *[val[HOP_A, m] for m in range(rs)],
            )
            put(MIDDLE, d.partial, core_pairs)

        def middle():
            d.middle, normed2, normed2_t, mine = seq(
                bind(middle_kernel, g),
                [
                    stored((tokens, width), F32),
                    shaped((tokens, width)),
                    shaped((width, tokens)),
                    shaped((seq_len, width)),
                ],
                x_own,
                val[CORE],
                d.partial,
                val[MIDDLE],
                d.gain_m,
                scratch=spare,
            )
            if not g.aligned:
                normed2 = permute_cols(normed2, relative())
                normed2_t, mine = normed2.T, normed2[:seq_len]
            put(MINE_X, mine, plain_pairs[0])
            put(MINE_XK, val[MINE_X], core_pairs)
            d.normed2, d.normed2_t = normed2, normed2_t

        sums = [shaped((2, seq_len, width), F32), shaped((2, seq_len, width))]
        weights_made = [shaped((width, cols))] * chunks + [shaped((cols, width))] * chunks

        def ffn_own():
            firsts = [d.ffn_own[0], val[CORE]] if g.aligned else d.ffn_own
            weights = (w_inner, w_outer) if g.aligned else ()
            outs = seq(
                bind(ffn_own_kernel, g),
                [shaped((tokens, width))]
                + sums
                + [shaped((zs, chunks * sub, width))]
                + [shaped((zs, 2 * hb, cols))] * chunks
                + weights_made,
                d.normed2,
                d.normed2_t,
                parts[COT],
                val[COT_SIB],
                *[val[(HOP_F, j), c] for c in range(chunks) for j in range(1, zs)],
                *firsts,
                *weights,
                hbm=len(weights),
                scratch=[copy_sem] if g.aligned else (),
                limit=24,
            )
            d.gl, d.ffn_part, swap, d.go = outs[:4]
            d.gi, d.weights = outs[4 : 4 + chunks], outs[4 + chunks :]
            put(SWAP, to_absolute(swap), core_pairs)

        def to_absolute(swap):
            if g.aligned:
                return swap
            return jnp.stack([permute_cols(swap[0], jnp.argsort(relative())), swap[1]])

        def ffn_other():
            nxk = val[MINE_XK]
            if not g.aligned:
                nxk = permute_cols(nxk, shards ^ 1)
            outs = seq(
                bind(ffn_other_kernel, g),
                sums + [shaped((zs, 2 * hb, cols))] * chunks + [shaped((chunks * sub, width))] * zs,
                val[MINE_X],
                nxk,
                val[COT_X],
                val[COT_XK],
                *d.weights,
                *d.gi,
                d.go,
                scratch=[
                    pltpu.VMEM((tokens, width), BF16),
                    pltpu.VMEM((width, tokens), BF16),
                    pltpu.VMEM((tokens, width), BF16),
                    pltpu.VMEM((zs, chunks * sub, width), BF16),
                ],
                limit=24,
            )
            d.cross_part, swap = outs[:2]
            parts[GI] = list(outs[2 : 2 + chunks])
            parts[OA] = outs[2 + chunks :]
            put(SWAP_X, to_absolute(swap), core_pairs)
            for c in range(1, chunks):
                if c % 2:
                    put((GI, c), parts[GI][c], plain_pairs[1])
            put((OA, 1), parts[OA][1], up_pairs)

        def cross_sum():
            part = d.cross_part
            if not g.aligned:
                part = jnp.stack([permute_cols(part[0], jnp.argsort(relative())), part[1]])
            gn, outer = seq(
                bind(cross_sum_kernel, g), [shaped((seq_len, width))] * 2, part, val[SWAP_X]
            )
            put(GN_X, gn, plain_pairs[0])
            put(OUTER_X, outer, plain_pairs[0])

        def own_sum():
            part = d.ffn_part
            if not g.aligned:
                part = jnp.stack([permute_cols(part[0], jnp.argsort(relative())), part[1]])
            shape = [shaped((seq_len, width))]
            d.gn2 = seq(bind(own_sum_kernel, g), shape, part, val[SWAP], val[GN_X])[0]
            put(GN_K, d.gn2, core_pairs)

        def add(*terms):
            shape = [shaped(terms[0].shape)]
            return seq(bind(sum_kernel, [None] * len(terms)), shape, *terms)[0]

        def sum_step(name, j):
            put((name, j), add(val[name, j - 1], parts[name][j]), up_pairs)

        def hop_start(name, m):
            put((name, m), parts[name][m], rep_pairs[low(m)])

        def inner_add(c):
            some = parts[GI]
            above = [c | 1 << b for b in range(nb - 1) if not (c >> b) & 1 and low(c | 1 << b) == b]
            terms = [some[c]] + [val[GI, i] for i in above]
            if c:
                some[c] = add(*terms)
                put((GI, c), some[c], plain_pairs[low(c) + 1])
            else:
                shape = [shaped(some[0].shape[1:])] * zs
                parts[GI_SUM] = seq(bind(cut_sum_kernel, g), shape, *terms)
                put((GI_SUM, 1), parts[GI_SUM][1], up_pairs)

        def hop_add(name, ring, m):
            some = parts[name]
            bits = [b for b in range(nb) if not (m >> b) & 1 and low(m | 1 << b) == b]
            terms = [some[m]] + [val[name, m | 1 << b] for b in bits]
            if m:
                some[m] = add(*terms)
                hop_start(name, m)
            else:
                shape = [shaped(some[0].shape[1:])] * zs
                parts[ring] = seq(bind(cut_sum_kernel, g), shape, *terms)
                put((ring, 1), parts[ring][1], up_pairs)

        def outer_end():
            shape = [shaped((sub, width))] * chunks
            some = list(seq(bind(outer_end_kernel, g), shape, parts[OA][0], val[OA, zs - 1]))
            names = []
            for c in range(chunks - 1, 0, -1):
                b = low(c)
                put((LATE, c), some[c], plain_pairs[b + 1])
                if c ^ (1 << b):
                    some[c ^ (1 << b)] = add(some[c ^ (1 << b)], val[LATE, c])
                else:
                    names.append((LATE, c))
            d.late, d.late_names = some, names

        def inner_split():
            keep, give = seq(
                bind(inner_split_kernel, g),
                [shaped((hb, cols))] * 2,
                parts[GI_SUM][0],
                val[GI_SUM, zs - 1],
            )
            d.inner_keep = keep
            put(INNER, give, core_pairs)

        def spread(name, value):
            val[name, 0] = value
            put((name, 1), value, rep_pairs[0])

        def spread_next(name):
            for b in range(1, nb):
                some = [val[name, i] for i in range(b + 1)]
                shape = [shaped((1 << b, *some[0].shape))]
                put((name, b + 1), seq(spread_pack_kernel, shape, *some)[0], rep_pairs[b])

        def ffn_pack():
            late = [d.late[0]] + [val[name] for name in d.late_names]
            shape = [shaped((hb + sub, width))]
            body = bind(ffn_pack_kernel, g)
            spread(SPREAD_F, seq(body, shape, d.inner_keep, val[INNER], *late)[0])

        def ffn_end():
            shape = (hb, 2 * zs * fb) if g.aligned else (rs, hb, 2 * zs * sub)
            inner, d.sum_out = seq(
                bind(ffn_end_kernel, g),
                [stored(shape, F32), stored((fb, width), F32)],
                *[val[SPREAD_F, i] for i in range(nb + 1)],
            )
            if not g.aligned:
                inner = jnp.transpose(inner.reshape(rs, hb, 2 * zs, sub), (1, 2, 0, 3))
                inner = inner.reshape(hb, -1)
            d.sum_in = inner

        def attn_split():
            d.attn_keep, d.mixer_keep, give = seq(
                bind(attn_split_kernel, g),
                [
                    shaped((hb + PAD, 3 * hb)),
                    shaped((hb, 2 * hb)),
                    shaped((hb + PAD, 3 * hb)),
                ],
                parts[GH_SUM][0],
                val[GH_SUM, zs - 1],
            )
            put(ATTN, give, core_pairs)

        def attn_pack():
            shape = [shaped((hb + PAD, 8 * hb))]
            args = d.attn_keep, d.mixer_keep, val[ATTN]
            spread(SPREAD_T, seq(bind(attn_pack_kernel, g), shape, *args)[0])

        def attn_end():
            *d.sum_attn, d.gains, d.table = seq(
                bind(attn_end_kernel, g),
                [stored((hb, width), F32)] * 4 + [shaped((8, hb), F32), shaped((heads, hb), F32)],
                *[val[SPREAD_T, i] for i in range(nb + 1)],
            )

        def middle_back():
            more = [pltpu.VMEM((1, width), F32)] if g.aligned else []
            d.grad_mid, d.gmix, ggain, d.grad_wo = seq(
                bind(middle_back_kernel, g),
                [
                    stored((seq_len, width), F32),
                    shaped((tokens, rs * hb)),
                    shaped((1, width), F32),
                    shaped((zs, hb, width)),
                ],
                d.gn2,
                val[GN_K],
                d.middle,
                d.gl,
                d.gain_m,
                d.mixed,
                d.wo,
                scratch=[pltpu.VMEM((tokens, width), BF16), pltpu.VMEM((seq_len, width), F32)]
                + more,
            )
            d.ggain_m = ggain if g.aligned else permute_cols(ggain, relative())
            parts[GH] = [None] * rs

        def attend_back(m, turn):
            if turn == rs - 1:
                outs = [shaped((seq_len, width), F32), shaped((seq_len, width))]
            else:
                outs = [shaped((tokens, width), F32)]
            outs = seq(
                bind(attn_back_kernel, g, m, turn),
                [shaped((zs, 2 * hb + PAD, 4 * hb))] + outs,
                seq_lengths,
                d.normed_t,
                d.offsets[m],
                d.qkv[m],
                d.gmix,
                d.grad_wo,
                d.hot,
                d.scaled,
                d.attn_w[m],
                *([d.ggain_m] if m == 0 else []),
                *([d.gn] if turn else []),
                scalars=1,
                scratch=[pltpu.VMEM((tokens, 3 * hb), BF16)],
            )
            parts[GH][m] = outs[0]
            if m % 2:
                hop_start(GH, m)
            if turn < rs - 1:
                d.gn = outs[1]
            else:
                own, sib = outs[1:]
                if not g.aligned:
                    back_to = jnp.argsort(relative())
                    own, sib = permute_cols(own, back_to), permute_cols(sib, back_to)
                d.gn = own
                put(NORMED, sib, core_pairs)

        def input_back():
            d.input_grad = seq(
                bind(input_back_kernel, g),
                [stored((seq_len, width))],
                d.gn,
                val[NORMED],
                d.grad_mid,
                x_own,
                d.gain_a,
                scratch=[pltpu.VMEM((seq_len, width), F32)],
            )[0]

        def layer_out():
            parts[LAYER] = seq(
                bind(layer_kernel, g),
                [shaped((seq_len, width))],
                seq_lengths,
                d.middle,
                d.ffn_part,
                val[SWAP],
                val[OUTER_X],
                scalars=1,
            )[0]

        def cot_end():
            deal_last(COT, True)
            put(COT_SIB, parts[COT], core_pairs)
            put(COT_X, parts[COT], plain_pairs[0])
            put(COT_XK, val[COT_X], core_pairs)

        parts[COT] = cotangent[0]
        bits = list(range(nb))
        step(start_core)
        step(start_attn)
        step(start_ffn)
        step(stack_attn)
        deal(COT, [nb] + bits, bits + [nb], True, cot_end)
        step(norm)
        for m in range(rs):
            step(attend, m)
        step(mixer)
        step(middle)
        step(ffn_own)
        step(ffn_other)
        step(cross_sum)
        step(own_sum)
        step(middle_back)
        step(layer_out)
        back_order = [m for m in range(1, rs, 2)] + [m for m in range(rs - 2, -1, -2)]
        for turn, m in enumerate(back_order):
            step(attend_back, m, turn)
        step(input_back)
        for j in range(2, zs):
            step(sum_step, OA, j)
        for i in range(chunks - 2, -1, -2):
            step(inner_add, i)
        for m in range(rs - 2, -1, -2):
            step(hop_add, GH, GH_SUM, m)
        deal(LAYER, [nb] + bits, bits + [nb], False, bind(deal_last, LAYER, False))
        step(outer_end)
        for j in range(2, zs):
            step(sum_step, GI_SUM, j)
            step(sum_step, GH_SUM, j)
        step(inner_split)
        step(ffn_pack)
        step(attn_split)
        step(attn_pack)
        step(spread_next, SPREAD_F)
        step(spread_next, SPREAD_T)
        step(ffn_end)
        step(attn_end)
        for item in ORDER if (rs, zs) == (4, 4) else range(len(steps)):
            if isinstance(item, int):
                steps[item]()
            else:
                seq.arrived(val[item if len(item) > 1 else item[0]])

        gains, table = d.gains, d.table[:, :n_buckets].T
        sum_tab = lax.dynamic_slice(table, (c * (n_buckets // ss), 0), (n_buckets // ss, heads))
        return (
            parts[LAYER][None],
            d.input_grad[None],
            *d.sum_attn,
            d.sum_in,
            d.sum_out,
            gains[0],
            gains[1],
            sum_tab,
        )

    tokens_spec = P(AXES, None, None)
    rows_spec, part_spec = P("shard", None), P("shard")
    in_specs = (
        (tokens_spec,) * 2 + (P(),) * 3 + (rows_spec,) * 6 + (part_spec,) * 2 + (rows_spec,)
    )
    out_specs = (tokens_spec,) * 2 + (rows_spec,) * 6 + (part_spec,) * 2 + (rows_spec,)
    return jax.shard_map(local, mesh=mesh, in_specs=in_specs, out_specs=out_specs, check_vma=False)
```

```python
import functools

import jax
import jax.numpy as jnp
from jax import lax
from jax.experimental import pallas as pl
from jax.experimental.pallas import tpu as pltpu
from jax.sharding import PartitionSpec as P

EPSILON = 1e-06
MASKED = -1000000000.0
AXES = ("rep", "shard")
BF16 = jnp.bfloat16
F32 = jnp.float32
INV_SQRT2 = 0.7071067811865476
INV_SQRT2PI = 0.3989422804014327
PAD = 16

VMEM = pl.BlockSpec(memory_space=pltpu.VMEM)
SMEM = pl.BlockSpec(memory_space=pltpu.SMEM)
ANY = pl.BlockSpec(memory_space=pl.ANY)
HBM = pl.BlockSpec(memory_space=pltpu.HBM)


def shaped(shape, dtype=BF16):
    return jax.ShapeDtypeStruct(shape, dtype)


def kept(shape, dtype=BF16):
    return pltpu.VMEM(shape, dtype)


def stored(shape, dtype=BF16):
    return pltpu.HBM(shape, dtype)


class Sequence:
    def __init__(self):
        self.last = None

    def __call__(self, body, outs, *args, scalars=0, hbm=0, scratch=(), limit=12, after=()):
        n = len(args)
        args = [pltpu.with_memory_space_constraint(a, pltpu.HBM) if i >= n - hbm else a for i, a in enumerate(args)]
        specs = [SMEM] * scalars + [VMEM] * (n - scalars - hbm) + [HBM] * hbm
        extra = list(after) + ([] if self.last is None else [self.last])
        m = len(extra)

        def run(*refs):
            body(*refs[:n], *refs[n + m :])

        result = pl.pallas_call(
            run,
            out_shape=outs,
            in_specs=specs + [ANY] * m,
            out_specs=[VMEM] * len(outs),
            scratch_shapes=list(scratch),
            cost_estimate=pl.CostEstimate(flops=0, bytes_accessed=0, transcendentals=0),
            compiler_params=pltpu.CompilerParams(vmem_limit_bytes=limit * 1024 * 1024),
        )(*args, *extra)
        self.last = result[-1]
        return result

    def arrived(self, value):
        self(token_kernel, [kept((8, 128), F32)], after=[value], limit=4)


def dot(a, b):
    return jnp.dot(a, b, preferred_element_type=F32)


def dot_nt(a, b):
    return lax.dot_general(a, b, (((1,), (1,)), ((), ())), preferred_element_type=F32)


def dot_tn(a, b):
    return lax.dot_general(a, b, (((0,), (0,)), ((), ())), preferred_element_type=F32)


def lanes(block, size):
    return pl.ds(pl.multiple_of(block * size, size), size)


class Geometry:
    def __init__(self, rs, zs, hb, fb, heads, seq_len, width):
        self.rs, self.zs, self.hb, self.fb = rs, zs, hb, fb
        self.seq_len, self.width = seq_len, width
        self.tokens = 2 * seq_len
        self.bits = rs.bit_length() - 1
        self.sub = fb // rs
        self.cols = zs * self.sub
        self.hd = width // heads
        self.nh = hb // self.hd
        self.chips = rs * zs
        self.rows = seq_len // self.chips
        self.aligned = hb % 128 == 0 and self.sub % 128 == 0
        self.parts = width // self.cols

    def turned(self, m):
        out = 0
        for b in range(self.bits):
            out = out + (((m >> b) & 1) << (self.bits - 1 - b))
        return out

    def here(self):
        return Here(self)


class Here:
    def __init__(self, g):
        self.g = g
        self.r = lax.axis_index("rep").astype(jnp.int32)
        c = lax.axis_index("shard").astype(jnp.int32)
        self.z = lax.div(c, jnp.int32(2))
        self.k = lax.rem(c, jnp.int32(2))
        self.me = self.r * (2 * g.zs) + c

    def code(self, m, k=None):
        k = self.k if k is None else k
        return m + k * (self.g.turned(m) - m)

    def quarter(self, m):
        return self.r if m == 0 else lax.bitwise_xor(self.r, self.code(jnp.int32(m)))

    def even(self, c):
        return self.r if c == 0 else lax.bitwise_xor(self.r, jnp.int32(2 * c))

    def behind(self, j):
        return self.z if j == 0 else lax.rem(self.z + (self.g.zs - j), jnp.int32(self.g.zs))

    def shard(self, j, h):
        return 2 * self.behind(j) + (1 - self.k if h else self.k)


class Box:
    pass


class Copies:
    def __init__(self, sem):
        self.sem, self.all = sem, []

    def start(self, src, dst):
        copy = pltpu.make_async_copy(src, dst, self.sem)
        copy.start()
        self.all.append(copy)

    def wait(self):
        for copy in self.all:
            copy.wait()


def fetch_heads(g, at, copies, s, core, weights, dst, row):
    hb = g.hb
    for i, w in enumerate(weights):
        part = dst.at[pl.ds(row, hb), pl.ds(i * hb, hb)]
        copies.start(w.at[:, lanes(2 * s + core, hb)], part)


def fetch_inner(g, at, copies, s, core, wi, dst, row, col):
    hb, sub = g.hb, g.sub
    for b in range(g.zs):
        place = pl.ds(pl.multiple_of((2 * b + core) * g.fb + s * sub, sub), sub)
        copies.start(wi.at[:, place], dst.at[pl.ds(row, hb), pl.ds(col + b * sub, sub)])


def small_tile(g, gain_a, gain_m, table, out):
    hb = g.hb
    zero = jnp.zeros((PAD, hb), F32)
    row = lax.broadcasted_iota(jnp.int32, (PAD, hb), 0)
    for i, gain in enumerate((gain_a, gain_m)):
        tile = jnp.where(row == 0, jnp.broadcast_to(gain[...].astype(F32), (PAD, hb)), zero)
        out[:, i * hb : (i + 1) * hb] = tile.astype(BF16)
    out[:, 2 * hb :] = jnp.zeros((PAD, out.shape[1] - 2 * hb), BF16)
    n, heads = table.shape
    out[8 : 8 + n, 2 * hb : 2 * hb + heads] = table[...]


def send_prep_kernel(g, gain_a, gain_m, table, wq, wk, wv, wi, x, out, sem):
    at, hb = g.here(), g.hb
    copies, other = Copies(sem), 1 - at.k
    copies.start(x, out.at[pl.ds(g.rs * hb + PAD, g.seq_len), :])
    small_tile(g, gain_a, gain_m, table, out.at[pl.ds(g.rs * hb, PAD), :])
    for m in range(g.rs):
        s = lax.bitwise_xor(at.r, at.code(jnp.int32(m), other))
        fetch_heads(g, at, copies, s, other, (wq, wk, wv), out, m * hb)
    for c in range(g.rs // 2):
        fetch_inner(g, at, copies, at.even(c), other, wi, out, c * hb, 3 * hb)
    copies.wait()


def attn_prep_kernel(g, gain_a, gain_m, table, got, wq, wk, wv, wm, out, mine, sem):
    at, hb = g.here(), g.hb
    copies = Copies(sem)
    fetch_heads(g, at, copies, at.r, at.k, (wq, wk, wv), out, 0)
    for h in range(2):
        part = out.at[pl.ds(h * hb, hb), pl.ds(3 * hb, hb)]
        copies.start(wm.at[:, lanes(2 * at.r + h, hb)], part)
    out[hb : 2 * hb, : 3 * hb] = got[:hb, : 3 * hb]
    small_tile(g, gain_a, gain_m, table, mine)
    row = lax.broadcasted_iota(jnp.int32, (PAD, 4 * hb), 0)
    theirs = got[g.rs * hb : g.rs * hb + PAD, : 4 * hb].astype(F32)
    theirs = jnp.where(row < 8, pltpu.roll(theirs, 1, 0), pltpu.roll(theirs, 4, 0))
    ours = mine[...].astype(F32)
    both = jnp.where((row == 1) | (row >= 12), theirs, ours)
    out[2 * hb :, :] = both.astype(BF16)
    copies.wait()


def ffn_prep_kernel(g, got, wi, wu, out, sem):
    at, hb, sub, cols = g.here(), g.hb, g.sub, g.cols
    copies = Copies(sem)
    fetch_inner(g, at, copies, at.r, at.k, wi, out, 0, 0)
    for i in range(g.parts):
        part = out.at[pl.ds(2 * hb + i * sub, sub), :]
        copies.start(wu.at[lanes(at.r, sub), pl.ds(i * cols, cols)], part)
    out[hb : 2 * hb, :] = got[:hb, 3 * hb : 3 * hb + cols]
    copies.wait()


def spread_pack_kernel(*refs):
    *ins, out = refs
    for i, ref in enumerate(ins[:2]):
        out[i] = ref[...]
    at = 2
    for ref in ins[2:]:
        out[at : at + ref.shape[0]] = ref[...]
        at += ref.shape[0]


def spread_part(refs, m):
    if m < 2:
        return refs[m]
    b = m.bit_length() - 1
    return refs[b + 1].at[m - (1 << b)]


def stack_kernel(rows, *refs):
    *ins, out = refs
    for i, ref in enumerate(ins):
        out[i] = ref[:rows, :]


def token_kernel(out):
    out[...] = jnp.zeros_like(out)


def deal_first_kernel(g, labels, src, *outs):
    at = g.here()
    for out, some in zip(outs, labels):
        for i, (f, zz) in enumerate(some):
            chip = lax.bitwise_xor(at.r, at.code(jnp.int32(f))) * g.zs
            out[i] = src[chip + lax.bitwise_xor(at.z, zz)]


def deal_stage_kernel(places, n_in, *refs):
    ins, outs = refs[:n_in], refs[n_in:]
    for out, some in zip(outs, places):
        for i, (a, b) in enumerate(some):
            out[i] = ins[a][b]


def deal_middle_kernel(g, labels, back, table, own, got, *refs):
    outs, (lookup,) = refs[:-1], refs[-1:]
    at = g.here()
    if back:
        for s in range(2 * g.chips):
            lookup[table[s]] = jnp.int32(s)
    else:
        lookup = table
    for out, some in zip(outs, labels):
        for i, (f, zz) in enumerate(some):
            chip = lax.bitwise_xor(at.r, at.code(jnp.int32(f))) * g.zs
            dest = (chip + lax.bitwise_xor(at.z, zz)) * 2 + at.k
            src = lookup[dest]
            core = lax.rem(src, 2)
            src = lax.div(src, 2)
            sz, sr = lax.rem(src, g.zs), lax.div(src, g.zs)
            sf = at.code(lax.bitwise_xor(at.r, sr), core)
            place = sf * g.zs + lax.bitwise_xor(at.z, sz)
            mine = own[place].astype(F32)
            theirs = got[place].astype(F32)
            out[i] = jnp.where(core == at.k, mine, theirs).astype(BF16)


def deal_last_kernel(g, places, n_in, masked, lengths, *refs):
    ins, (out, pool) = refs[:n_in], refs[n_in:]
    at = g.here()
    for e, (a, b) in enumerate(places):
        pool[e] = ins[a][b]
    for chip in range(g.chips):
        f = at.code(lax.bitwise_xor(at.r, chip // g.zs))
        value = pool[f * g.zs + lax.bitwise_xor(at.z, chip % g.zs)]
        if masked:
            row = lax.broadcasted_iota(jnp.int32, value.shape, 0) + chip * g.rows
            value = jnp.where(row < lengths[at.me], value.astype(F32), 0.0).astype(BF16)
        out[chip] = value


def sum_kernel(picks, *refs):
    *ins, out = refs
    total = None
    for ref, pick in zip(ins, picks):
        v = (ref[...] if pick is None else ref[pick]).astype(F32)
        total = v if total is None else total + v
    out[...] = total.astype(out.dtype)


def cut_sum_kernel(g, *refs):
    n = len(refs) - g.zs
    for j, out in enumerate(refs[n:]):
        out[...] = sum(ref[j].astype(F32) for ref in refs[:n]).astype(BF16)


def outer_end_kernel(g, own, got, *outs):
    sub = g.sub
    for c, out in enumerate(outs):
        rows = slice(c * sub, (c + 1) * sub)
        out[...] = (own[rows, :].astype(F32) + got[rows, :].astype(F32)).astype(BF16)


def inner_split_kernel(g, *refs):
    *ins, keep, give = refs
    total = sum(ref[...].astype(F32) for ref in ins).astype(BF16)
    keep[...] = total[: g.hb]
    give[...] = total[g.hb :]


def ffn_pack_kernel(g, keep, got, *refs):
    *ins, out = refs
    first = g.here().k == 0
    hb, sub = g.hb, g.sub
    for b in range(g.zs):
        cols = slice(b * sub, (b + 1) * sub)
        mine, theirs = keep[:, cols].astype(F32), got[:, cols].astype(F32)
        out[:hb, 2 * b * sub : (2 * b + 1) * sub] = jnp.where(first, mine, theirs).astype(BF16)
        out[:hb, (2 * b + 1) * sub : (2 * b + 2) * sub] = jnp.where(first, theirs, mine).astype(BF16)
    out[hb:, :] = sum(ref[...].astype(F32) for ref in ins).astype(BF16)


def ffn_end_kernel(g, *refs):
    at, (inner, outer) = g.here(), refs[-2:]
    parts = [spread_part(refs, m) for m in range(g.rs)]
    hb, sub = g.hb, g.sub
    for m in range(g.rs):
        s = at.quarter(m)
        outer[lanes(s, sub), :] = parts[m][hb:, :].astype(F32)
        if g.aligned:
            for b in range(2 * g.zs):
                place = pl.ds(pl.multiple_of(b * g.fb + s * sub, sub), sub)
                inner[:, place] = parts[m][:hb, b * sub : (b + 1) * sub].astype(F32)
        else:
            inner[s] = parts[m][:hb, : 2 * g.zs * sub].astype(F32)


def attn_split_kernel(g, *refs):
    *ins, keep, mixer, give = refs
    hb = g.hb
    total = sum(ref[...].astype(F32) for ref in ins).astype(BF16)
    keep[:hb, :] = total[:hb, : 3 * hb]
    keep[hb:, :] = total[2 * hb :, : 3 * hb]
    mixer[:, :hb] = total[:hb, 3 * hb :]
    mixer[:, hb:] = total[hb : 2 * hb, 3 * hb :]
    give[:hb, :] = total[hb : 2 * hb, : 3 * hb]
    give[hb:, :] = total[2 * hb :, : 3 * hb]


def attn_pack_kernel(g, keep, mixer, got, out):
    first = g.here().k == 0
    hb = g.hb
    for b in range(3):
        cols = slice(b * hb, (b + 1) * hb)
        mine, theirs = keep[:, cols].astype(F32), got[:, cols].astype(F32)
        out[:, 2 * b * hb : (2 * b + 1) * hb] = jnp.where(first, mine, theirs).astype(BF16)
        out[:, (2 * b + 1) * hb : (2 * b + 2) * hb] = jnp.where(first, theirs, mine).astype(BF16)
    out[:hb, 6 * hb :] = mixer[...]
    out[hb:, 6 * hb :] = jnp.zeros((PAD, 2 * hb), BF16)


def attn_end_kernel(g, *refs):
    at, outs = g.here(), refs[-6:]
    parts = [spread_part(refs, m) for m in range(g.rs)]
    hb, size = g.hb, 2 * g.hb
    gains, table = outs[4:]
    total = None
    for m in range(g.rs):
        q = at.quarter(m)
        for i in range(4):
            outs[i][:, lanes(q, size)] = parts[m][:hb, size * i : size * (i + 1)].astype(F32)
        tiles = parts[m][hb:, :].astype(F32)
        pair = []
        for core in range(2):
            both = [tiles[:, (2 * b + core) * hb : (2 * b + core + 1) * hb] for b in range(3)]
            for i in range(g.nh):
                head = (2 * q + core) * g.nh + i
                table[pl.ds(head, 1), :] = both[2][2 + i : 3 + i, :]
            pair.append(both)
        own = [jnp.where(at.k == 0, pair[0][b][0:1], pair[1][b][0:1]) for b in range(2)]
        their = [jnp.where(at.k == 0, pair[1][b][1:2], pair[0][b][1:2]) for b in range(2)]
        some = [own[b] + their[b] for b in range(2)]
        total = some if total is None else [total[b] + some[b] for b in range(2)]
    for b in range(2):
        gains[b : b + 1, :] = total[b]


def to_relative(g, at, src, dst):
    hb = g.hb
    for j in range(g.zs):
        for h in range(2):
            e = 2 * j + h
            dst[:, e * hb : (e + 1) * hb] = src[:, lanes(at.shard(j, h), hb)]


def norm_kernel(g, own, got, gain, normed, normed_t, scaled, *scratch):
    half = own.shape[0]
    sib = got.at[pl.ds(g.rs * g.hb + PAD, half), :]
    plain, plain_scaled = scratch if g.aligned else (normed, scaled)
    for start, src in ((0, own), (half, sib)):
        v = src[...].astype(F32)
        scale = lax.rsqrt(jnp.mean(v * v, axis=-1, keepdims=True) + EPSILON)
        plain[start : start + half, :] = (v * scale * gain[...]).astype(BF16)
        plain_scaled[start : start + half, :] = (v * scale).astype(BF16)
    if g.aligned:
        to_relative(g, g.here(), plain, normed)
        to_relative(g, g.here(), plain_scaled, scaled)
    normed_t[...] = normed[...].T


def toeplitz(row, n):
    wide = jnp.broadcast_to(row, (n, 2 * n))
    return pltpu.roll(wide, n + 1, 1, stride=1, stride_axis=0)[:, :n]


def probabilities(q, kk, bias, length):
    n = q.shape[0]
    s = dot_nt(q, kk) + bias
    col = lax.broadcasted_iota(jnp.int32, (n, n), 1)
    s = jnp.where(col < length, s, MASKED)
    e = jnp.exp(s - jnp.max(s, axis=-1, keepdims=True))
    return e * (1.0 / jnp.sum(e, axis=-1, keepdims=True))


def two_lengths(at, lengths):
    return lengths[at.me], lengths[lax.bitwise_xor(at.me, 1)]


def attn_kernel(g, m, lengths, normed, off, first, rest, *refs):
    hb, hd = g.hb, g.hd
    at = g.here()
    both = two_lengths(at, lengths)
    if m == 0 or not g.aligned:
        qkv, mixed, w = refs
        w[: 2 * hb, :] = first[: 2 * hb, : 3 * hb]
        copies = None
    else:
        weights, (qkv, mixed, w, sem) = refs[:3], refs[3:]
        copies = Copies(sem)
        fetch_heads(g, at, copies, at.quarter(m), at.k, weights, w, 0)
        w[hb : 2 * hb, :] = first[m * hb : (m + 1) * hb, : 3 * hb]
    for j in range(1, g.zs):
        w[2 * hb * j : 2 * hb * (j + 1), :] = rest[j - 1, :, : 3 * hb]
    if copies is not None:
        copies.wait()
    qkv[...] = dot(normed[...], w[...]).astype(BF16)
    half = normed.shape[0] // 2
    for h in range(g.nh):
        bias = toeplitz(off[h : h + 1, :], half)
        for s in range(2):
            rows = slice(s * half, (s + 1) * half)
            q, kk, v = (qkv[rows, i * hb + h * hd : i * hb + (h + 1) * hd] for i in range(3))
            p = probabilities(q, kk, bias, both[s]).astype(BF16)
            mixed[rows, h * hd : (h + 1) * hd] = dot(p, v).astype(BF16)


def turned_head(g, at, block):
    return at.code(lax.bitwise_xor(block, at.r))


def mixer_kernel(g, *refs):
    rs, zs, hb = g.rs, g.zs, g.hb
    at = g.here()
    mixed_parts, own, rest = refs[:rs], refs[rs], refs[rs + 1 : 2 * rs + 1]
    mixed, wo, partial = refs[2 * rs + 1 :]
    for m in range(rs):
        mixed[:, m * hb : (m + 1) * hb] = mixed_parts[m][...]
    wo[lanes(turned_head(g, at, at.z), hb), :] = own[...]
    for m in range(rs):
        for j in range(1, zs):
            rows = lanes(turned_head(g, at, at.behind(j)), hb)
            piece = rest[m][j - 1, :, 3 * hb :]
            both = jnp.concatenate([piece[:hb], piece[hb:]], axis=1)
            wo[rows, lanes(at.quarter(m), 2 * hb)] = both
    partial[...] = dot(mixed[...], wo[...]).astype(BF16)


def middle_kernel(g, own, got, part, other, gain, *refs):
    sib = got.at[pl.ds(g.rs * g.hb + PAD, g.seq_len), :]
    middle, normed2, normed2_t, mine = refs[:4]
    plain = refs[4] if g.aligned else normed2
    half = own.shape[0]
    for s, src in ((0, own), (1, sib)):
        rows = slice(s * half, (s + 1) * half)
        swapped = slice((1 - s) * half, (2 - s) * half)
        v = src[...].astype(F32) + part[rows, :].astype(F32) + other[swapped, :].astype(F32)
        middle[rows, :] = v
        scale = lax.rsqrt(jnp.mean(v * v, axis=-1, keepdims=True) + EPSILON)
        plain[rows, :] = (v * scale * gain[...]).astype(BF16)
    if g.aligned:
        to_relative(g, g.here(), plain, normed2)
    normed2_t[...] = normed2[...].T
    mine[...] = normed2[:half, :]


def pair_swapped(g, value):
    if not g.aligned:
        return value
    hb = g.hb
    blocks = [value[:, e * hb : (e + 1) * hb] for e in range(2 * g.zs)]
    return jnp.concatenate([blocks[e ^ 1] for e in range(2 * g.zs)], axis=1)


def ffn_work(g, at, n2, n2_t, gl, w1s, w2s, done):
    out_sum, gn_sum = None, None
    for c in range(g.rs // 2):
        w1, w2 = w1s[c], w2s[c]
        h = dot(n2[...], w1[...])
        cdf = 0.5 * (1.0 + lax.erf(h * INV_SQRT2))
        pdf = jnp.exp(-0.5 * h * h) * INV_SQRT2PI
        act = (h * cdf).astype(BF16)
        ga = dot_nt(gl[...], w2[...])
        gh = (ga * (cdf + h * pdf)).astype(BF16)
        done(c, dot(n2_t[...], gh), dot_tn(act, gl[...]))
        out_part = dot(act, w2[...])
        gn_part = dot_nt(gh, w1[...])
        out_sum = out_part if out_sum is None else out_sum + out_part
        gn_sum = gn_part if gn_sum is None else gn_sum + gn_part
    return gn_sum, out_sum


def share_out(g, sums, own, swap):
    half = g.seq_len
    for i, total in enumerate(sums):
        own[i] = total[:half]
        swap[i] = total[half:].astype(BF16)


def ffn_own_kernel(g, n2, n2_t, gl_own, gl_sib, *refs):
    hb, sub, zs, cols = g.hb, g.sub, g.zs, g.cols
    at = g.here()
    half, n = g.seq_len, g.rs // 2
    pieces, refs = refs[: n * (zs - 1)], refs[n * (zs - 1) :]
    n_first = 2 if g.aligned else n
    firsts, refs = refs[:n_first], refs[n_first:]
    if g.aligned:
        wi, wu, refs = *refs[:2], refs[2:]
    gl, own, swap, go, refs = *refs[:4], refs[4:]
    grads, w1s, w2s, refs = refs[:n], refs[n : 2 * n], refs[2 * n : 3 * n], refs[3 * n :]
    copies = Copies(refs[0]) if g.aligned else None
    gl[:half, :] = gl_own[...]
    gl[half:, :] = gl_sib[...]

    def place_piece(piece, w1, w2, j):
        w1[2 * hb * j : 2 * hb * (j + 1), :] = piece[: 2 * hb, :]
        place = lanes(at.behind(j), sub)
        for b in range(g.parts):
            rows = slice(2 * hb + b * sub, 2 * hb + (b + 1) * sub)
            w2[place, b * cols : (b + 1) * cols] = piece[rows, :]

    for c in range(n):
        w1, w2 = w1s[c], w2s[c]
        if c and g.aligned:
            s = at.even(c)
            fetch_inner(g, at, copies, s, at.k, wi, w1, 0, 0)
            copies.start(wu.at[lanes(s, sub), :], w2.at[lanes(at.z, sub), :])
            w1[hb : 2 * hb, :] = firsts[-1][c * hb : (c + 1) * hb, 3 * hb : 3 * hb + cols]
        else:
            place_piece(firsts[c], w1, w2, 0)
        for j in range(1, zs):
            place_piece(pieces[c * (zs - 1) + j - 1], w1, w2, j)
    if copies is not None:
        copies.wait()

    def done(c, inner, outer):
        grads[c][...] = inner.astype(BF16).reshape(grads[c].shape)
        outer = outer.astype(BF16)
        for b in range(zs):
            place = lax.rem(at.z + (zs - b), zs)
            go[place, c * sub : (c + 1) * sub, :] = outer[b * sub : (b + 1) * sub, :]

    share_out(g, ffn_work(g, at, n2, n2_t, gl, w1s, w2s, done), own, swap)


def ffn_other_kernel(g, nx, nxk, gx, gxk, *refs):
    sub, zs, n, half = g.sub, g.zs, g.rs // 2, g.seq_len
    at = g.here()
    w1s, w2s, gi_in, refs = refs[:n], refs[n : 2 * n], refs[2 * n : 3 * n], refs[3 * n :]
    go_in, own, swap, refs = refs[0], refs[1], refs[2], refs[3:]
    grads, outs, (n2, n2_t, gl, go) = refs[:n], refs[n : n + zs], refs[n + zs :]
    n2[:half, :] = nx[...]
    n2[half:, :] = pair_swapped(g, nxk[...])
    n2_t[...] = n2[...].T
    gl[:half, :] = gx[...]
    gl[half:, :] = gxk[...]

    def done(c, inner, outer):
        shape = grads[c].shape
        grads[c][...] = (inner.reshape(shape) + gi_in[c][...].astype(F32)).astype(BF16)
        for b in range(zs):
            place = lax.rem(at.z + (zs - b), zs)
            rows = slice(c * sub, (c + 1) * sub)
            before = go_in[place, rows, :].astype(F32)
            go[place, rows, :] = (outer[b * sub : (b + 1) * sub, :] + before).astype(BF16)

    share_out(g, ffn_work(g, at, n2, n2_t, gl, w1s, w2s, done), own, swap)
    for j in range(zs):
        outs[j][...] = go[j]


def cross_sum_kernel(g, part, got, gn_out, outer_out):
    gn = part[0] + pair_swapped(g, got[0].astype(F32))
    gn_out[...] = gn.astype(BF16)
    outer_out[...] = (part[1] + got[1].astype(F32)).astype(BF16)


def own_sum_kernel(g, part, got, cross, out):
    total = part[0] + pair_swapped(g, got[0].astype(F32)) + cross[...].astype(F32)
    out[...] = total.astype(BF16)


def absolute_sum(g, at, part, other, rows, swapped, total):
    hb = g.hb
    if not g.aligned:
        total[...] = part[rows, :].astype(F32) + other[swapped, :].astype(F32)
        return
    for j in range(g.zs):
        for h in range(2):
            mine, theirs = 2 * j + h, 2 * j + 1 - h
            a = part[rows, mine * hb : (mine + 1) * hb].astype(F32)
            b = other[swapped, theirs * hb : (theirs + 1) * hb].astype(F32)
            total[:, lanes(at.shard(j, h), hb)] = a + b


def middle_back_kernel(g, own, other, middle, gl, gain, mixed, wo, *refs):
    grad_mid, gm, ggain, gwo, gatt, total = refs[:6]
    at, hb = g.here(), g.hb
    half, width = g.seq_len, g.width
    for s in range(2):
        rows = slice(s * half, (s + 1) * half)
        if g.aligned:
            for j in range(g.zs):
                for h in range(2):
                    e = 2 * j + (1 - h if s else h)
                    some = (other if s else own)[:, e * hb : (e + 1) * hb]
                    total[:, lanes(at.shard(j, h), hb)] = some.astype(F32)
        else:
            total[...] = (other if s else own)[...].astype(F32)
        gn = total[...]
        v = middle[rows, :]
        scale = lax.rsqrt(jnp.mean(v * v, axis=-1, keepdims=True) + EPSILON)
        gg = gn * gain[...]
        inner = jnp.sum(gg * v, axis=-1, keepdims=True) * (1.0 / width)
        grad = gl[rows, :].astype(F32) + scale * gg - v * (scale * scale * scale * inner)
        if s == 0:
            grad_mid[...] = grad
            sums = jnp.sum(gn * v * scale, axis=0, keepdims=True)
            if g.aligned:
                refs[6][...] = sums
                to_relative(g, at, refs[6], ggain)
            else:
                ggain[...] = sums
        gatt[rows, :] = grad.astype(BF16)
    gm[...] = dot_nt(gatt[...], wo[...]).astype(BF16)
    full = dot_tn(mixed[...], gatt[...]).astype(BF16)
    for m in range(g.rs):
        place = lax.rem(at.z + (g.zs - at.quarter(m)), g.zs)
        gwo[place] = full[m * hb : (m + 1) * hb, :]


def attn_back_kernel(g, m, step, lengths, normed_t, off, qkv, gmix, gwo, hot, scaled, w, *refs):
    hb, hd = g.hb, g.hd
    at = g.here()
    both = two_lengths(at, lengths)
    half = g.seq_len
    extra, refs = (refs[:1], refs[1:]) if m == 0 else ((), refs)
    before, refs = (refs[0], refs[1:]) if step else (None, refs)
    gw, *gn, gqkv = refs
    flip = (
        lax.broadcasted_iota(jnp.int32, (half, half), 0)
        + lax.broadcasted_iota(jnp.int32, (half, half), 1)
        == half - 1
    ).astype(BF16)
    table = []
    for h in range(g.nh):
        bias = toeplitz(off[h : h + 1, :], half)
        flipped = jnp.zeros((half, half), F32)
        for s in range(2):
            rows = slice(s * half, (s + 1) * half)
            q, kk, v = (qkv[rows, i * hb + h * hd : i * hb + (h + 1) * hd] for i in range(3))
            gm = gmix[rows, m * hb + h * hd : m * hb + (h + 1) * hd]
            p = probabilities(q, kk, bias, both[s])
            gp = dot_nt(gm, v)
            delta = jnp.sum(p * gp, axis=-1, keepdims=True)
            gs = (p * (gp - delta)).astype(BF16)
            flipped = flipped + dot(flip, gs)
            cols = [slice(i * hb + h * hd, i * hb + (h + 1) * hd) for i in range(3)]
            gqkv[rows, cols[0]] = dot(gs, kk).astype(BF16)
            gqkv[rows, cols[1]] = dot_tn(gs, q).astype(BF16)
            gqkv[rows, cols[2]] = dot_tn(p.astype(BF16), gm).astype(BF16)
        wide = jnp.concatenate([flipped, jnp.zeros((half, half), F32)], axis=1)
        skewed = pltpu.roll(wide, 0, 1, stride=1, stride_axis=0)
        diag = jnp.broadcast_to(jnp.sum(skewed, axis=0, keepdims=True), (8, 2 * half))
        top = diag.astype(BF16)
        table.append(dot_nt(top, hot[...]) + dot_nt((diag - top.astype(F32)).astype(BF16), hot[...]))
    gw[:, : 2 * hb, : 3 * hb] = (
        dot(normed_t[...], gqkv[...]).astype(BF16).reshape(g.zs, 2 * hb, 3 * hb)
    )
    row = lax.broadcasted_iota(jnp.int32, (PAD, hb), 0)
    buckets = jnp.zeros((PAD, hb), F32)
    for i, t in enumerate(table):
        buckets = jnp.where(row == 2 + i, jnp.broadcast_to(t[0:1], (PAD, hb)), buckets)
    for j in range(g.zs):
        piece = gwo[j, :, lanes(at.quarter(m), 2 * hb)]
        gw[j, :hb, 3 * hb :] = piece[:, :hb]
        gw[j, hb : 2 * hb, 3 * hb :] = piece[:, hb:]
        part = dot_nt(gqkv[...], w[2 * hb * j : 2 * hb * (j + 1), :])
        cols = slice(2 * hb * j, 2 * hb * (j + 1))
        gain = jnp.sum(part * scaled[:, cols].astype(F32), axis=0, keepdims=True)
        tile = [gain[:, :hb], gain[:, hb:]]
        tile = jnp.where(row == 0, tile[0], jnp.where(row == 1, tile[1], 0.0))
        gw[j, 2 * hb :, :hb] = tile.astype(BF16)
        if m == 0:
            tile = [extra[0][:, (2 * j + h) * hb : (2 * j + h + 1) * hb] for h in range(2)]
            tile = jnp.where(row == 0, tile[0], jnp.where(row == 1, tile[1], 0.0))
        else:
            tile = jnp.zeros((PAD, hb), F32)
        gw[j, 2 * hb :, hb : 2 * hb] = tile.astype(BF16)
        gw[j, 2 * hb :, 2 * hb : 3 * hb] = buckets.astype(BF16)
        gw[j, 2 * hb :, 3 * hb :] = jnp.zeros((PAD, hb), BF16)
        if before is not None:
            part = part + before[:, cols]
        if len(gn) == 1:
            gn[0][:, cols] = part
        else:
            gn[0][:, cols] = part[:half]
            gn[1][:, cols] = part[half:].astype(BF16)


def input_back_kernel(g, own, other, grad_mid, x, gain, out, total):
    everything = slice(None)
    absolute_sum(g, g.here(), own, other, everything, everything, total)
    gn = total[...]
    v = x[...].astype(F32)
    scale = lax.rsqrt(jnp.mean(v * v, axis=-1, keepdims=True) + EPSILON)
    gg = gn * gain[...]
    inner = jnp.mean(gg * v, axis=-1, keepdims=True)
    grad = grad_mid[...] + scale * gg - v * (scale * scale * scale * inner)
    out[...] = grad.astype(BF16)


def layer_kernel(g, lengths, middle, part, got, cross, out):
    half = g.seq_len
    row = lax.broadcasted_iota(jnp.int32, out.shape, 0)
    v = middle[:half, :] + part[1] + got[1].astype(F32) + cross[...].astype(F32)
    out[...] = jnp.where(row < lengths[g.here().me], v, 0.0).astype(BF16)


CORE, MIDDLE, SWAP, SWAP_X, NORMED, INNER, ATTN, COT, COT_SIB, COT_X, COT_XK, LAYER = range(12)
MINE_X, MINE_XK, GN_X, GN_K, OUTER_X = range(12, 17)
RING_A, RING_F, HOP_A, HOP_F, GI, GI_SUM, GH, GH_SUM, OA, LATE, SPREAD_F, SPREAD_T = range(17, 29)

ORDER = (
    0, 4, ((COT, 0), 1), 1, 5, (RING_A, 2), 6, 2, (RING_A, 3), ((COT, 2), 0), 3, 12, 13, 7, 15, 8,
    9, 14, 16, 10, (RING_F, 1), ((HOP_F, 1), 1), (RING_F, 3), 17, 18, ((HOP_F, 3), 1), 11, 19,
    (MINE_XK,), (RING_F, 2), (CORE,), 20, 21, 22, 30, 23, 25, 32, 31, 24, 35, 44, 26, (GH, 1), 46,
    27, 36, 33, 28, 43, 34, 37, 48, (GN_K,), 29, (LATE, 1), 45, (INNER,), (GH_SUM, 1),
    ((COT, 5), 1), 38, 49, (GI_SUM, 3), 47, 52, 39, (GI_SUM, 2), (GN_X,), ((LAYER, 0), 1), 50, 51,
    40, 54, (SPREAD_T, 1), 41, 53, 55, 42,
)


def solution(mesh):
    rs, ss = mesh.shape["rep"], mesh.shape["shard"]
    zs = ss // 2
    count = rs * ss
    nb = rs.bit_length() - 1

    def pairs(move):
        table = []
        for i in range(count):
            r, z, k = i // ss, (i % ss) // 2, i % 2
            r, z, k = move(r, z, k)
            table.append((i, (r * zs + z) * 2 + k))
        return table

    core_pairs = pairs(lambda r, z, k: (r, z, 1 - k))
    up_pairs = pairs(lambda r, z, k: (r, (z + 1) % zs, k))
    rep_pairs = [
        pairs(lambda r, z, k, b=b: (r ^ (1 << (nb - 1 - b if k else b)), z, k)) for b in range(nb)
    ]
    plain_pairs = [pairs(lambda r, z, k, b=b: (r ^ (1 << b), z, k)) for b in range(nb)]
    z_pairs = {m: pairs(lambda r, z, k, m=m: (r, z ^ m, k)) for m in range(1, zs)}

    def send(value, table):
        return lax.ppermute(value, AXES, table)

    by_size = sorted(range(1, rs), key=lambda m: (bin(m).count("1"), m))

    def high(m):
        return m.bit_length() - 1

    def low(m):
        return (m & -m).bit_length() - 1

    def local(
        inputs,
        cotangent,
        seq_lengths,
        dealing,
        rel_buckets,
        w_query,
        w_key,
        w_value,
        w_mixer,
        w_inner,
        w_outer,
        gain_attn,
        gain_mlp,
        bias_table,
    ):
        seq = Sequence()
        bind = functools.partial
        n_buckets, heads = bias_table.shape[0] * ss, bias_table.shape[1]
        g = Geometry(rs, zs, w_query.shape[0], w_outer.shape[0], heads, *inputs.shape[1:])
        hb, fb, sub, cols, nh = g.hb, g.fb, g.sub, g.cols, g.nh
        seq_len, width, tokens = g.seq_len, g.width, g.tokens
        chips, rows = g.chips, g.rows
        chunks = rs // 2

        r, c = lax.axis_index("rep"), lax.axis_index("shard")
        z, k = c // 2, c % 2
        shards = jnp.arange(ss, dtype=jnp.int32)
        x_own = inputs[0]
        d = Box()
        parts = {}

        def relative():
            return 2 * ((z + zs - shards // 2) % zs) + (k ^ (shards % 2))

        def permute_cols(x, order):
            return jnp.take(x.reshape(-1, ss, hb), order, axis=1).reshape(x.shape)

        val = {}
        steps = []

        def put(name, value, table):
            val[name] = send(value, table)

        def step(run, *args):
            steps.append(bind(run, *args))

        labels = [(f, zz) for f in range(rs) for zz in range(zs)]

        def groups_of(stage):
            if stage == nb:
                return [[e for e in labels if e[1] == zz] for zz in range(zs)]
            clear = [e for e in labels if not (e[0] >> stage) & 1]
            return [clear, [e for e in labels if e not in clear]]

        def block_shapes(groups):
            outs = [shaped((len(some), rows, width)) for some in groups]
            return outs if len(outs) == 1 else [stored(outs[0].shape)] + outs[1:]

        def dispatch(key, outs, stage):
            groups = groups_of(stage)
            val[key] = outs[0]
            state = [(key, groups[0])]
            for i, (out, some) in enumerate(zip(outs[1:], groups[1:])):
                put((key, i), out, z_pairs[i + 1] if stage == nb else rep_pairs[stage])
                state.append(((key, i), some))
            return state

        def places(state, some):
            at = {e: (a, b) for a, (_, named) in enumerate(state) for b, e in enumerate(named)}
            return [at[e] for e in some]

        def values(state):
            return [val[name] for name, _ in state]

        def deal_first(what, stage):
            groups = groups_of(stage)
            value = parts[what].reshape(chips, rows, width)
            outs = seq(bind(deal_first_kernel, g, groups), block_shapes(groups), value)
            parts[what] = dispatch((what, 0), outs, stage)

        def deal_stage(what, number, stage):
            groups, state = groups_of(stage), parts[what]
            body = bind(deal_stage_kernel, [places(state, some) for some in groups], len(state))
            outs = seq(body, block_shapes(groups), *values(state))
            parts[what] = dispatch((what, number), outs, stage)

        def deal_core(what):
            state = parts[what]
            body = bind(deal_stage_kernel, [places(state, labels)], len(state))
            parts[what] = seq(body, block_shapes([labels]), *values(state))[0]
            put((what, CORE), parts[what], core_pairs)

        def deal_middle(what, number, stage, back):
            groups = groups_of(stage)
            body = bind(deal_middle_kernel, g, groups, back)
            lookup = [pltpu.SMEM((count,), jnp.int32)]
            args = dealing, parts[what], val[what, CORE]
            outs = seq(body, block_shapes(groups), *args, scalars=1, scratch=lookup)
            parts[what] = dispatch((what, number), outs, stage)

        def deal_last(what, masked):
            state = parts[what]
            body = bind(deal_last_kernel, g, places(state, labels), len(state), masked)
            pool = [pltpu.VMEM((chips, rows, width), BF16)]
            shape = [shaped((chips, rows, width))]
            out = seq(body, shape, seq_lengths, *values(state), scalars=1, scratch=pool)[0]
            parts[what] = out.reshape(seq_len, width)

        def deal(what, first, second, back, end):
            step(deal_first, what, first[0])
            for i, stage in list(enumerate(first))[1:]:
                step(deal_stage, what, i, stage)
            step(deal_core, what)
            n = len(first)
            step(deal_middle, what, n, second[0], back)
            for i, stage in list(enumerate(second))[1:]:
                step(deal_stage, what, n + i, stage)
            step(end)

        copy_sem = pltpu.SemaphoreType.DMA(())

        def slices(m, core):
            s = r ^ (m + core * (g.turned(m) - m))
            at = (2 * s + core) * hb
            parts = [lax.dynamic_slice(w, (0, at), (hb, hb)) for w in (w_query, w_key, w_value)]
            return parts, lax.dynamic_slice(w_mixer, (0, s * 2 * hb), (hb, 2 * hb))

        def inner_slices(c, core):
            s = r ^ (2 * c)
            at = [(2 * b + core) * fb + s * sub for b in range(zs)]
            inner = [lax.dynamic_slice(w_inner, (0, a), (hb, sub)) for a in at]
            outer = lax.dynamic_slice(w_outer, (s * sub, 0), (sub, width))
            return inner, [outer[:, i * cols : (i + 1) * cols] for i in range(g.parts)]

        small_args = gain_attn.reshape(1, hb), gain_mlp.reshape(1, hb), bias_table

        def start_core():
            if g.aligned:
                sent = seq(
                    bind(send_prep_kernel, g),
                    [shaped((rs * hb + PAD + seq_len, width))],
                    *small_args,
                    w_query,
                    w_key,
                    w_value,
                    w_inner,
                    x_own,
                    hbm=5,
                    scratch=[copy_sem],
                )[0]
            else:
                sent = []
                for m in range(rs):
                    parts = slices(m, 1 - k)[0]
                    inner = inner_slices(m % (rs // 2), 1 - k)[0]
                    sent.append(jnp.concatenate(parts + inner, axis=1))
                sent = jnp.concatenate(sent + [small_rows()], axis=0)
                sent = jnp.pad(sent, ((0, 0), (0, width - sent.shape[1])))
                sent = jnp.concatenate([sent, x_own], axis=0)
            put(CORE, sent, core_pairs)

        def small_rows():
            tile = jnp.zeros((PAD, 3 * hb + cols), BF16)
            tile = tile.at[0, :hb].set(gain_attn).at[0, hb : 2 * hb].set(gain_mlp)
            n = bias_table.shape[0]
            return tile.at[8 : 8 + n, 2 * hb : 2 * hb + heads].set(bias_table)

        def start_attn():
            got = val[CORE]
            if g.aligned:
                own = seq(
                    bind(attn_prep_kernel, g),
                    [shaped((2 * hb + PAD, 4 * hb))],
                    *small_args,
                    got,
                    w_query,
                    w_key,
                    w_value,
                    w_mixer,
                    hbm=4,
                    scratch=[pltpu.VMEM((PAD, 4 * hb), BF16), copy_sem],
                )
            else:
                own = []
                for m in range(rs):
                    parts, mix = slices(m, k)
                    top = jnp.concatenate(parts + [mix[:, :hb]], axis=1)
                    bottom = [got[m * hb : (m + 1) * hb, : 3 * hb], mix[:, hb:]]
                    own.append(jnp.concatenate([top, jnp.concatenate(bottom, axis=1)], axis=0))
                mine = small_rows()[:, : 4 * hb]
                theirs = got[rs * hb : rs * hb + PAD, : 4 * hb]
                both = [mine[:1], theirs[:1], mine[2:12], theirs[8:12]]
                both = jnp.concatenate(both, axis=0)
                own[0] = jnp.concatenate([own[0], both], axis=0)
            d.attn_own = own
            ring(RING_A, own[0])

        def start_ffn():
            got = val[CORE]
            if g.aligned:
                own = seq(
                    bind(ffn_prep_kernel, g),
                    [shaped((4 * hb, cols))],
                    got,
                    w_inner,
                    w_outer,
                    hbm=2,
                    scratch=[copy_sem],
                )
            else:
                own = []
                for c in range(rs // 2):
                    top, below = inner_slices(c, k)
                    bottom = got[c * hb : (c + 1) * hb, 3 * hb : 3 * hb + cols]
                    own.append(
                        jnp.concatenate([jnp.concatenate(top, axis=1), bottom] + below, axis=0)
                    )
            d.ffn_own = own
            ring(RING_F, own[0])
            for j in range(1, zs):
                even_hops((HOP_F, j), val[RING_F, j])

        def ring(name, value):
            for j in range(1, zs):
                put((name, j), value if j == 1 else val[name, j - 1], up_pairs)

        def hops(name, value):
            val[name, 0] = value
            for m in by_size:
                put((name, m), val[name, m ^ (1 << high(m))], rep_pairs[high(m)])

        def even_hops(name, value):
            val[name, 0] = value
            for c in range(1, rs // 2):
                b = high(c)
                put((name, c), val[name, c ^ (1 << b)], plain_pairs[b + 1])

        def stack_attn():
            pieces = [val[RING_A, j] for j in range(1, zs)]
            shape = [shaped((zs - 1, 2 * hb, 4 * hb))]
            hops(HOP_A, seq(bind(stack_kernel, 2 * hb), shape, *pieces)[0])

        def small_params():
            pieces = [d.attn_own[0]] + [val[RING_A, j] for j in range(1, zs)]
            tiles = jnp.stack([piece[2 * hb :, :] for piece in pieces])
            order = (shards[:, None] == relative()[None, :]).astype(BF16)
            gains = dot(order, tiles[:, :2, : 2 * hb].reshape(ss, 2 * hb))
            d.gain_a = gains[:, :hb].reshape(1, width)
            d.gain_m = gains[:, hb:].reshape(1, width)
            n = n_buckets // ss
            table = tiles[:, 8:, 2 * hb : 2 * hb + heads].reshape(ss, 4, heads)[:, :n]
            table = dot(order, table.reshape(ss, n * heads)).reshape(n_buckets, heads)
            quarters = jnp.arange(rs, dtype=jnp.int32)
            quarters = r ^ (quarters + k * (g.turned(quarters) - quarters))
            head_ids = ((2 * quarters + k) * nh)[:, None] + jnp.arange(nh, dtype=jnp.int32)[None]
            pick = jnp.arange(heads, dtype=jnp.int32)[:, None] == head_ids.reshape(1, -1)
            padded = jnp.concatenate([rel_buckets, jnp.full((1,), -1, jnp.int32)])
            hot = padded[None, :] == jnp.arange(hb, dtype=jnp.int32)[:, None]
            d.hot = hot.astype(BF16)
            my_table = dot(table.astype(BF16), pick.astype(BF16)).astype(BF16)
            d.offsets = lax.dot_general(
                my_table,
                d.hot[:n_buckets],
                (((0,), (0,)), ((), ())),
                preferred_element_type=F32,
            ).reshape(rs, nh, 2 * seq_len)

        spare = [pltpu.VMEM((tokens, width), BF16)] if g.aligned else []

        def norm():
            small_params()
            normed, normed_t, scaled = seq(
                bind(norm_kernel, g),
                [shaped((tokens, width)), stored((width, tokens)), stored((tokens, width))],
                x_own,
                val[CORE],
                d.gain_a,
                scratch=spare * 2,
            )
            if not g.aligned:
                normed = permute_cols(normed, relative())
                scaled = permute_cols(scaled, relative())
                normed_t = normed.T
            d.normed, d.normed_t, d.scaled = normed, normed_t, scaled
            d.qkv, d.mixed_parts, d.attn_w = ([None] * rs for _ in range(3))

        def attend(m):
            own = m == 0 or not g.aligned
            weights = () if own else (w_query, w_key, w_value)
            d.qkv[m], d.mixed_parts[m], d.attn_w[m] = seq(
                bind(attn_kernel, g, m),
                [stored((tokens, 3 * hb)), stored((tokens, hb)), stored((width, 3 * hb))],
                seq_lengths,
                d.normed,
                d.offsets[m],
                d.attn_own[m] if own else val[CORE],
                val[HOP_A, m],
                *weights,
                scalars=1,
                hbm=len(weights),
                scratch=() if own else [copy_sem],
            )

        def mixer():
            d.mixed, d.wo, d.partial = seq(
                bind(mixer_kernel, g),
                [stored((tokens, rs * hb)), stored((rs * hb, width)), shaped((tokens, width))],
                *d.mixed_parts,
                w_mixer,
                *[val[HOP_A, m] for m in range(rs)],
            )
            put(MIDDLE, d.partial, core_pairs)

        def middle():
            d.middle, normed2, normed2_t, mine = seq(
                bind(middle_kernel, g),
                [
                    stored((tokens, width), F32),
                    shaped((tokens, width)),
                    shaped((width, tokens)),
                    shaped((seq_len, width)),
                ],
                x_own,
                val[CORE],
                d.partial,
                val[MIDDLE],
                d.gain_m,
                scratch=spare,
            )
            if not g.aligned:
                normed2 = permute_cols(normed2, relative())
                normed2_t, mine = normed2.T, normed2[:seq_len]
            put(MINE_X, mine, plain_pairs[0])
            put(MINE_XK, val[MINE_X], core_pairs)
            d.normed2, d.normed2_t = normed2, normed2_t

        sums = [shaped((2, seq_len, width), F32), shaped((2, seq_len, width))]
        weights_made = [shaped((width, cols))] * chunks + [shaped((cols, width))] * chunks

        def ffn_own():
            firsts = [d.ffn_own[0], val[CORE]] if g.aligned else d.ffn_own
            weights = (w_inner, w_outer) if g.aligned else ()
            outs = seq(
                bind(ffn_own_kernel, g),
                [shaped((tokens, width))]
                + sums
                + [shaped((zs, chunks * sub, width))]
                + [shaped((zs, 2 * hb, cols))] * chunks
                + weights_made,
                d.normed2,
                d.normed2_t,
                parts[COT],
                val[COT_SIB],
                *[val[(HOP_F, j), c] for c in range(chunks) for j in range(1, zs)],
                *firsts,
                *weights,
                hbm=len(weights),
                scratch=[copy_sem] if g.aligned else (),
                limit=24,
            )
            d.gl, d.ffn_part, swap, d.go = outs[:4]
            d.gi, d.weights = outs[4 : 4 + chunks], outs[4 + chunks :]
            put(SWAP, to_absolute(swap), core_pairs)

        def to_absolute(swap):
            if g.aligned:
                return swap
            return jnp.stack([permute_cols(swap[0], jnp.argsort(relative())), swap[1]])

        def ffn_other():
            nxk = val[MINE_XK]
            if not g.aligned:
                nxk = permute_cols(nxk, shards ^ 1)
            outs = seq(
                bind(ffn_other_kernel, g),
                sums + [shaped((zs, 2 * hb, cols))] * chunks + [shaped((chunks * sub, width))] * zs,
                val[MINE_X],
                nxk,
                val[COT_X],
                val[COT_XK],
                *d.weights,
                *d.gi,
                d.go,
                scratch=[
                    pltpu.VMEM((tokens, width), BF16),
                    pltpu.VMEM((width, tokens), BF16),
                    pltpu.VMEM((tokens, width), BF16),
                    pltpu.VMEM((zs, chunks * sub, width), BF16),
                ],
                limit=24,
            )
            d.cross_part, swap = outs[:2]
            parts[GI] = list(outs[2 : 2 + chunks])
            parts[OA] = outs[2 + chunks :]
            put(SWAP_X, to_absolute(swap), core_pairs)
            for c in range(1, chunks):
                if c % 2:
                    put((GI, c), parts[GI][c], plain_pairs[1])
            put((OA, 1), parts[OA][1], up_pairs)

        def cross_sum():
            part = d.cross_part
            if not g.aligned:
                part = jnp.stack([permute_cols(part[0], jnp.argsort(relative())), part[1]])
            gn, outer = seq(
                bind(cross_sum_kernel, g), [shaped((seq_len, width))] * 2, part, val[SWAP_X]
            )
            put(GN_X, gn, plain_pairs[0])
            put(OUTER_X, outer, plain_pairs[0])

        def own_sum():
            part = d.ffn_part
            if not g.aligned:
                part = jnp.stack([permute_cols(part[0], jnp.argsort(relative())), part[1]])
            shape = [shaped((seq_len, width))]
            d.gn2 = seq(bind(own_sum_kernel, g), shape, part, val[SWAP], val[GN_X])[0]
            put(GN_K, d.gn2, core_pairs)

        def add(*terms):
            shape = [shaped(terms[0].shape)]
            return seq(bind(sum_kernel, [None] * len(terms)), shape, *terms)[0]

        def sum_step(name, j):
            put((name, j), add(val[name, j - 1], parts[name][j]), up_pairs)

        def hop_start(name, m):
            put((name, m), parts[name][m], rep_pairs[low(m)])

        def inner_add(c):
            some = parts[GI]
            above = [c | 1 << b for b in range(nb - 1) if not (c >> b) & 1 and low(c | 1 << b) == b]
            terms = [some[c]] + [val[GI, i] for i in above]
            if c:
                some[c] = add(*terms)
                put((GI, c), some[c], plain_pairs[low(c) + 1])
            else:
                shape = [shaped(some[0].shape[1:])] * zs
                parts[GI_SUM] = seq(bind(cut_sum_kernel, g), shape, *terms)
                put((GI_SUM, 1), parts[GI_SUM][1], up_pairs)

        def hop_add(name, ring, m):
            some = parts[name]
            bits = [b for b in range(nb) if not (m >> b) & 1 and low(m | 1 << b) == b]
            terms = [some[m]] + [val[name, m | 1 << b] for b in bits]
            if m:
                some[m] = add(*terms)
                hop_start(name, m)
            else:
                shape = [shaped(some[0].shape[1:])] * zs
                parts[ring] = seq(bind(cut_sum_kernel, g), shape, *terms)
                put((ring, 1), parts[ring][1], up_pairs)

        def outer_end():
            shape = [shaped((sub, width))] * chunks
            some = list(seq(bind(outer_end_kernel, g), shape, parts[OA][0], val[OA, zs - 1]))
            names = []
            for c in range(chunks - 1, 0, -1):
                b = low(c)
                put((LATE, c), some[c], plain_pairs[b + 1])
                if c ^ (1 << b):
                    some[c ^ (1 << b)] = add(some[c ^ (1 << b)], val[LATE, c])
                else:
                    names.append((LATE, c))
            d.late, d.late_names = some, names

        def inner_split():
            keep, give = seq(
                bind(inner_split_kernel, g),
                [shaped((hb, cols))] * 2,
                parts[GI_SUM][0],
                val[GI_SUM, zs - 1],
            )
            d.inner_keep = keep
            put(INNER, give, core_pairs)

        def spread(name, value):
            val[name, 0] = value
            put((name, 1), value, rep_pairs[0])

        def spread_next(name):
            for b in range(1, nb):
                some = [val[name, i] for i in range(b + 1)]
                shape = [shaped((1 << b, *some[0].shape))]
                put((name, b + 1), seq(spread_pack_kernel, shape, *some)[0], rep_pairs[b])

        def ffn_pack():
            late = [d.late[0]] + [val[name] for name in d.late_names]
            shape = [shaped((hb + sub, width))]
            body = bind(ffn_pack_kernel, g)
            spread(SPREAD_F, seq(body, shape, d.inner_keep, val[INNER], *late)[0])

        def ffn_end():
            shape = (hb, 2 * zs * fb) if g.aligned else (rs, hb, 2 * zs * sub)
            inner, d.sum_out = seq(
                bind(ffn_end_kernel, g),
                [stored(shape, F32), stored((fb, width), F32)],
                *[val[SPREAD_F, i] for i in range(nb + 1)],
            )
            if not g.aligned:
                inner = jnp.transpose(inner.reshape(rs, hb, 2 * zs, sub), (1, 2, 0, 3))
                inner = inner.reshape(hb, -1)
            d.sum_in = inner

        def attn_split():
            d.attn_keep, d.mixer_keep, give = seq(
                bind(attn_split_kernel, g),
                [
                    shaped((hb + PAD, 3 * hb)),
                    shaped((hb, 2 * hb)),
                    shaped((hb + PAD, 3 * hb)),
                ],
                parts[GH_SUM][0],
                val[GH_SUM, zs - 1],
            )
            put(ATTN, give, core_pairs)

        def attn_pack():
            shape = [shaped((hb + PAD, 8 * hb))]
            args = d.attn_keep, d.mixer_keep, val[ATTN]
            spread(SPREAD_T, seq(bind(attn_pack_kernel, g), shape, *args)[0])

        def attn_end():
            *d.sum_attn, d.gains, d.table = seq(
                bind(attn_end_kernel, g),
                [stored((hb, width), F32)] * 4 + [shaped((8, hb), F32), shaped((heads, hb), F32)],
                *[val[SPREAD_T, i] for i in range(nb + 1)],
            )

        def middle_back():
            more = [pltpu.VMEM((1, width), F32)] if g.aligned else []
            d.grad_mid, d.gmix, ggain, d.grad_wo = seq(
                bind(middle_back_kernel, g),
                [
                    stored((seq_len, width), F32),
                    shaped((tokens, rs * hb)),
                    shaped((1, width), F32),
                    shaped((zs, hb, width)),
                ],
                d.gn2,
                val[GN_K],
                d.middle,
                d.gl,
                d.gain_m,
                d.mixed,
                d.wo,
                scratch=[pltpu.VMEM((tokens, width), BF16), pltpu.VMEM((seq_len, width), F32)]
                + more,
            )
            d.ggain_m = ggain if g.aligned else permute_cols(ggain, relative())
            parts[GH] = [None] * rs

        def attend_back(m, turn):
            if turn == rs - 1:
                outs = [shaped((seq_len, width), F32), shaped((seq_len, width))]
            else:
                outs = [shaped((tokens, width), F32)]
            outs = seq(
                bind(attn_back_kernel, g, m, turn),
                [shaped((zs, 2 * hb + PAD, 4 * hb))] + outs,
                seq_lengths,
                d.normed_t,
                d.offsets[m],
                d.qkv[m],
                d.gmix,
                d.grad_wo,
                d.hot,
                d.scaled,
                d.attn_w[m],
                *([d.ggain_m] if m == 0 else []),
                *([d.gn] if turn else []),
                scalars=1,
                scratch=[pltpu.VMEM((tokens, 3 * hb), BF16)],
            )
            parts[GH][m] = outs[0]
            if m % 2:
                hop_start(GH, m)
            if turn < rs - 1:
                d.gn = outs[1]
            else:
                own, sib = outs[1:]
                if not g.aligned:
                    back_to = jnp.argsort(relative())
                    own, sib = permute_cols(own, back_to), permute_cols(sib, back_to)
                d.gn = own
                put(NORMED, sib, core_pairs)

        def input_back():
            d.input_grad = seq(
                bind(input_back_kernel, g),
                [stored((seq_len, width))],
                d.gn,
                val[NORMED],
                d.grad_mid,
                x_own,
                d.gain_a,
                scratch=[pltpu.VMEM((seq_len, width), F32)],
            )[0]

        def layer_out():
            parts[LAYER] = seq(
                bind(layer_kernel, g),
                [shaped((seq_len, width))],
                seq_lengths,
                d.middle,
                d.ffn_part,
                val[SWAP],
                val[OUTER_X],
                scalars=1,
            )[0]

        def cot_end():
            deal_last(COT, True)
            put(COT_SIB, parts[COT], core_pairs)
            put(COT_X, parts[COT], plain_pairs[0])
            put(COT_XK, val[COT_X], core_pairs)

        parts[COT] = cotangent[0]
        bits = list(range(nb))
        step(start_core)
        step(start_attn)
        step(start_ffn)
        step(stack_attn)
        deal(COT, [nb] + bits, bits + [nb], True, cot_end)
        step(norm)
        for m in range(rs):
            step(attend, m)
        step(mixer)
        step(middle)
        step(ffn_own)
        step(ffn_other)
        step(cross_sum)
        step(own_sum)
        step(middle_back)
        step(layer_out)
        back_order = [m for m in range(1, rs, 2)] + [m for m in range(rs - 2, -1, -2)]
        for turn, m in enumerate(back_order):
            step(attend_back, m, turn)
        step(input_back)
        for j in range(2, zs):
            step(sum_step, OA, j)
        for i in range(chunks - 2, -1, -2):
            step(inner_add, i)
        for m in range(rs - 2, -1, -2):
            step(hop_add, GH, GH_SUM, m)
        deal(LAYER, [nb] + bits, bits + [nb], False, bind(deal_last, LAYER, False))
        step(outer_end)
        for j in range(2, zs):
            step(sum_step, GI_SUM, j)
            step(sum_step, GH_SUM, j)
        step(inner_split)
        step(ffn_pack)
        step(attn_split)
        step(attn_pack)
        step(spread_next, SPREAD_F)
        step(spread_next, SPREAD_T)
        step(ffn_end)
        step(attn_end)
        for item in ORDER if (rs, zs) == (4, 4) else range(len(steps)):
            if isinstance(item, int):
                steps[item]()
            else:
                seq.arrived(val[item if len(item) > 1 else item[0]])

        gains, table = d.gains, d.table[:, :n_buckets].T
        sum_tab = lax.dynamic_slice(table, (c * (n_buckets // ss), 0), (n_buckets // ss, heads))
        return (
            parts[LAYER][None],
            d.input_grad[None],
            *d.sum_attn,
            d.sum_in,
            d.sum_out,
            gains[0],
            gains[1],
            sum_tab,
        )

    tokens_spec = P(AXES, None, None)
    rows_spec, part_spec = P("shard", None), P("shard")
    in_specs = (
        (tokens_spec,) * 2 + (P(),) * 3 + (rows_spec,) * 6 + (part_spec,) * 2 + (rows_spec,)
    )
    out_specs = (tokens_spec,) * 2 + (rows_spec,) * 6 + (part_spec,) * 2 + (rows_spec,)
    return jax.shard_map(local, mesh=mesh, in_specs=in_specs, out_specs=out_specs, check_vma=False)
```

```python
import functools

import jax
import jax.numpy as jnp
from jax import lax
from jax.experimental import pallas as pl
from jax.experimental.pallas import tpu as pltpu
from jax.sharding import PartitionSpec as P

EPSILON = 1e-06
MASKED = -1000000000.0
AXES = ("rep", "shard")
BF16 = jnp.bfloat16
F32 = jnp.float32
INV_SQRT2 = 0.7071067811865476
INV_SQRT2PI = 0.3989422804014327
PAD = 16

VMEM = pl.BlockSpec(memory_space=pltpu.VMEM)
SMEM = pl.BlockSpec(memory_space=pltpu.SMEM)
ANY = pl.BlockSpec(memory_space=pl.ANY)
HBM = pl.BlockSpec(memory_space=pltpu.HBM)


def shaped(shape, dtype=BF16):
    return jax.ShapeDtypeStruct(shape, dtype)


def kept(shape, dtype=BF16):
    return pltpu.VMEM(shape, dtype)


def stored(shape, dtype=BF16):
    return pltpu.HBM(shape, dtype)


class Sequence:
    def __init__(self):
        self.last = None

    def __call__(self, body, outs, *args, scalars=0, hbm=0, scratch=(), limit=12, after=()):
        n = len(args)
        args = [pltpu.with_memory_space_constraint(a, pltpu.HBM) if i >= n - hbm else a for i, a in enumerate(args)]
        specs = [SMEM] * scalars + [VMEM] * (n - scalars - hbm) + [HBM] * hbm
        extra = list(after) + ([] if self.last is None else [self.last])
        m = len(extra)

        def run(*refs):
            body(*refs[:n], *refs[n + m :])

        result = pl.pallas_call(
            run,
            out_shape=outs,
            in_specs=specs + [ANY] * m,
            out_specs=[VMEM] * len(outs),
            scratch_shapes=list(scratch),
            cost_estimate=pl.CostEstimate(flops=0, bytes_accessed=0, transcendentals=0),
            compiler_params=pltpu.CompilerParams(vmem_limit_bytes=limit * 1024 * 1024),
        )(*args, *extra)
        self.last = result[-1]
        return result

    def arrived(self, value):
        self(token_kernel, [kept((8, 128), F32)], after=[value], limit=4)


def dot(a, b):
    return jnp.dot(a, b, preferred_element_type=F32)


def dot_nt(a, b):
    return lax.dot_general(a, b, (((1,), (1,)), ((), ())), preferred_element_type=F32)


def dot_tn(a, b):
    return lax.dot_general(a, b, (((0,), (0,)), ((), ())), preferred_element_type=F32)


def lanes(block, size):
    return pl.ds(pl.multiple_of(block * size, size), size)


class Geometry:
    def __init__(self, rs, zs, hb, fb, heads, seq_len, width):
        self.rs, self.zs, self.hb, self.fb = rs, zs, hb, fb
        self.seq_len, self.width = seq_len, width
        self.tokens = 2 * seq_len
        self.bits = rs.bit_length() - 1
        self.sub = fb // rs
        self.cols = zs * self.sub
        self.hd = width // heads
        self.nh = hb // self.hd
        self.chips = rs * zs
        self.rows = seq_len // self.chips
        self.aligned = hb % 128 == 0 and self.sub % 128 == 0
        self.parts = width // self.cols

    def turned(self, m):
        out = 0
        for b in range(self.bits):
            out = out + (((m >> b) & 1) << (self.bits - 1 - b))
        return out

    def here(self):
        return Here(self)


class Here:
    def __init__(self, g):
        self.g = g
        self.r = lax.axis_index("rep").astype(jnp.int32)
        c = lax.axis_index("shard").astype(jnp.int32)
        self.z = lax.div(c, jnp.int32(2))
        self.k = lax.rem(c, jnp.int32(2))
        self.me = self.r * (2 * g.zs) + c

    def code(self, m, k=None):
        k = self.k if k is None else k
        return m + k * (self.g.turned(m) - m)

    def quarter(self, m):
        return self.r if m == 0 else lax.bitwise_xor(self.r, self.code(jnp.int32(m)))

    def even(self, c):
        return self.r if c == 0 else lax.bitwise_xor(self.r, jnp.int32(2 * c))

    def behind(self, j):
        return self.z if j == 0 else lax.rem(self.z + (self.g.zs - j), jnp.int32(self.g.zs))

    def shard(self, j, h):
        return 2 * self.behind(j) + (1 - self.k if h else self.k)


class Box:
    pass


class Copies:
    def __init__(self, sem):
        self.sem, self.all = sem, []

    def start(self, src, dst):
        copy = pltpu.make_async_copy(src, dst, self.sem)
        copy.start()
        self.all.append(copy)

    def wait(self):
        for copy in self.all:
            copy.wait()


def fetch_heads(g, at, copies, s, core, weights, dst, row):
    hb = g.hb
    for i, w in enumerate(weights):
        part = dst.at[pl.ds(row, hb), pl.ds(i * hb, hb)]
        copies.start(w.at[:, lanes(2 * s + core, hb)], part)


def fetch_inner(g, at, copies, s, core, wi, dst, row, col):
    hb, sub = g.hb, g.sub
    for b in range(g.zs):
        place = pl.ds(pl.multiple_of((2 * b + core) * g.fb + s * sub, sub), sub)
        copies.start(wi.at[:, place], dst.at[pl.ds(row, hb), pl.ds(col + b * sub, sub)])


def small_tile(g, gain_a, gain_m, table, out):
    hb = g.hb
    zero = jnp.zeros((PAD, hb), F32)
    row = lax.broadcasted_iota(jnp.int32, (PAD, hb), 0)
    for i, gain in enumerate((gain_a, gain_m)):
        tile = jnp.where(row == 0, jnp.broadcast_to(gain[...].astype(F32), (PAD, hb)), zero)
        out[:, i * hb : (i + 1) * hb] = tile.astype(BF16)
    out[:, 2 * hb :] = jnp.zeros((PAD, out.shape[1] - 2 * hb), BF16)
    n, heads = table.shape
    values = table[...].astype(F32)
    row = lax.broadcasted_iota(jnp.int32, (PAD, heads), 0)
    tile = jnp.zeros((PAD, heads), F32)
    for i in range(n):
        tile = jnp.where(row == 8 + i, jnp.broadcast_to(values[i : i + 1], (PAD, heads)), tile)
    out[:, 2 * hb : 2 * hb + heads] = tile.astype(BF16)


def send_prep_kernel(g, gain_a, gain_m, table, wq, wk, wv, wi, x, out, sem):
    at, hb = g.here(), g.hb
    copies, other = Copies(sem), 1 - at.k
    copies.start(x, out.at[pl.ds(g.rs * hb + PAD, g.seq_len), :])
    small_tile(g, gain_a, gain_m, table, out.at[pl.ds(g.rs * hb, PAD), :])
    for m in range(g.rs):
        s = lax.bitwise_xor(at.r, at.code(jnp.int32(m), other))
        fetch_heads(g, at, copies, s, other, (wq, wk, wv), out, m * hb)
    for c in range(g.rs // 2):
        fetch_inner(g, at, copies, at.even(c), other, wi, out, c * hb, 3 * hb)
    copies.wait()


def attn_prep_kernel(g, gain_a, gain_m, table, got, wq, wk, wv, wm, out, mine, sem):
    at, hb = g.here(), g.hb
    copies = Copies(sem)
    fetch_heads(g, at, copies, at.r, at.k, (wq, wk, wv), out, 0)
    for h in range(2):
        part = out.at[pl.ds(h * hb, hb), pl.ds(3 * hb, hb)]
        copies.start(wm.at[:, lanes(2 * at.r + h, hb)], part)
    out[hb : 2 * hb, : 3 * hb] = got[:hb, : 3 * hb]
    small_tile(g, gain_a, gain_m, table, mine)
    row = lax.broadcasted_iota(jnp.int32, (PAD, 4 * hb), 0)
    theirs = got[g.rs * hb : g.rs * hb + PAD, : 4 * hb].astype(F32)
    theirs = jnp.where(row < 8, pltpu.roll(theirs, 1, 0), pltpu.roll(theirs, 4, 0))
    ours = mine[...].astype(F32)
    both = jnp.where((row == 1) | (row >= 12), theirs, ours)
    out[2 * hb :, :] = both.astype(BF16)
    copies.wait()


def ffn_prep_kernel(g, got, wi, wu, out, sem):
    at, hb, sub, cols = g.here(), g.hb, g.sub, g.cols
    copies = Copies(sem)
    fetch_inner(g, at, copies, at.r, at.k, wi, out, 0, 0)
    for i in range(g.parts):
        part = out.at[pl.ds(2 * hb + i * sub, sub), :]
        copies.start(wu.at[lanes(at.r, sub), pl.ds(i * cols, cols)], part)
    out[hb : 2 * hb, :] = got[:hb, 3 * hb : 3 * hb + cols]
    copies.wait()


def spread_pack_kernel(*refs):
    *ins, out = refs
    for i, ref in enumerate(ins[:2]):
        out[i] = ref[...]
    at = 2
    for ref in ins[2:]:
        out[at : at + ref.shape[0]] = ref[...]
        at += ref.shape[0]


def spread_part(refs, m):
    if m < 2:
        return refs[m]
    b = m.bit_length() - 1
    return refs[b + 1].at[m - (1 << b)]


def stack_kernel(rows, *refs):
    *ins, out = refs
    for i, ref in enumerate(ins):
        out[i] = ref[:rows, :]


def token_kernel(out):
    out[...] = jnp.zeros_like(out)


def deal_first_kernel(g, labels, src, *outs):
    at = g.here()
    for out, some in zip(outs, labels):
        for i, (f, zz) in enumerate(some):
            chip = lax.bitwise_xor(at.r, at.code(jnp.int32(f))) * g.zs
            out[i] = src[chip + lax.bitwise_xor(at.z, zz)]


def deal_stage_kernel(places, n_in, *refs):
    ins, outs = refs[:n_in], refs[n_in:]
    for out, some in zip(outs, places):
        for i, (a, b) in enumerate(some):
            out[i] = ins[a][b]


def deal_middle_kernel(g, labels, back, table, own, got, *refs):
    outs, (lookup,) = refs[:-1], refs[-1:]
    at = g.here()
    if back:
        for s in range(2 * g.chips):
            lookup[table[s]] = jnp.int32(s)
    else:
        lookup = table
    for out, some in zip(outs, labels):
        for i, (f, zz) in enumerate(some):
            chip = lax.bitwise_xor(at.r, at.code(jnp.int32(f))) * g.zs
            dest = (chip + lax.bitwise_xor(at.z, zz)) * 2 + at.k
            src = lookup[dest]
            core = lax.rem(src, 2)
            src = lax.div(src, 2)
            sz, sr = lax.rem(src, g.zs), lax.div(src, g.zs)
            sf = at.code(lax.bitwise_xor(at.r, sr), core)
            place = sf * g.zs + lax.bitwise_xor(at.z, sz)
            mine = own[place].astype(F32)
            theirs = got[place].astype(F32)
            out[i] = jnp.where(core == at.k, mine, theirs).astype(BF16)


def deal_last_kernel(g, places, n_in, masked, lengths, *refs):
    ins, (out, pool) = refs[:n_in], refs[n_in:]
    at = g.here()
    for e, (a, b) in enumerate(places):
        pool[e] = ins[a][b]
    for chip in range(g.chips):
        f = at.code(lax.bitwise_xor(at.r, chip // g.zs))
        value = pool[f * g.zs + lax.bitwise_xor(at.z, chip % g.zs)]
        if masked:
            row = lax.broadcasted_iota(jnp.int32, value.shape, 0) + chip * g.rows
            value = jnp.where(row < lengths[at.me], value.astype(F32), 0.0).astype(BF16)
        out[chip] = value


def sum_kernel(picks, *refs):
    *ins, out = refs
    total = None
    for ref, pick in zip(ins, picks):
        v = (ref[...] if pick is None else ref[pick]).astype(F32)
        total = v if total is None else total + v
    out[...] = total.astype(out.dtype)


def cut_sum_kernel(g, *refs):
    n = len(refs) - g.zs
    for j, out in enumerate(refs[n:]):
        out[...] = sum(ref[j].astype(F32) for ref in refs[:n]).astype(BF16)


def outer_end_kernel(g, own, got, *outs):
    sub = g.sub
    for c, out in enumerate(outs):
        rows = slice(c * sub, (c + 1) * sub)
        out[...] = (own[rows, :].astype(F32) + got[rows, :].astype(F32)).astype(BF16)


def inner_split_kernel(g, *refs):
    *ins, keep, give = refs
    total = sum(ref[...].astype(F32) for ref in ins).astype(BF16)
    keep[...] = total[: g.hb]
    give[...] = total[g.hb :]


def ffn_pack_kernel(g, keep, got, *refs):
    *ins, out = refs
    first = g.here().k == 0
    hb, sub = g.hb, g.sub
    for b in range(g.zs):
        cols = slice(b * sub, (b + 1) * sub)
        mine, theirs = keep[:, cols].astype(F32), got[:, cols].astype(F32)
        out[:hb, 2 * b * sub : (2 * b + 1) * sub] = jnp.where(first, mine, theirs).astype(BF16)
        out[:hb, (2 * b + 1) * sub : (2 * b + 2) * sub] = jnp.where(first, theirs, mine).astype(BF16)
    out[hb:, :] = sum(ref[...].astype(F32) for ref in ins).astype(BF16)


def ffn_end_kernel(g, *refs):
    at, (inner, outer) = g.here(), refs[-2:]
    parts = [spread_part(refs, m) for m in range(g.rs)]
    hb, sub = g.hb, g.sub
    for m in range(g.rs):
        s = at.quarter(m)
        outer[lanes(s, sub), :] = parts[m][hb:, :].astype(F32)
        if g.aligned:
            for b in range(2 * g.zs):
                place = pl.ds(pl.multiple_of(b * g.fb + s * sub, sub), sub)
                inner[:, place] = parts[m][:hb, b * sub : (b + 1) * sub].astype(F32)
        else:
            inner[s] = parts[m][:hb, : 2 * g.zs * sub].astype(F32)


def attn_split_kernel(g, *refs):
    *ins, keep, mixer, give = refs
    hb = g.hb
    total = sum(ref[...].astype(F32) for ref in ins).astype(BF16)
    keep[:hb, :] = total[:hb, : 3 * hb]
    keep[hb:, :] = total[2 * hb :, : 3 * hb]
    mixer[:, :hb] = total[:hb, 3 * hb :]
    mixer[:, hb:] = total[hb : 2 * hb, 3 * hb :]
    give[:hb, :] = total[hb : 2 * hb, : 3 * hb]
    give[hb:, :] = total[2 * hb :, : 3 * hb]


def attn_pack_kernel(g, keep, mixer, got, out):
    first = g.here().k == 0
    hb = g.hb
    for b in range(3):
        cols = slice(b * hb, (b + 1) * hb)
        mine, theirs = keep[:, cols].astype(F32), got[:, cols].astype(F32)
        out[:, 2 * b * hb : (2 * b + 1) * hb] = jnp.where(first, mine, theirs).astype(BF16)
        out[:, (2 * b + 1) * hb : (2 * b + 2) * hb] = jnp.where(first, theirs, mine).astype(BF16)
    out[:hb, 6 * hb :] = mixer[...]
    out[hb:, 6 * hb :] = jnp.zeros((PAD, 2 * hb), BF16)


def attn_end_kernel(g, *refs):
    at, outs = g.here(), refs[-6:]
    parts = [spread_part(refs, m) for m in range(g.rs)]
    hb, size = g.hb, 2 * g.hb
    gains, table = outs[4:]
    total = None
    for m in range(g.rs):
        q = at.quarter(m)
        for i in range(4):
            outs[i][:, lanes(q, size)] = parts[m][:hb, size * i : size * (i + 1)].astype(F32)
        tiles = parts[m][hb:, :].astype(F32)
        pair = []
        for core in range(2):
            both = [tiles[:, (2 * b + core) * hb : (2 * b + core + 1) * hb] for b in range(3)]
            for i in range(g.nh):
                head = (2 * q + core) * g.nh + i
                table[pl.ds(head, 1), :] = both[2][2 + i : 3 + i, :]
            pair.append(both)
        own = [jnp.where(at.k == 0, pair[0][b][0:1], pair[1][b][0:1]) for b in range(2)]
        their = [jnp.where(at.k == 0, pair[1][b][1:2], pair[0][b][1:2]) for b in range(2)]
        some = [own[b] + their[b] for b in range(2)]
        total = some if total is None else [total[b] + some[b] for b in range(2)]
    for b in range(2):
        gains[b : b + 1, :] = total[b]


def to_relative(g, at, src, dst):
    hb = g.hb
    for j in range(g.zs):
        for h in range(2):
            e = 2 * j + h
            dst[:, e * hb : (e + 1) * hb] = src[:, lanes(at.shard(j, h), hb)]


def norm_kernel(g, own, got, gain, normed, normed_t, scaled, *scratch):
    half = own.shape[0]
    sib = got.at[pl.ds(g.rs * g.hb + PAD, half), :]
    plain, plain_scaled = scratch if g.aligned else (normed, scaled)
    for start, src in ((0, own), (half, sib)):
        v = src[...].astype(F32)
        scale = lax.rsqrt(jnp.mean(v * v, axis=-1, keepdims=True) + EPSILON)
        plain[start : start + half, :] = (v * scale * gain[...]).astype(BF16)
        plain_scaled[start : start + half, :] = (v * scale).astype(BF16)
    if g.aligned:
        to_relative(g, g.here(), plain, normed)
        to_relative(g, g.here(), plain_scaled, scaled)
    normed_t[...] = normed[...].T


def toeplitz(row, n):
    wide = jnp.broadcast_to(row, (n, 2 * n))
    return pltpu.roll(wide, n + 1, 1, stride=1, stride_axis=0)[:, :n]


def probabilities(q, kk, bias, length):
    n = q.shape[0]
    s = dot_nt(q, kk) + bias
    col = lax.broadcasted_iota(jnp.int32, (n, n), 1)
    s = jnp.where(col < length, s, MASKED)
    e = jnp.exp(s - jnp.max(s, axis=-1, keepdims=True))
    return e * (1.0 / jnp.sum(e, axis=-1, keepdims=True))


def two_lengths(at, lengths):
    return lengths[at.me], lengths[lax.bitwise_xor(at.me, 1)]


def attn_kernel(g, m, lengths, normed, off, first, rest, *refs):
    hb, hd = g.hb, g.hd
    at = g.here()
    both = two_lengths(at, lengths)
    if m == 0 or not g.aligned:
        qkv, mixed, w = refs
        w[: 2 * hb, :] = first[: 2 * hb, : 3 * hb]
        copies = None
    else:
        weights, (qkv, mixed, w, sem) = refs[:3], refs[3:]
        copies = Copies(sem)
        fetch_heads(g, at, copies, at.quarter(m), at.k, weights, w, 0)
        w[hb : 2 * hb, :] = first[m * hb : (m + 1) * hb, : 3 * hb]
    for j in range(1, g.zs):
        w[2 * hb * j : 2 * hb * (j + 1), :] = rest[j - 1, :, : 3 * hb]
    if copies is not None:
        copies.wait()
    qkv[...] = dot(normed[...], w[...]).astype(BF16)
    half = normed.shape[0] // 2
    for h in range(g.nh):
        bias = toeplitz(off[h : h + 1, :], half)
        for s in range(2):
            rows = slice(s * half, (s + 1) * half)
            q, kk, v = (qkv[rows, i * hb + h * hd : i * hb + (h + 1) * hd] for i in range(3))
            p = probabilities(q, kk, bias, both[s]).astype(BF16)
            mixed[rows, h * hd : (h + 1) * hd] = dot(p, v).astype(BF16)


def turned_head(g, at, block):
    return at.code(lax.bitwise_xor(block, at.r))


def mixer_kernel(g, *refs):
    rs, zs, hb = g.rs, g.zs, g.hb
    at = g.here()
    mixed_parts, own, rest = refs[:rs], refs[rs], refs[rs + 1 : 2 * rs + 1]
    mixed, wo, partial = refs[2 * rs + 1 :]
    for m in range(rs):
        mixed[:, m * hb : (m + 1) * hb] = mixed_parts[m][...]
    wo[lanes(turned_head(g, at, at.z), hb), :] = own[...]
    for m in range(rs):
        for j in range(1, zs):
            rows = lanes(turned_head(g, at, at.behind(j)), hb)
            piece = rest[m][j - 1, :, 3 * hb :]
            both = jnp.concatenate([piece[:hb], piece[hb:]], axis=1)
            wo[rows, lanes(at.quarter(m), 2 * hb)] = both
    partial[...] = dot(mixed[...], wo[...]).astype(BF16)


def middle_kernel(g, own, got, part, other, gain, *refs):
    sib = got.at[pl.ds(g.rs * g.hb + PAD, g.seq_len), :]
    middle, normed2, normed2_t, mine = refs[:4]
    plain = refs[4] if g.aligned else normed2
    half = own.shape[0]
    for s, src in ((0, own), (1, sib)):
        rows = slice(s * half, (s + 1) * half)
        swapped = slice((1 - s) * half, (2 - s) * half)
        v = src[...].astype(F32) + part[rows, :].astype(F32) + other[swapped, :].astype(F32)
        middle[rows, :] = v
        scale = lax.rsqrt(jnp.mean(v * v, axis=-1, keepdims=True) + EPSILON)
        plain[rows, :] = (v * scale * gain[...]).astype(BF16)
    if g.aligned:
        to_relative(g, g.here(), plain, normed2)
    normed2_t[...] = normed2[...].T
    mine[...] = normed2[:half, :]


def pair_swapped(g, value):
    if not g.aligned:
        return value
    hb = g.hb
    blocks = [value[:, e * hb : (e + 1) * hb] for e in range(2 * g.zs)]
    return jnp.concatenate([blocks[e ^ 1] for e in range(2 * g.zs)], axis=1)


def ffn_work(g, at, n2, n2_t, gl, w1s, w2s, done):
    out_sum, gn_sum = None, None
    for c in range(g.rs // 2):
        w1, w2 = w1s[c], w2s[c]
        h = dot(n2[...], w1[...])
        cdf = 0.5 * (1.0 + lax.erf(h * INV_SQRT2))
        pdf = jnp.exp(-0.5 * h * h) * INV_SQRT2PI
        act = (h * cdf).astype(BF16)
        ga = dot_nt(gl[...], w2[...])
        gh = (ga * (cdf + h * pdf)).astype(BF16)
        done(c, dot(n2_t[...], gh), dot_tn(act, gl[...]))
        out_part = dot(act, w2[...])
        gn_part = dot_nt(gh, w1[...])
        out_sum = out_part if out_sum is None else out_sum + out_part
        gn_sum = gn_part if gn_sum is None else gn_sum + gn_part
    return gn_sum, out_sum


def share_out(g, sums, own, swap):
    half = g.seq_len
    for i, total in enumerate(sums):
        own[i] = total[:half]
        swap[i] = total[half:].astype(BF16)


def ffn_own_kernel(g, n2, n2_t, gl_own, gl_sib, *refs):
    hb, sub, zs, cols = g.hb, g.sub, g.zs, g.cols
    at = g.here()
    half, n = g.seq_len, g.rs // 2
    pieces, refs = refs[: n * (zs - 1)], refs[n * (zs - 1) :]
    n_first = 2 if g.aligned else n
    firsts, refs = refs[:n_first], refs[n_first:]
    if g.aligned:
        wi, wu, refs = *refs[:2], refs[2:]
    gl, own, swap, go, refs = *refs[:4], refs[4:]
    grads, w1s, w2s, refs = refs[:n], refs[n : 2 * n], refs[2 * n : 3 * n], refs[3 * n :]
    copies = Copies(refs[0]) if g.aligned else None
    gl[:half, :] = gl_own[...]
    gl[half:, :] = gl_sib[...]

    def place_piece(piece, w1, w2, j):
        w1[2 * hb * j : 2 * hb * (j + 1), :] = piece[: 2 * hb, :]
        place = lanes(at.behind(j), sub)
        for b in range(g.parts):
            rows = slice(2 * hb + b * sub, 2 * hb + (b + 1) * sub)
            w2[place, b * cols : (b + 1) * cols] = piece[rows, :]

    for c in range(n):
        w1, w2 = w1s[c], w2s[c]
        if c and g.aligned:
            s = at.even(c)
            fetch_inner(g, at, copies, s, at.k, wi, w1, 0, 0)
            copies.start(wu.at[lanes(s, sub), :], w2.at[lanes(at.z, sub), :])
            w1[hb : 2 * hb, :] = firsts[-1][c * hb : (c + 1) * hb, 3 * hb : 3 * hb + cols]
        else:
            place_piece(firsts[c], w1, w2, 0)
        for j in range(1, zs):
            place_piece(pieces[c * (zs - 1) + j - 1], w1, w2, j)
    if copies is not None:
        copies.wait()

    def done(c, inner, outer):
        grads[c][...] = inner.astype(BF16).reshape(grads[c].shape)
        outer = outer.astype(BF16)
        for b in range(zs):
            place = lax.rem(at.z + (zs - b), zs)
            go[place, c * sub : (c + 1) * sub, :] = outer[b * sub : (b + 1) * sub, :]

    share_out(g, ffn_work(g, at, n2, n2_t, gl, w1s, w2s, done), own, swap)


def ffn_other_kernel(g, nx, nxk, gx, gxk, *refs):
    sub, zs, n, half = g.sub, g.zs, g.rs // 2, g.seq_len
    at = g.here()
    w1s, w2s, gi_in, refs = refs[:n], refs[n : 2 * n], refs[2 * n : 3 * n], refs[3 * n :]
    go_in, own, swap, refs = refs[0], refs[1], refs[2], refs[3:]
    grads, outs, (n2, n2_t, gl, go) = refs[:n], refs[n : n + zs], refs[n + zs :]
    n2[:half, :] = nx[...]
    n2[half:, :] = pair_swapped(g, nxk[...])
    n2_t[...] = n2[...].T
    gl[:half, :] = gx[...]
    gl[half:, :] = gxk[...]

    def done(c, inner, outer):
        shape = grads[c].shape
        grads[c][...] = (inner.reshape(shape) + gi_in[c][...].astype(F32)).astype(BF16)
        for b in range(zs):
            place = lax.rem(at.z + (zs - b), zs)
            rows = slice(c * sub, (c + 1) * sub)
            before = go_in[place, rows, :].astype(F32)
            go[place, rows, :] = (outer[b * sub : (b + 1) * sub, :] + before).astype(BF16)

    share_out(g, ffn_work(g, at, n2, n2_t, gl, w1s, w2s, done), own, swap)
    for j in range(zs):
        outs[j][...] = go[j]


def cross_sum_kernel(g, part, got, gn_out, outer_out):
    gn = part[0] + pair_swapped(g, got[0].astype(F32))
    gn_out[...] = gn.astype(BF16)
    outer_out[...] = (part[1] + got[1].astype(F32)).astype(BF16)


def own_sum_kernel(g, part, got, cross, out):
    total = part[0] + pair_swapped(g, got[0].astype(F32)) + cross[...].astype(F32)
    out[...] = total.astype(BF16)


def absolute_sum(g, at, part, other, rows, swapped, total):
    hb = g.hb
    if not g.aligned:
        total[...] = part[rows, :].astype(F32) + other[swapped, :].astype(F32)
        return
    for j in range(g.zs):
        for h in range(2):
            mine, theirs = 2 * j + h, 2 * j + 1 - h
            a = part[rows, mine * hb : (mine + 1) * hb].astype(F32)
            b = other[swapped, theirs * hb : (theirs + 1) * hb].astype(F32)
            total[:, lanes(at.shard(j, h), hb)] = a + b


def middle_back_kernel(g, own, other, middle, gl, gain, mixed, wo, *refs):
    grad_mid, gm, ggain, gwo, gatt, total = refs[:6]
    at, hb = g.here(), g.hb
    half, width = g.seq_len, g.width
    for s in range(2):
        rows = slice(s * half, (s + 1) * half)
        if g.aligned:
            for j in range(g.zs):
                for h in range(2):
                    e = 2 * j + (1 - h if s else h)
                    some = (other if s else own)[:, e * hb : (e + 1) * hb]
                    total[:, lanes(at.shard(j, h), hb)] = some.astype(F32)
        else:
            total[...] = (other if s else own)[...].astype(F32)
        gn = total[...]
        v = middle[rows, :]
        scale = lax.rsqrt(jnp.mean(v * v, axis=-1, keepdims=True) + EPSILON)
        gg = gn * gain[...]
        inner = jnp.sum(gg * v, axis=-1, keepdims=True) * (1.0 / width)
        grad = gl[rows, :].astype(F32) + scale * gg - v * (scale * scale * scale * inner)
        if s == 0:
            grad_mid[...] = grad
            sums = jnp.sum(gn * v * scale, axis=0, keepdims=True)
            if g.aligned:
                refs[6][...] = sums
                to_relative(g, at, refs[6], ggain)
            else:
                ggain[...] = sums
        gatt[rows, :] = grad.astype(BF16)
    gm[...] = dot_nt(gatt[...], wo[...]).astype(BF16)
    full = dot_tn(mixed[...], gatt[...]).astype(BF16)
    for m in range(g.rs):
        place = lax.rem(at.z + (g.zs - at.quarter(m)), g.zs)
        gwo[place] = full[m * hb : (m + 1) * hb, :]


def attn_back_kernel(g, m, step, lengths, normed_t, off, qkv, gmix, gwo, hot, scaled, w, *refs):
    hb, hd = g.hb, g.hd
    at = g.here()
    both = two_lengths(at, lengths)
    half = g.seq_len
    extra, refs = (refs[:1], refs[1:]) if m == 0 else ((), refs)
    before, refs = (refs[0], refs[1:]) if step else (None, refs)
    gw, *gn, gqkv = refs
    flip = (
        lax.broadcasted_iota(jnp.int32, (half, half), 0)
        + lax.broadcasted_iota(jnp.int32, (half, half), 1)
        == half - 1
    ).astype(BF16)
    table = []
    for h in range(g.nh):
        bias = toeplitz(off[h : h + 1, :], half)
        flipped = jnp.zeros((half, half), F32)
        for s in range(2):
            rows = slice(s * half, (s + 1) * half)
            q, kk, v = (qkv[rows, i * hb + h * hd : i * hb + (h + 1) * hd] for i in range(3))
            gm = gmix[rows, m * hb + h * hd : m * hb + (h + 1) * hd]
            p = probabilities(q, kk, bias, both[s])
            gp = dot_nt(gm, v)
            delta = jnp.sum(p * gp, axis=-1, keepdims=True)
            gs = (p * (gp - delta)).astype(BF16)
            flipped = flipped + dot(flip, gs)
            cols = [slice(i * hb + h * hd, i * hb + (h + 1) * hd) for i in range(3)]
            gqkv[rows, cols[0]] = dot(gs, kk).astype(BF16)
            gqkv[rows, cols[1]] = dot_tn(gs, q).astype(BF16)
            gqkv[rows, cols[2]] = dot_tn(p.astype(BF16), gm).astype(BF16)
        wide = jnp.concatenate([flipped, jnp.zeros((half, half), F32)], axis=1)
        skewed = pltpu.roll(wide, 0, 1, stride=1, stride_axis=0)
        diag = jnp.broadcast_to(jnp.sum(skewed, axis=0, keepdims=True), (8, 2 * half))
        top = diag.astype(BF16)
        table.append(dot_nt(top, hot[...]) + dot_nt((diag - top.astype(F32)).astype(BF16), hot[...]))
    gw[:, : 2 * hb, : 3 * hb] = (
        dot(normed_t[...], gqkv[...]).astype(BF16).reshape(g.zs, 2 * hb, 3 * hb)
    )
    row = lax.broadcasted_iota(jnp.int32, (PAD, hb), 0)
    buckets = jnp.zeros((PAD, hb), F32)
    for i, t in enumerate(table):
        buckets = jnp.where(row == 2 + i, jnp.broadcast_to(t[0:1], (PAD, hb)), buckets)
    for j in range(g.zs):
        piece = gwo[j, :, lanes(at.quarter(m), 2 * hb)]
        gw[j, :hb, 3 * hb :] = piece[:, :hb]
        gw[j, hb : 2 * hb, 3 * hb :] = piece[:, hb:]
        part = dot_nt(gqkv[...], w[2 * hb * j : 2 * hb * (j + 1), :])
        cols = slice(2 * hb * j, 2 * hb * (j + 1))
        gain = jnp.sum(part * scaled[:, cols].astype(F32), axis=0, keepdims=True)
        tile = [gain[:, :hb], gain[:, hb:]]
        tile = jnp.where(row == 0, tile[0], jnp.where(row == 1, tile[1], 0.0))
        gw[j, 2 * hb :, :hb] = tile.astype(BF16)
        if m == 0:
            tile = [extra[0][:, (2 * j + h) * hb : (2 * j + h + 1) * hb] for h in range(2)]
            tile = jnp.where(row == 0, tile[0], jnp.where(row == 1, tile[1], 0.0))
        else:
            tile = jnp.zeros((PAD, hb), F32)
        gw[j, 2 * hb :, hb : 2 * hb] = tile.astype(BF16)
        gw[j, 2 * hb :, 2 * hb : 3 * hb] = buckets.astype(BF16)
        gw[j, 2 * hb :, 3 * hb :] = jnp.zeros((PAD, hb), BF16)
        if before is not None:
            part = part + before[:, cols]
        if len(gn) == 1:
            gn[0][:, cols] = part
        else:
            gn[0][:, cols] = part[:half]
            gn[1][:, cols] = part[half:].astype(BF16)


def input_back_kernel(g, own, other, grad_mid, x, gain, out, total):
    everything = slice(None)
    absolute_sum(g, g.here(), own, other, everything, everything, total)
    gn = total[...]
    v = x[...].astype(F32)
    scale = lax.rsqrt(jnp.mean(v * v, axis=-1, keepdims=True) + EPSILON)
    gg = gn * gain[...]
    inner = jnp.mean(gg * v, axis=-1, keepdims=True)
    grad = grad_mid[...] + scale * gg - v * (scale * scale * scale * inner)
    out[...] = grad.astype(BF16)


def layer_kernel(g, lengths, middle, part, got, cross, out):
    half = g.seq_len
    row = lax.broadcasted_iota(jnp.int32, out.shape, 0)
    v = middle[:half, :] + part[1] + got[1].astype(F32) + cross[...].astype(F32)
    out[...] = jnp.where(row < lengths[g.here().me], v, 0.0).astype(BF16)


CORE, MIDDLE, SWAP, SWAP_X, NORMED, INNER, ATTN, COT, COT_SIB, COT_X, COT_XK, LAYER = range(12)
MINE_X, MINE_XK, GN_X, GN_K, OUTER_X = range(12, 17)
RING_A, RING_F, HOP_A, HOP_F, GI, GI_SUM, GH, GH_SUM, OA, LATE, SPREAD_F, SPREAD_T = range(17, 29)

ORDER = (
    0, 4, ((COT, 0), 1), 1, 5, (RING_A, 2), 6, 2, (RING_A, 3), ((COT, 2), 0), 3, 12, 13, 7, 15, 8,
    9, 14, 16, 10, (RING_F, 1), ((HOP_F, 1), 1), (RING_F, 3), 17, 18, ((HOP_F, 3), 1), 11, 19,
    (MINE_XK,), (RING_F, 2), (CORE,), 20, 21, 22, 30, 23, 25, 32, 31, 24, 35, 44, 26, (GH, 1), 46,
    27, 36, 33, 28, 43, 34, 37, 48, (GN_K,), 29, (LATE, 1), 45, (INNER,), (GH_SUM, 1),
    ((COT, 5), 1), 38, 49, (GI_SUM, 3), 47, 52, 39, (GI_SUM, 2), (GN_X,), ((LAYER, 0), 1), 50, 51,
    40, 54, (SPREAD_T, 1), 41, 53, 55, 42,
)


def solution(mesh):
    rs, ss = mesh.shape["rep"], mesh.shape["shard"]
    zs = ss // 2
    count = rs * ss
    nb = rs.bit_length() - 1

    def pairs(move):
        table = []
        for i in range(count):
            r, z, k = i // ss, (i % ss) // 2, i % 2
            r, z, k = move(r, z, k)
            table.append((i, (r * zs + z) * 2 + k))
        return table

    core_pairs = pairs(lambda r, z, k: (r, z, 1 - k))
    up_pairs = pairs(lambda r, z, k: (r, (z + 1) % zs, k))
    rep_pairs = [
        pairs(lambda r, z, k, b=b: (r ^ (1 << (nb - 1 - b if k else b)), z, k)) for b in range(nb)
    ]
    plain_pairs = [pairs(lambda r, z, k, b=b: (r ^ (1 << b), z, k)) for b in range(nb)]
    z_pairs = {m: pairs(lambda r, z, k, m=m: (r, z ^ m, k)) for m in range(1, zs)}

    def send(value, table):
        return lax.ppermute(value, AXES, table)

    by_size = sorted(range(1, rs), key=lambda m: (bin(m).count("1"), m))

    def high(m):
        return m.bit_length() - 1

    def low(m):
        return (m & -m).bit_length() - 1

    def local(
        inputs,
        cotangent,
        seq_lengths,
        dealing,
        rel_buckets,
        w_query,
        w_key,
        w_value,
        w_mixer,
        w_inner,
        w_outer,
        gain_attn,
        gain_mlp,
        bias_table,
    ):
        seq = Sequence()
        bind = functools.partial
        n_buckets, heads = bias_table.shape[0] * ss, bias_table.shape[1]
        g = Geometry(rs, zs, w_query.shape[0], w_outer.shape[0], heads, *inputs.shape[1:])
        hb, fb, sub, cols, nh = g.hb, g.fb, g.sub, g.cols, g.nh
        seq_len, width, tokens = g.seq_len, g.width, g.tokens
        chips, rows = g.chips, g.rows
        chunks = rs // 2

        r, c = lax.axis_index("rep"), lax.axis_index("shard")
        z, k = c // 2, c % 2
        shards = jnp.arange(ss, dtype=jnp.int32)
        x_own = inputs[0]
        d = Box()
        parts = {}

        def relative():
            return 2 * ((z + zs - shards // 2) % zs) + (k ^ (shards % 2))

        def permute_cols(x, order):
            return jnp.take(x.reshape(-1, ss, hb), order, axis=1).reshape(x.shape)

        val = {}
        steps = []

        def put(name, value, table):
            val[name] = send(value, table)

        def step(run, *args):
            steps.append(bind(run, *args))

        labels = [(f, zz) for f in range(rs) for zz in range(zs)]

        def groups_of(stage):
            if stage == nb:
                return [[e for e in labels if e[1] == zz] for zz in range(zs)]
            clear = [e for e in labels if not (e[0] >> stage) & 1]
            return [clear, [e for e in labels if e not in clear]]

        def block_shapes(groups):
            outs = [shaped((len(some), rows, width)) for some in groups]
            return outs if len(outs) == 1 else [stored(outs[0].shape)] + outs[1:]

        def dispatch(key, outs, stage):
            groups = groups_of(stage)
            val[key] = outs[0]
            state = [(key, groups[0])]
            for i, (out, some) in enumerate(zip(outs[1:], groups[1:])):
                put((key, i), out, z_pairs[i + 1] if stage == nb else rep_pairs[stage])
                state.append(((key, i), some))
            return state

        def places(state, some):
            at = {e: (a, b) for a, (_, named) in enumerate(state) for b, e in enumerate(named)}
            return [at[e] for e in some]

        def values(state):
            return [val[name] for name, _ in state]

        def deal_first(what, stage):
            groups = groups_of(stage)
            value = parts[what].reshape(chips, rows, width)
            outs = seq(bind(deal_first_kernel, g, groups), block_shapes(groups), value)
            parts[what] = dispatch((what, 0), outs, stage)

        def deal_stage(what, number, stage):
            groups, state = groups_of(stage), parts[what]
            body = bind(deal_stage_kernel, [places(state, some) for some in groups], len(state))
            outs = seq(body, block_shapes(groups), *values(state))
            parts[what] = dispatch((what, number), outs, stage)

        def deal_core(what):
            state = parts[what]
            body = bind(deal_stage_kernel, [places(state, labels)], len(state))
            parts[what] = seq(body, block_shapes([labels]), *values(state))[0]
            put((what, CORE), parts[what], core_pairs)

        def deal_middle(what, number, stage, back):
            groups = groups_of(stage)
            body = bind(deal_middle_kernel, g, groups, back)
            lookup = [pltpu.SMEM((count,), jnp.int32)]
            args = dealing, parts[what], val[what, CORE]
            outs = seq(body, block_shapes(groups), *args, scalars=1, scratch=lookup)
            parts[what] = dispatch((what, number), outs, stage)

        def deal_last(what, masked):
            state = parts[what]
            body = bind(deal_last_kernel, g, places(state, labels), len(state), masked)
            pool = [pltpu.VMEM((chips, rows, width), BF16)]
            shape = [shaped((chips, rows, width))]
            out = seq(body, shape, seq_lengths, *values(state), scalars=1, scratch=pool)[0]
            parts[what] = out.reshape(seq_len, width)

        def deal(what, first, second, back, end):
            step(deal_first, what, first[0])
            for i, stage in list(enumerate(first))[1:]:
                step(deal_stage, what, i, stage)
            step(deal_core, what)
            n = len(first)
            step(deal_middle, what, n, second[0], back)
            for i, stage in list(enumerate(second))[1:]:
                step(deal_stage, what, n + i, stage)
            step(end)

        copy_sem = pltpu.SemaphoreType.DMA(())

        def slices(m, core):
            s = r ^ (m + core * (g.turned(m) - m))
            at = (2 * s + core) * hb
            parts = [lax.dynamic_slice(w, (0, at), (hb, hb)) for w in (w_query, w_key, w_value)]
            return parts, lax.dynamic_slice(w_mixer, (0, s * 2 * hb), (hb, 2 * hb))

        def inner_slices(c, core):
            s = r ^ (2 * c)
            at = [(2 * b + core) * fb + s * sub for b in range(zs)]
            inner = [lax.dynamic_slice(w_inner, (0, a), (hb, sub)) for a in at]
            outer = lax.dynamic_slice(w_outer, (s * sub, 0), (sub, width))
            return inner, [outer[:, i * cols : (i + 1) * cols] for i in range(g.parts)]

        small_args = gain_attn.reshape(1, hb), gain_mlp.reshape(1, hb), bias_table

        def start_core():
            if g.aligned:
                sent = seq(
                    bind(send_prep_kernel, g),
                    [shaped((rs * hb + PAD + seq_len, width))],
                    *small_args,
                    w_query,
                    w_key,
                    w_value,
                    w_inner,
                    x_own,
                    hbm=5,
                    scratch=[copy_sem],
                )[0]
            else:
                sent = []
                for m in range(rs):
                    parts = slices(m, 1 - k)[0]
                    inner = inner_slices(m % (rs // 2), 1 - k)[0]
                    sent.append(jnp.concatenate(parts + inner, axis=1))
                sent = jnp.concatenate(sent + [small_rows()], axis=0)
                sent = jnp.pad(sent, ((0, 0), (0, width - sent.shape[1])))
                sent = jnp.concatenate([sent, x_own], axis=0)
            put(CORE, sent, core_pairs)

        def small_rows():
            tile = jnp.zeros((PAD, 3 * hb + cols), BF16)
            tile = tile.at[0, :hb].set(gain_attn).at[0, hb : 2 * hb].set(gain_mlp)
            n = bias_table.shape[0]
            return tile.at[8 : 8 + n, 2 * hb : 2 * hb + heads].set(bias_table)

        def start_attn():
            got = val[CORE]
            if g.aligned:
                own = seq(
                    bind(attn_prep_kernel, g),
                    [shaped((2 * hb + PAD, 4 * hb))],
                    *small_args,
                    got,
                    w_query,
                    w_key,
                    w_value,
                    w_mixer,
                    hbm=4,
                    scratch=[pltpu.VMEM((PAD, 4 * hb), BF16), copy_sem],
                )
            else:
                own = []
                for m in range(rs):
                    parts, mix = slices(m, k)
                    top = jnp.concatenate(parts + [mix[:, :hb]], axis=1)
                    bottom = [got[m * hb : (m + 1) * hb, : 3 * hb], mix[:, hb:]]
                    own.append(jnp.concatenate([top, jnp.concatenate(bottom, axis=1)], axis=0))
                mine = small_rows()[:, : 4 * hb]
                theirs = got[rs * hb : rs * hb + PAD, : 4 * hb]
                both = [mine[:1], theirs[:1], mine[2:12], theirs[8:12]]
                both = jnp.concatenate(both, axis=0)
                own[0] = jnp.concatenate([own[0], both], axis=0)
            d.attn_own = own
            ring(RING_A, own[0])

        def start_ffn():
            got = val[CORE]
            if g.aligned:
                own = seq(
                    bind(ffn_prep_kernel, g),
                    [shaped((4 * hb, cols))],
                    got,
                    w_inner,
                    w_outer,
                    hbm=2,
                    scratch=[copy_sem],
                )
            else:
                own = []
                for c in range(rs // 2):
                    top, below = inner_slices(c, k)
                    bottom = got[c * hb : (c + 1) * hb, 3 * hb : 3 * hb + cols]
                    own.append(
                        jnp.concatenate([jnp.concatenate(top, axis=1), bottom] + below, axis=0)
                    )
            d.ffn_own = own
            ring(RING_F, own[0])
            for j in range(1, zs):
                even_hops((HOP_F, j), val[RING_F, j])

        def ring(name, value):
            for j in range(1, zs):
                put((name, j), value if j == 1 else val[name, j - 1], up_pairs)

        def hops(name, value):
            val[name, 0] = value
            for m in by_size:
                put((name, m), val[name, m ^ (1 << high(m))], rep_pairs[high(m)])

        def even_hops(name, value):
            val[name, 0] = value
            for c in range(1, rs // 2):
                b = high(c)
                put((name, c), val[name, c ^ (1 << b)], plain_pairs[b + 1])

        def stack_attn():
            pieces = [val[RING_A, j] for j in range(1, zs)]
            shape = [shaped((zs - 1, 2 * hb, 4 * hb))]
            hops(HOP_A, seq(bind(stack_kernel, 2 * hb), shape, *pieces)[0])

        def small_params():
            pieces = [d.attn_own[0]] + [val[RING_A, j] for j in range(1, zs)]
            tiles = jnp.stack([piece[2 * hb :, :] for piece in pieces])
            order = (shards[:, None] == relative()[None, :]).astype(BF16)
            gains = dot(order, tiles[:, :2, : 2 * hb].reshape(ss, 2 * hb))
            d.gain_a = gains[:, :hb].reshape(1, width)
            d.gain_m = gains[:, hb:].reshape(1, width)
            n = n_buckets // ss
            table = tiles[:, 8:, 2 * hb : 2 * hb + heads].reshape(ss, 4, heads)[:, :n]
            table = dot(order, table.reshape(ss, n * heads)).reshape(n_buckets, heads)
            quarters = jnp.arange(rs, dtype=jnp.int32)
            quarters = r ^ (quarters + k * (g.turned(quarters) - quarters))
            head_ids = ((2 * quarters + k) * nh)[:, None] + jnp.arange(nh, dtype=jnp.int32)[None]
            pick = jnp.arange(heads, dtype=jnp.int32)[:, None] == head_ids.reshape(1, -1)
            padded = jnp.concatenate([rel_buckets, jnp.full((1,), -1, jnp.int32)])
            hot = padded[None, :] == jnp.arange(hb, dtype=jnp.int32)[:, None]
            d.hot = hot.astype(BF16)
            my_table = dot(table.astype(BF16), pick.astype(BF16)).astype(BF16)
            d.offsets = lax.dot_general(
                my_table,
                d.hot[:n_buckets],
                (((0,), (0,)), ((), ())),
                preferred_element_type=F32,
            ).reshape(rs, nh, 2 * seq_len)

        spare = [pltpu.VMEM((tokens, width), BF16)] if g.aligned else []

        def norm():
            small_params()
            normed, normed_t, scaled = seq(
                bind(norm_kernel, g),
                [shaped((tokens, width)), stored((width, tokens)), stored((tokens, width))],
                x_own,
                val[CORE],
                d.gain_a,
                scratch=spare * 2,
            )
            if not g.aligned:
                normed = permute_cols(normed, relative())
                scaled = permute_cols(scaled, relative())
                normed_t = normed.T
            d.normed, d.normed_t, d.scaled = normed, normed_t, scaled
            d.qkv, d.mixed_parts, d.attn_w = ([None] * rs for _ in range(3))

        def attend(m):
            own = m == 0 or not g.aligned
            weights = () if own else (w_query, w_key, w_value)
            d.qkv[m], d.mixed_parts[m], d.attn_w[m] = seq(
                bind(attn_kernel, g, m),
                [stored((tokens, 3 * hb)), stored((tokens, hb)), stored((width, 3 * hb))],
                seq_lengths,
                d.normed,
                d.offsets[m],
                d.attn_own[m] if own else val[CORE],
                val[HOP_A, m],
                *weights,
                scalars=1,
                hbm=len(weights),
                scratch=() if own else [copy_sem],
            )

        def mixer():
            d.mixed, d.wo, d.partial = seq(
                bind(mixer_kernel, g),
                [stored((tokens, rs * hb)), stored((rs * hb, width)), shaped((tokens, width))],
                *d.mixed_parts,
                w_mixer,
                *[val[HOP_A, m] for m in range(rs)],
            )
            put(MIDDLE, d.partial, core_pairs)

        def middle():
            d.middle, normed2, normed2_t, mine = seq(
                bind(middle_kernel, g),
                [
                    stored((tokens, width), F32),
                    shaped((tokens, width)),
                    shaped((width, tokens)),
                    shaped((seq_len, width)),
                ],
                x_own,
                val[CORE],
                d.partial,
                val[MIDDLE],
                d.gain_m,
                scratch=spare,
            )
            if not g.aligned:
                normed2 = permute_cols(normed2, relative())
                normed2_t, mine = normed2.T, normed2[:seq_len]
            put(MINE_X, mine, plain_pairs[0])
            put(MINE_XK, val[MINE_X], core_pairs)
            d.normed2, d.normed2_t = normed2, normed2_t

        sums = [shaped((2, seq_len, width), F32), shaped((2, seq_len, width))]
        weights_made = [shaped((width, cols))] * chunks + [shaped((cols, width))] * chunks

        def ffn_own():
            firsts = [d.ffn_own[0], val[CORE]] if g.aligned else d.ffn_own
            weights = (w_inner, w_outer) if g.aligned else ()
            outs = seq(
                bind(ffn_own_kernel, g),
                [shaped((tokens, width))]
                + sums
                + [shaped((zs, chunks * sub, width))]
                + [shaped((zs, 2 * hb, cols))] * chunks
                + weights_made,
                d.normed2,
                d.normed2_t,
                parts[COT],
                val[COT_SIB],
                *[val[(HOP_F, j), c] for c in range(chunks) for j in range(1, zs)],
                *firsts,
                *weights,
                hbm=len(weights),
                scratch=[copy_sem] if g.aligned else (),
                limit=24,
            )
            d.gl, d.ffn_part, swap, d.go = outs[:4]
            d.gi, d.weights = outs[4 : 4 + chunks], outs[4 + chunks :]
            put(SWAP, to_absolute(swap), core_pairs)

        def to_absolute(swap):
            if g.aligned:
                return swap
            return jnp.stack([permute_cols(swap[0], jnp.argsort(relative())), swap[1]])

        def ffn_other():
            nxk = val[MINE_XK]
            if not g.aligned:
                nxk = permute_cols(nxk, shards ^ 1)
            outs = seq(
                bind(ffn_other_kernel, g),
                sums + [shaped((zs, 2 * hb, cols))] * chunks + [shaped((chunks * sub, width))] * zs,
                val[MINE_X],
                nxk,
                val[COT_X],
                val[COT_XK],
                *d.weights,
                *d.gi,
                d.go,
                scratch=[
                    pltpu.VMEM((tokens, width), BF16),
                    pltpu.VMEM((width, tokens), BF16),
                    pltpu.VMEM((tokens, width), BF16),
                    pltpu.VMEM((zs, chunks * sub, width), BF16),
                ],
                limit=24,
            )
            d.cross_part, swap = outs[:2]
            parts[GI] = list(outs[2 : 2 + chunks])
            parts[OA] = outs[2 + chunks :]
            put(SWAP_X, to_absolute(swap), core_pairs)
            for c in range(1, chunks):
                if c % 2:
                    put((GI, c), parts[GI][c], plain_pairs[1])
            put((OA, 1), parts[OA][1], up_pairs)

        def cross_sum():
            part = d.cross_part
            if not g.aligned:
                part = jnp.stack([permute_cols(part[0], jnp.argsort(relative())), part[1]])
            gn, outer = seq(
                bind(cross_sum_kernel, g), [shaped((seq_len, width))] * 2, part, val[SWAP_X]
            )
            put(GN_X, gn, plain_pairs[0])
            put(OUTER_X, outer, plain_pairs[0])

        def own_sum():
            part = d.ffn_part
            if not g.aligned:
                part = jnp.stack([permute_cols(part[0], jnp.argsort(relative())), part[1]])
            shape = [shaped((seq_len, width))]
            d.gn2 = seq(bind(own_sum_kernel, g), shape, part, val[SWAP], val[GN_X])[0]
            put(GN_K, d.gn2, core_pairs)

        def add(*terms):
            shape = [shaped(terms[0].shape)]
            return seq(bind(sum_kernel, [None] * len(terms)), shape, *terms)[0]

        def sum_step(name, j):
            put((name, j), add(val[name, j - 1], parts[name][j]), up_pairs)

        def hop_start(name, m):
            put((name, m), parts[name][m], rep_pairs[low(m)])

        def inner_add(c):
            some = parts[GI]
            above = [c | 1 << b for b in range(nb - 1) if not (c >> b) & 1 and low(c | 1 << b) == b]
            terms = [some[c]] + [val[GI, i] for i in above]
            if c:
                some[c] = add(*terms)
                put((GI, c), some[c], plain_pairs[low(c) + 1])
            else:
                shape = [shaped(some[0].shape[1:])] * zs
                parts[GI_SUM] = seq(bind(cut_sum_kernel, g), shape, *terms)
                put((GI_SUM, 1), parts[GI_SUM][1], up_pairs)

        def hop_add(name, ring, m):
            some = parts[name]
            bits = [b for b in range(nb) if not (m >> b) & 1 and low(m | 1 << b) == b]
            terms = [some[m]] + [val[name, m | 1 << b] for b in bits]
            if m:
                some[m] = add(*terms)
                hop_start(name, m)
            else:
                shape = [shaped(some[0].shape[1:])] * zs
                parts[ring] = seq(bind(cut_sum_kernel, g), shape, *terms)
                put((ring, 1), parts[ring][1], up_pairs)

        def outer_end():
            shape = [shaped((sub, width))] * chunks
            some = list(seq(bind(outer_end_kernel, g), shape, parts[OA][0], val[OA, zs - 1]))
            names = []
            for c in range(chunks - 1, 0, -1):
                b = low(c)
                put((LATE, c), some[c], plain_pairs[b + 1])
                if c ^ (1 << b):
                    some[c ^ (1 << b)] = add(some[c ^ (1 << b)], val[LATE, c])
                else:
                    names.append((LATE, c))
            d.late, d.late_names = some, names

        def inner_split():
            keep, give = seq(
                bind(inner_split_kernel, g),
                [shaped((hb, cols))] * 2,
                parts[GI_SUM][0],
                val[GI_SUM, zs - 1],
            )
            d.inner_keep = keep
            put(INNER, give, core_pairs)

        def spread(name, value):
            val[name, 0] = value
            put((name, 1), value, rep_pairs[0])

        def spread_next(name):
            for b in range(1, nb):
                some = [val[name, i] for i in range(b + 1)]
                shape = [shaped((1 << b, *some[0].shape))]
                put((name, b + 1), seq(spread_pack_kernel, shape, *some)[0], rep_pairs[b])

        def ffn_pack():
            late = [d.late[0]] + [val[name] for name in d.late_names]
            shape = [shaped((hb + sub, width))]
            body = bind(ffn_pack_kernel, g)
            spread(SPREAD_F, seq(body, shape, d.inner_keep, val[INNER], *late)[0])

        def ffn_end():
            shape = (hb, 2 * zs * fb) if g.aligned else (rs, hb, 2 * zs * sub)
            inner, d.sum_out = seq(
                bind(ffn_end_kernel, g),
                [stored(shape, F32), stored((fb, width), F32)],
                *[val[SPREAD_F, i] for i in range(nb + 1)],
            )
            if not g.aligned:
                inner = jnp.transpose(inner.reshape(rs, hb, 2 * zs, sub), (1, 2, 0, 3))
                inner = inner.reshape(hb, -1)
            d.sum_in = inner

        def attn_split():
            d.attn_keep, d.mixer_keep, give = seq(
                bind(attn_split_kernel, g),
                [
                    shaped((hb + PAD, 3 * hb)),
                    shaped((hb, 2 * hb)),
                    shaped((hb + PAD, 3 * hb)),
                ],
                parts[GH_SUM][0],
                val[GH_SUM, zs - 1],
            )
            put(ATTN, give, core_pairs)

        def attn_pack():
            shape = [shaped((hb + PAD, 8 * hb))]
            args = d.attn_keep, d.mixer_keep, val[ATTN]
            spread(SPREAD_T, seq(bind(attn_pack_kernel, g), shape, *args)[0])

        def attn_end():
            *d.sum_attn, d.gains, d.table = seq(
                bind(attn_end_kernel, g),
                [stored((hb, width), F32)] * 4 + [shaped((8, hb), F32), shaped((heads, hb), F32)],
                *[val[SPREAD_T, i] for i in range(nb + 1)],
            )

        def middle_back():
            more = [pltpu.VMEM((1, width), F32)] if g.aligned else []
            d.grad_mid, d.gmix, ggain, d.grad_wo = seq(
                bind(middle_back_kernel, g),
                [
                    stored((seq_len, width), F32),
                    shaped((tokens, rs * hb)),
                    shaped((1, width), F32),
                    shaped((zs, hb, width)),
                ],
                d.gn2,
                val[GN_K],
                d.middle,
                d.gl,
                d.gain_m,
                d.mixed,
                d.wo,
                scratch=[pltpu.VMEM((tokens, width), BF16), pltpu.VMEM((seq_len, width), F32)]
                + more,
            )
            d.ggain_m = ggain if g.aligned else permute_cols(ggain, relative())
            parts[GH] = [None] * rs

        def attend_back(m, turn):
            if turn == rs - 1:
                outs = [shaped((seq_len, width), F32), shaped((seq_len, width))]
            else:
                outs = [shaped((tokens, width), F32)]
            outs = seq(
                bind(attn_back_kernel, g, m, turn),
                [shaped((zs, 2 * hb + PAD, 4 * hb))] + outs,
                seq_lengths,
                d.normed_t,
                d.offsets[m],
                d.qkv[m],
                d.gmix,
                d.grad_wo,
                d.hot,
                d.scaled,
                d.attn_w[m],
                *([d.ggain_m] if m == 0 else []),
                *([d.gn] if turn else []),
                scalars=1,
                scratch=[pltpu.VMEM((tokens, 3 * hb), BF16)],
            )
            parts[GH][m] = outs[0]
            if m % 2:
                hop_start(GH, m)
            if turn < rs - 1:
                d.gn = outs[1]
            else:
                own, sib = outs[1:]
                if not g.aligned:
                    back_to = jnp.argsort(relative())
                    own, sib = permute_cols(own, back_to), permute_cols(sib, back_to)
                d.gn = own
                put(NORMED, sib, core_pairs)

        def input_back():
            d.input_grad = seq(
                bind(input_back_kernel, g),
                [stored((seq_len, width))],
                d.gn,
                val[NORMED],
                d.grad_mid,
                x_own,
                d.gain_a,
                scratch=[pltpu.VMEM((seq_len, width), F32)],
            )[0]

        def layer_out():
            parts[LAYER] = seq(
                bind(layer_kernel, g),
                [shaped((seq_len, width))],
                seq_lengths,
                d.middle,
                d.ffn_part,
                val[SWAP],
                val[OUTER_X],
                scalars=1,
            )[0]

        def cot_end():
            deal_last(COT, True)
            put(COT_SIB, parts[COT], core_pairs)
            put(COT_X, parts[COT], plain_pairs[0])
            put(COT_XK, val[COT_X], core_pairs)

        parts[COT] = cotangent[0]
        bits = list(range(nb))
        step(start_core)
        step(start_attn)
        step(start_ffn)
        step(stack_attn)
        deal(COT, [nb] + bits, bits + [nb], True, cot_end)
        step(norm)
        for m in range(rs):
            step(attend, m)
        step(mixer)
        step(middle)
        step(ffn_own)
        step(ffn_other)
        step(cross_sum)
        step(own_sum)
        step(middle_back)
        step(layer_out)
        back_order = [m for m in range(1, rs, 2)] + [m for m in range(rs - 2, -1, -2)]
        for turn, m in enumerate(back_order):
            step(attend_back, m, turn)
        step(input_back)
        for j in range(2, zs):
            step(sum_step, OA, j)
        for i in range(chunks - 2, -1, -2):
            step(inner_add, i)
        for m in range(rs - 2, -1, -2):
            step(hop_add, GH, GH_SUM, m)
        deal(LAYER, [nb] + bits, bits + [nb], False, bind(deal_last, LAYER, False))
        step(outer_end)
        for j in range(2, zs):
            step(sum_step, GI_SUM, j)
            step(sum_step, GH_SUM, j)
        step(inner_split)
        step(ffn_pack)
        step(attn_split)
        step(attn_pack)
        step(spread_next, SPREAD_F)
        step(spread_next, SPREAD_T)
        step(ffn_end)
        step(attn_end)
        for item in ORDER if (rs, zs) == (4, 4) else range(len(steps)):
            if isinstance(item, int):
                steps[item]()
            else:
                seq.arrived(val[item if len(item) > 1 else item[0]])

        gains, table = d.gains, d.table[:, :n_buckets].T
        sum_tab = lax.dynamic_slice(table, (c * (n_buckets // ss), 0), (n_buckets // ss, heads))
        return (
            parts[LAYER][None],
            d.input_grad[None],
            *d.sum_attn,
            d.sum_in,
            d.sum_out,
            gains[0],
            gains[1],
            sum_tab,
        )

    tokens_spec = P(AXES, None, None)
    rows_spec, part_spec = P("shard", None), P("shard")
    in_specs = (
        (tokens_spec,) * 2 + (P(),) * 3 + (rows_spec,) * 6 + (part_spec,) * 2 + (rows_spec,)
    )
    out_specs = (tokens_spec,) * 2 + (rows_spec,) * 6 + (part_spec,) * 2 + (rows_spec,)
    return jax.shard_map(local, mesh=mesh, in_specs=in_specs, out_specs=out_specs, check_vma=False)
```
